128 devices in a mesh: dp: 32 (over x_hi, y, z), tensor: 4 (over x_lo, core).
Axes of the slice: x: 4 (x_hi: 2, x_lo: 2; x = x_hi * 2 + x_lo), y: 4, z: 4, core: 2. Of those that a mesh axis runs over, the one named last changes fastest.
Arguments:
- inputs: bfloat16 [32768, 640], P('dp'), may hold values from -6 to 6
- segments: int32 [32768], P('dp'), may hold values from 0 to 63, never falling along the last dimension, each value on 1 to 2048 neighbouring positions
- positions: int32 [32768], P('dp'), may hold values from 0 to 2047
- cotangent: bfloat16 [32768, 640], P('dp'), may hold values from -6 to 6
- w_query: bfloat16 [640, 1024], P(None, 'tensor'), may hold values from -0.25 to 0.25
- w_key: bfloat16 [640, 256], replicated, may hold values from -0.25 to 0.25
- w_value: bfloat16 [640, 256], replicated, may hold values from -0.25 to 0.25
- w_out: bfloat16 [1024, 640], P('tensor'), may hold values from -0.1875 to 0.1875
- w_gate: bfloat16 [640, 2048], P(None, 'tensor'), may hold values from -0.25 to 0.25
- w_up: bfloat16 [640, 2048], P(None, 'tensor'), may hold values from -0.25 to 0.25
- w_down: bfloat16 [2048, 640], P('tensor'), may hold values from -0.125 to 0.125
- g_attn_in: float32 [640], replicated, may hold values from 0.1 to 1.9
- g_attn_out: float32 [640], replicated, may hold values from 0.1 to 1.9
- g_ffn_in: float32 [640], replicated, may hold values from 0.1 to 1.9
- g_ffn_out: float32 [640], replicated, may hold values from 0.1 to 1.9
- g_query: float32 [256], replicated, may hold values from 0.1 to 1.9
- g_key: float32 [256], replicated, may hold values from 0.1 to 1.9
Outputs:
- output: bfloat16 [32768, 640], P('dp')
- input_grad: bfloat16 [32768, 640], P('dp')
- grad_query: float32 [640, 1024], P(None, 'tensor')
- grad_key: float32 [640, 256], replicated
- grad_value: float32 [640, 256], replicated
- grad_out: float32 [1024, 640], P('tensor')
- grad_gate: float32 [640, 2048], P(None, 'tensor')
- grad_up: float32 [640, 2048], P(None, 'tensor')
- grad_down: float32 [2048, 640], P('tensor')
- grad_attn_in: float32 [640], replicated
- grad_attn_out: float32 [640], replicated
- grad_ffn_in: float32 [640], replicated
- grad_ffn_out: float32 [640], replicated
- grad_qnorm: float32 [256], replicated
- grad_knorm: float32 [256], replicated
The draws below stay inside these ranges and needn't reach their ends.
Inputs may be any that keep to these rules, and one draw needn't show every extreme that they name: `segments`: document numbers never fall along the tokens; a document holds at most 2048 tokens.
All inputs are finite; a program needn't handle non-finite values.
Results may differ from the reference program's by a relative error of at most 0.03.
Values may be sent and summed in bfloat16 or wider, within the bound.
A program may use at most 128 MiB of HBM per device.

```python
import math
import jax
import jax.numpy as jnp
import numpy as np
from jax import lax

D = 640
FF = 2048
HEADS = 4
HD = 256
WINDOW = 512
LENGTH = 1024
TOKENS = 32768
SEGS = 64
SEG_MOST = 2048
N_TENSOR = 4


def set_ends(drawn, rng, low, top_value):
    spot = [jax.random.randint(jax.random.fold_in(rng, axis), (), 0, length) for axis, length in enumerate(drawn.shape)]
    main_axis = drawn.shape.index(max(drawn.shape))
    beside = spot[:main_axis] + [(spot[main_axis] + 1) % drawn.shape[main_axis]] + spot[main_axis + 1:]
    return drawn.at[tuple(spot)].set(low).at[tuple(beside)].set(top_value)


def block_scale(rng, shape, shards, smallest, top_value):
    def one(dim, shards_of):
        heights = jax.random.uniform(jax.random.fold_in(jax.random.fold_in(rng, 6), dim), (shards_of,), jnp.float32, smallest / len(shards), top_value / len(shards))
        return jnp.repeat(jnp.exp(heights), shape[dim] // shards_of).reshape((-1,) + (1,) * (len(shape) - dim - 1))

    gain = one(*shards[0])
    for cut in shards[1:]:
        gain = gain * one(*cut)
    return gain


def split_up(number_of, total, bound, lean):
    portions = [(1 << 20) // math.isqrt(rank ** lean) + 1 for rank in range(2, number_of + 1)]
    surplus, given = total - bound - (number_of - 1), [1] * (number_of - 1)
    while surplus > 0:
        candidates = [i for i in range(number_of - 1) if given[i] < bound]
        mass, remaining = sum([portions[i] for i in candidates]), surplus
        for i in candidates:
            addition = min(bound - given[i], max(1, remaining * portions[i] // mass), surplus)
            given[i] = given[i] + addition
            surplus = surplus - addition
    return np.array([bound] + given)


def ragged(own_key, number_of, total, reach, lean):
    if number_of == 2:
        one = jax.random.randint(own_key, (), max(1, total - reach), min(reach, total - 1) + 1)
        return jnp.stack([one, total - one])
    sizes = jnp.asarray(split_up(number_of, total, reach, lean), jnp.int32)
    couples = (number_of - 1) // 2
    source_of, sink = sizes[1:1 + 2 * couples:2], sizes[2:2 + 2 * couples:2]
    room = jnp.minimum(source_of - 1, reach - sink)
    shifted = jax.random.randint(jax.random.fold_in(own_key, 1), (couples,), 0, 1 << 20) % (room + 1)
    sizes = sizes.at[1:1 + 2 * couples:2].set(source_of - shifted).at[2:2 + 2 * couples:2].set(sink + shifted)
    return sizes[jax.random.permutation(jax.random.fold_in(own_key, 2), number_of)]


def scatter_about(key, extent, scale, reach, cuts=(), kind=jnp.bfloat16):
    factor_of = block_scale(key, extent, cuts, -0.22, 0.18) if cuts else 1.0
    values = jax.random.normal(key, extent, jnp.float32) * scale * factor_of
    return jnp.minimum(jnp.maximum(values, -reach), reach).astype(kind)


def setup_inputs(seed: int = 0) -> dict:
    seeds = jax.random.split(jax.random.key(seed), 18)
    return {
        "inputs": scatter_about(seeds[0], (TOKENS, D), 1.0, 6.0, ((0, 32),)),
        "segments": jnp.searchsorted(jnp.cumsum(ragged(seeds[1], SEGS, TOKENS, SEG_MOST, 0)), jnp.arange(TOKENS), side="right").astype(jnp.int32),
        "positions": set_ends(jax.random.randint(seeds[2], (TOKENS,), 0, 2 * LENGTH), jax.random.fold_in(seeds[2], 1), 0, (2 * LENGTH) - 1).astype(jnp.int32),
        "cotangent": scatter_about(seeds[3], (TOKENS, D), 1.0, 6.0, ((0, 32),)),
        "w_query": scatter_about(seeds[4], (D, HEADS * HD), D ** -0.5, 0.25, ((1, 4),)),
        "w_key": scatter_about(seeds[5], (D, HD), D ** -0.5, 0.25),
        "w_value": scatter_about(seeds[6], (D, HD), D ** -0.5, 0.25),
        "w_out": scatter_about(seeds[7], (HEADS * HD, D), (HEADS * HD) ** -0.5, 0.1875, ((0, 4),)),
        "w_gate": scatter_about(seeds[8], (D, FF), D ** -0.5, 0.25, ((1, 4),)),
        "w_up": scatter_about(seeds[9], (D, FF), D ** -0.5, 0.25, ((1, 4),)),
        "w_down": scatter_about(seeds[10], (FF, D), FF ** -0.5, 0.125, ((0, 4),)),
        "g_attn_in": jnp.clip(1.0 + 0.18 * jax.random.normal(seeds[11], (D,), jnp.float32), 0.1, 1.9),
        "g_attn_out": jnp.clip(1.0 + 0.18 * jax.random.normal(seeds[12], (D,), jnp.float32), 0.1, 1.9),
        "g_ffn_in": jnp.clip(1.0 + 0.18 * jax.random.normal(seeds[13], (D,), jnp.float32), 0.1, 1.9),
        "g_ffn_out": jnp.clip(1.0 + 0.18 * jax.random.normal(seeds[14], (D,), jnp.float32), 0.1, 1.9),
        "g_query": jnp.clip(1.0 + 0.18 * jax.random.normal(seeds[15], (HD,), jnp.float32), 0.1, 1.9),
        "g_key": jnp.clip(1.0 + 0.18 * jax.random.normal(seeds[16], (HD,), jnp.float32), 0.1, 1.9),
    }


EPSILON = 1e-06
ROPE_BASE = 10000.0
NEG_LARGE = -1e+30
HIGHEST = lax.Precision.HIGHEST

@jax.custom_vjp
def low(v):
    return lax.optimization_barrier(v.astype(jnp.bfloat16)).astype(jnp.float32)

@jax.custom_vjp
def low_back(v):
    return v

def low_keep(v):
    return (low(v), None)

def low_pass(kept, grad):
    return (grad,)

def back_keep(v):
    return (v, None)

def back_low(kept, grad):
    return (low(grad),)
low.defvjp(low_keep, low_pass)
low_back.defvjp(back_keep, back_low)

def matmul_hi(left, right):
    return jnp.dot(left, right, precision=HIGHEST, preferred_element_type=jnp.float32)

def rms_scale(values, gain_vec):
    return values * lax.rsqrt(lax.optimization_barrier(jnp.mean(values * values, axis=-1, keepdims=True)) + EPSILON) * gain_vec

def rope_tables(positions, head_size):
    half_size = head_size // 2
    inv_freq = ROPE_BASE ** (-2.0 * jnp.arange(half_size, dtype=jnp.float32) / head_size)
    angles = positions.astype(jnp.float32)[:, None] * inv_freq[None, :]
    return (jnp.cos(angles), jnp.sin(angles))

def rotate(values, cosine, sine_table):
    half_size = values.shape[-1] // 2
    first_half = values[..., :half_size]
    second_half = values[..., half_size:]
    return jnp.concatenate([first_half * cosine - second_half * sine_table, second_half * cosine + first_half * sine_table], axis=-1)

def windows(blocks, fill_value):
    earlier = jnp.concatenate([jnp.full_like(blocks[:, :1], fill_value), blocks[:, :-1]], axis=1)
    return jnp.concatenate([earlier, blocks], axis=2)

def allowed_mask(seg_rows, seg_keys, width):
    row_ids = lax.broadcasted_iota(jnp.int32, (width, 2 * width), 0)
    key_ids = lax.broadcasted_iota(jnp.int32, (width, 2 * width), 1)
    in_window = (key_ids > row_ids) & (key_ids <= row_ids + width)
    return in_window & (seg_rows[:, None] == seg_keys[None, :])

def attention(q_low, k_low, v_low, seg_seq):
    block_count = LENGTH // WINDOW
    score_scale = 1.0 / math.sqrt(HD)
    q_blocks = q_low.reshape(HEADS, block_count, WINDOW, HD).transpose(1, 0, 2, 3)
    k_windows = windows(k_low.reshape(1, block_count, WINDOW, HD), 0.0).reshape(block_count, 2 * WINDOW, HD)
    v_windows = windows(v_low.reshape(1, block_count, WINDOW, HD), 0.0).reshape(block_count, 2 * WINDOW, HD)
    seg_rows = seg_seq.reshape(block_count, WINDOW)
    seg_keys = windows(seg_seq.reshape(1, block_count, WINDOW), -1).reshape(block_count, 2 * WINDOW)

    def one_block(block_item):
        q_block, k_window, v_window, rows_seg, keys_seg = block_item
        scores = low_back(jnp.einsum('hqd,kd->hqk', q_block, k_window, precision=HIGHEST) * score_scale)
        allowed = allowed_mask(rows_seg, keys_seg, WINDOW)[None]
        masked = jnp.where(allowed, scores, NEG_LARGE)
        row_max = lax.optimization_barrier(jnp.max(masked, axis=-1, keepdims=True))
        expo_terms = jnp.where(allowed, jnp.exp(masked - row_max), 0.0)
        prob_full = expo_terms / lax.optimization_barrier(jnp.sum(expo_terms, axis=-1, keepdims=True))
        return jnp.einsum('hqk,kd->hqd', low(prob_full), v_window, precision=HIGHEST)
    block_outs = lax.map(jax.checkpoint(one_block), (q_blocks, k_windows, v_windows, seg_rows, seg_keys))
    return block_outs.transpose(1, 0, 2, 3).reshape(HEADS, LENGTH, HD)

def layer_pass(x_in, params, seg_seq, pos_seq):
    w_query, w_key, w_value, w_out, w_gate, w_up, w_down, g_attn_in, g_attn_out, g_ffn_in, g_ffn_out, g_query, g_key = params
    normed = low(rms_scale(x_in, g_attn_in))
    query_raw = low_back(matmul_hi(normed, w_query)).reshape(LENGTH, HEADS, HD).transpose(1, 0, 2)
    key_raw = low_back(matmul_hi(normed, w_key))
    value_raw = low_back(matmul_hi(normed, w_value))
    cosine, sine_table = rope_tables(pos_seq, HD)
    q_low = low(rotate(rms_scale(query_raw, g_query), cosine, sine_table))
    k_low = low(rotate(rms_scale(key_raw, g_key), cosine, sine_table))
    v_low = low(value_raw)
    heads_out = low(low_back(attention(q_low, k_low, v_low, seg_seq)))
    head_cols = heads_out.transpose(1, 0, 2).reshape(LENGTH, N_TENSOR, HEADS * HD // N_TENSOR)
    out_rows = w_out.reshape(N_TENSOR, HEADS * HD // N_TENSOR, D)
    attn_sum = low_back(lax.optimization_barrier(jnp.sum(low(jnp.einsum('lgk,gkd->gld', head_cols, out_rows, precision=HIGHEST)), axis=0)))
    mid_rows = x_in + rms_scale(attn_sum, g_attn_out)
    ffn_low = low(rms_scale(mid_rows, g_ffn_in))
    gate_raw = low_back(matmul_hi(ffn_low, w_gate))
    up_raw = low_back(matmul_hi(ffn_low, w_up))
    hidden = low(jax.nn.gelu(gate_raw, approximate=True) * up_raw)
    hidden_cols = hidden.reshape(LENGTH, N_TENSOR, FF // N_TENSOR)
    down_rows = w_down.reshape(N_TENSOR, FF // N_TENSOR, D)
    ffn_sum = low_back(lax.optimization_barrier(jnp.sum(low(jnp.einsum('lgk,gkd->gld', hidden_cols, down_rows, precision=HIGHEST)), axis=0)))
    return mid_rows + rms_scale(ffn_sum, g_ffn_out)

def reference(inputs, segments, positions, cotangent, w_query, w_key, w_value, w_out, w_gate, w_up, w_down, g_attn_in, g_attn_out, g_ffn_in, g_ffn_out, g_query, g_key):
    weights = tuple((member.astype(jnp.float32) for member in (w_query, w_key, w_value, w_out, w_gate, w_up, w_down, g_attn_in, g_attn_out, g_ffn_in, g_ffn_out, g_query, g_key)))
    seq_total = TOKENS // LENGTH
    seq_items = (inputs.astype(jnp.float32).reshape(seq_total, LENGTH, D), segments.reshape(seq_total, LENGTH), positions.reshape(seq_total, LENGTH), cotangent.astype(jnp.float32).reshape(seq_total, LENGTH, D))

    def step(totals, seq_item):
        x_seq, seg_seq, pos_seq, cot_seq = seq_item
        result, pull = jax.vjp(lambda x_in, params: layer_pass(x_in, params, seg_seq, pos_seq), x_seq, weights)
        grad_x, grad_params = pull(cot_seq)
        summed = tuple((total + extra for total, extra in zip(totals, grad_params)))
        return (summed, (result.astype(jnp.bfloat16), grad_x.astype(jnp.bfloat16)))
    zero_grads = tuple((jnp.zeros_like(member) for member in weights))
    totals, (outputs, grads_x) = lax.scan(step, zero_grads, seq_items)
    return (outputs.reshape(TOKENS, D), grads_x.reshape(TOKENS, D), totals[0], totals[1], totals[2], totals[3], totals[4], totals[5], totals[6], totals[7], totals[8], totals[9], totals[10], totals[11], totals[12])
```

```python
import math

import jax
import jax.numpy as jnp
from jax import lax
from jax.experimental import pallas as pl
from jax.experimental.pallas import tpu as pltpu
from jax.sharding import PartitionSpec as P

MESH = pl.DeviceIdType.MESH
BF = jnp.bfloat16
F32 = jnp.float32
VMEM = pl.BlockSpec(memory_space=pltpu.VMEM)
VMEM_LIMIT = 60 * 1024 * 1024


def neighbours():
    dp = lax.axis_index("dp")
    t = lax.axis_index("tensor")
    z = lax.rem(dp, 4)
    y = lax.rem(dp // 4, 4)
    xh = dp // 16
    xl = t // 2
    core = lax.rem(t, 2)
    ya = y + 1 - 2 * lax.rem(y, 2)
    za = z + 1 - 2 * lax.rem(z, 2)
    links = [
        (dp + (ya - y) * 4, t),
        (dp + (za - z), t),
        (dp + (3 - 2 * y) * 4, t),
        (dp + (3 - 2 * z), t),
    ]
    bits = [lax.rem((y + 1) // 2, 2), lax.rem((z + 1) // 2, 2), y // 2, z // 2]
    across = (dp + 16 - 32 * xh, t)
    sibling = (dp, t + 1 - 2 * core)
    beside = (dp, t + 2 - 4 * xl)
    return links, bits, across, sibling, beside, xl, core


def greet(devices):
    barrier = pltpu.get_barrier_semaphore()
    for d in devices:
        pl.semaphore_signal(barrier, inc=1, device_id=d, device_id_type=MESH)
    pl.semaphore_wait(barrier, len(devices))


def send(src, dst, ssem, rsem, device):
    copy = pltpu.make_async_remote_copy(
        src_ref=src, dst_ref=dst, send_sem=ssem, recv_sem=rsem, device_id=device, device_id_type=MESH
    )
    copy.start()
    return copy


class Reduction:
    def __init__(self, bufs, recvs, outs, ssem, rsem, links, bits, across):
        self.bufs, self.recvs, self.outs, self.ssem, self.rsem = bufs, recvs, outs, ssem, rsem
        self.links, self.bits, self.across = links, bits, across
        self.base = [jnp.int32(0)] * 4
        self.bases = []
        self.copies = None

    def start(self, step):
        copies = []
        for p in range(4):
            buf, recv = self.bufs[p], self.recvs[p]
            ss, rs = self.ssem.at[p, step], self.rsem.at[p, step]
            if step < 3:
                n = 4 >> step
                bit = self.bits[(p + step) % 4]
                there = self.base[p] + (1 - bit) * n
                self.base[p] = self.base[p] + bit * n
                at = (0, 4, 6)[step]
                src, dst, dev = buf.at[pl.ds(there, n)], recv.at[pl.ds(at, n)], self.links[(p + step) % 4]
            elif step < 5:
                dev = self.links[(p + 3) % 4] if step == 3 else self.across
                src, dst = buf.at[pl.ds(self.base[p], 1)], recv.at[pl.ds(4 + step, 1)]
            else:
                s = 7 - step
                n = 4 >> s
                bit = self.bits[(p + s) % 4]
                src = dst = self.outs[p].at[pl.ds(self.base[p], n)]
                self.base[p] = self.base[p] - bit * n
                dev = self.links[(p + s) % 4]
            copies.append(send(src, dst, ss, rs, dev))
        self.copies = copies

    def finish(self, step):
        for p in range(4):
            buf, recv = self.bufs[p], self.recvs[p]
            into = self.outs[p] if step == 4 else buf
            self.copies[p].wait()
            if step < 5:
                n = (4, 2, 1, 1, 1)[step]
                at = (0, 4, 6, 7, 8)[step]
                base = self.base[p]

                def add(i, carry):
                    into[base + i] = (buf[base + i].astype(F32) + recv[at + i].astype(F32)).astype(BF)
                    return carry

                lax.fori_loop(0, n, add, 0)


def sum_kernel(gate, up, down, query, out, kv, gains, a_out, o0, o1, o2, o3, kv_out, gains_out,
               a_buf, b0, b1, b2, b3, a_recv, r0, r1, r2, r3, kv_work, kv_recv, g_recv, a_ss, a_rs, b_ss, b_rs, k_ss, k_rs, g_ss, g_rs):
    links, bits, across, sibling, beside, xl, core = neighbours()
    greet(links + [across, sibling, beside])
    first = Reduction([a_buf.at[p] for p in range(4)], [a_recv.at[p] for p in range(4)],
                      [a_out.at[p] for p in range(4)], a_ss, a_rs, links, bits, across)
    second = Reduction([b0, b1, b2, b3], [r0, r1, r2, r3], [o0, o1, o2, o3], b_ss, b_rs, links, bits, across)
    gains_out[...] = gains[...]

    def swap_gains(i, device):
        return send(gains_out, g_recv.at[i], g_ss.at[i], g_rs.at[i], device)

    def add_gains(i, copy):
        copy.wait()
        gains_out[...] = gains_out[...] + g_recv[i]

    kc = send(kv.at[pl.ds((1 - core) * 2, 2)], kv_recv.at[pl.ds(0, 2)], k_ss.at[0], k_rs.at[0], sibling)
    gc = swap_gains(0, sibling)
    for p in range(4):
        cols = pl.ds(128 * p, 128)
        for c in range(8):
            a_buf[p, c, 0:80] = gate[80 * c:80 * c + 80, cols]
            a_buf[p, c, 80:160] = up[80 * c:80 * c + 80, cols]
            a_buf[p, c, 160:224] = down[64 * c:64 * c + 64, cols]
    first.start(0)
    kc.wait()
    for i in range(2):
        kv_work[i] = (kv[core * 2 + i].astype(F32) + kv_recv[i].astype(F32)).astype(BF)
    kc = send(kv_work.at[pl.ds(1 - xl, 1)], kv_recv.at[pl.ds(2, 1)], k_ss.at[1], k_rs.at[1], beside)
    add_gains(0, gc)
    gc = swap_gains(1, beside)
    for c in range(8):
        for p, b in ((0, b0), (1, b1)):
            b[c, 0:80] = query[80 * c:80 * c + 80, 128 * p:128 * p + 128]
            b[c, 80:112] = out[32 * c:32 * c + 32, 128 * p:128 * p + 128]
        b2[c, 80:112] = out[32 * c:32 * c + 32, 256:384]
        b3[c, 0:64] = down[64 * c:64 * c + 64, 512:640]
        b3[c, 64:96] = out[32 * c:32 * c + 32, 384:512]
        b3[c, 96:128] = out[32 * c:32 * c + 32, 512:640]
    kc.wait()
    mine = core * 2 + xl
    for c in range(8):
        b2[c, 0:80] = (kv_work[xl, 80 * c:80 * c + 80].astype(F32) + kv_recv[2, 80 * c:80 * c + 80].astype(F32)).astype(BF)
    second.start(0)
    add_gains(1, gc)
    for step in range(8):
        if step < 5:
            gc = swap_gains(2 + step, links[step] if step < 4 else across)
        first.finish(step)
        if step < 7:
            first.start(step + 1)
        second.finish(step)
        if step < 7:
            second.start(step + 1)
        if step < 5:
            add_gains(2 + step, gc)
    for c in range(8):
        kv_out[mine, 80 * c:80 * c + 80] = o2[c, 0:80]
    kc = send(kv_out.at[pl.ds(mine, 1)], kv_out.at[pl.ds(mine, 1)], k_ss.at[2], k_rs.at[2], beside)
    kc.wait()
    kc = send(kv_out.at[pl.ds(core * 2, 2)], kv_out.at[pl.ds(core * 2, 2)], k_ss.at[3], k_rs.at[3], sibling)
    kc.wait()


def unpack_kernel(a, b0, b1, b2, b3, kv, gains, query, key, value, out, gate, up, down, g0, g1, g2, g3, g4, g5):
    for p in range(4):
        cols = slice(128 * p, 128 * p + 128)
        for c in range(8):
            gate[80 * c:80 * c + 80, cols] = a[p, c, 0:80].astype(F32)
            up[80 * c:80 * c + 80, cols] = a[p, c, 80:160].astype(F32)
            down[64 * c:64 * c + 64, cols] = a[p, c, 160:224].astype(F32)
    for c in range(8):
        for p, b in ((0, b0), (1, b1)):
            query[80 * c:80 * c + 80, 128 * p:128 * p + 128] = b[c, 0:80].astype(F32)
            out[32 * c:32 * c + 32, 128 * p:128 * p + 128] = b[c, 80:112].astype(F32)
        out[32 * c:32 * c + 32, 256:384] = b2[c, 80:112].astype(F32)
        down[64 * c:64 * c + 64, 512:640] = b3[c, 0:64].astype(F32)
        out[32 * c:32 * c + 32, 384:512] = b3[c, 64:96].astype(F32)
        out[32 * c:32 * c + 32, 512:640] = b3[c, 96:128].astype(F32)
    for j in range(2):
        key[:, 128 * j:128 * j + 128] = kv[j].astype(F32)
        value[:, 128 * j:128 * j + 128] = kv[2 + j].astype(F32)
    for i, g in enumerate((g0, g1, g2, g3)):
        g[...] = gains[i:i + 1, :]
    g4[...] = gains[4:5, 0:256]
    g5[...] = gains[4:5, 256:512]


def sum_grads(query, key, value, out, gate, up, down, gains):
    kv = jnp.stack([key[:, :128], key[:, 128:], value[:, :128], value[:, 128:]])
    sds = jax.ShapeDtypeStruct
    dma = pltpu.SemaphoreType.DMA
    stacks = pl.pallas_call(
        sum_kernel,
        out_shape=(sds((4, 8, 224, 128), BF), sds((8, 112, 128), BF), sds((8, 112, 128), BF), sds((8, 112, 128), BF),
                   sds((8, 128, 128), BF), sds((4, 640, 128), BF), sds((8, 640), F32)),
        in_specs=[VMEM] * 7,
        out_specs=[VMEM] * 7,
        scratch_shapes=[
            pltpu.VMEM((4, 8, 224, 128), BF),
            pltpu.VMEM((8, 112, 128), BF), pltpu.VMEM((8, 112, 128), BF), pltpu.VMEM((8, 112, 128), BF),
            pltpu.VMEM((8, 128, 128), BF),
            pltpu.VMEM((4, 9, 224, 128), BF),
            pltpu.VMEM((9, 112, 128), BF), pltpu.VMEM((9, 112, 128), BF), pltpu.VMEM((9, 112, 128), BF),
            pltpu.VMEM((9, 128, 128), BF),
            pltpu.VMEM((2, 640, 128), BF),
            pltpu.VMEM((3, 640, 128), BF),
            pltpu.VMEM((7, 8, 640), F32),
            dma((4, 8)), dma((4, 8)), dma((4, 8)), dma((4, 8)), dma((4,)), dma((4,)), dma((7,)), dma((7,)),
        ],
        compiler_params=pltpu.CompilerParams(collective_id=7, has_side_effects=True, vmem_limit_bytes=VMEM_LIMIT),
        name="sum_grads",
    )(gate, up, down, query, out, kv, gains)
    outs = pl.pallas_call(
        unpack_kernel,
        out_shape=(sds((640, 256), F32), sds((640, 256), F32), sds((640, 256), F32), sds((256, 640), F32),
                   sds((640, 512), F32), sds((640, 512), F32), sds((512, 640), F32),
                   sds((1, 640), F32), sds((1, 640), F32), sds((1, 640), F32), sds((1, 640), F32),
                   sds((1, 256), F32), sds((1, 256), F32)),
        in_specs=[VMEM] * 7,
        out_specs=[VMEM] * 13,
        compiler_params=pltpu.CompilerParams(vmem_limit_bytes=VMEM_LIMIT),
        name="unpack_grads",
    )(*stacks)
    return outs

WINDOW = 512
LENGTH = 1024


EPSILON = 1e-06
ROPE_BASE = 10000.0
NEG_LARGE = -1e30


def in_blocks(x, dim, size):
    before, after = (x.shape[:dim], x.shape[dim + 1 :])
    return jnp.moveaxis(x.reshape(*before, size, -1, *after), dim, 0)


def sum_at_owner(x, axis, dim):
    size = lax.axis_size(axis)
    tiles = lax.all_to_all(in_blocks(x, dim, size), axis, 0, 0, tiled=True)
    return jnp.sum(tiles.astype(jnp.float32), axis=0)


def in_order(tiles, dim):
    tiles = jnp.moveaxis(tiles, 0, dim)
    lengths = tiles.shape
    return tiles.reshape(*lengths[:dim], lengths[dim] * lengths[dim + 1], *lengths[dim + 2 :])


def copy_for_each(x, axis):
    copies = jnp.broadcast_to(x, (lax.axis_size(axis), *x.shape))
    return lax.all_to_all(copies, axis, split_axis=0, concat_axis=0, tiled=True)


def collect(x, axis, dim):
    return in_order(copy_for_each(x, axis), dim)


def in_one_piece(arrays, axis, dim, along):
    both = jnp.concatenate(arrays, axis=along)
    out, at, gathered = (lax.all_gather(both, axis, axis=dim, tiled=True), 0, [])
    for a in arrays:
        gathered.append(lax.slice_in_dim(out, at, at + a.shape[along], axis=along))
        at += a.shape[along]
    return tuple(gathered)


def rms_scale(values, gain_vec):
    return (
        values * lax.rsqrt(jnp.mean(values * values, axis=-1, keepdims=True) + EPSILON) * gain_vec
    )


def gain_term(values, grad_vec):
    scaled = values * lax.rsqrt(jnp.mean(values * values, axis=-1, keepdims=True) + EPSILON)
    return jnp.sum(grad_vec * scaled, axis=0)


def rope_tables(positions, head_size):
    half_size = head_size // 2
    inv_freq = ROPE_BASE ** (-2.0 * jnp.arange(half_size, dtype=jnp.float32) / head_size)
    angles = positions.astype(jnp.float32)[:, None] * inv_freq[None, :]
    return (jnp.cos(angles), jnp.sin(angles))


def rotate(values, cosine, sine_table):
    half_size = values.shape[-1] // 2
    first_half = values[..., :half_size]
    second_half = values[..., half_size:]
    return jnp.concatenate(
        [
            first_half * cosine - second_half * sine_table,
            second_half * cosine + first_half * sine_table,
        ],
        axis=-1,
    )


def rotary_norm(raw_vec, gain_vec, cosine, sine_table):
    return rotate(rms_scale(raw_vec, gain_vec), cosine, sine_table)


def windows(blocks, fill_value):
    earlier = jnp.concatenate([jnp.full_like(blocks[:, :1], fill_value), blocks[:, :-1]], axis=1)
    return jnp.concatenate([earlier, blocks], axis=2)


def unwindow(grads, width):
    front_half = grads[:, :, :width]
    back_half = grads[:, :, width:]
    shifted = jnp.concatenate([front_half[:, 1:], jnp.zeros_like(front_half[:, :1])], axis=1)
    return back_half + shifted


def allowed_mask(seg_rows, seg_keys, width):
    row_ids = lax.broadcasted_iota(jnp.int32, (width, 2 * width), 0)
    key_ids = lax.broadcasted_iota(jnp.int32, (width, 2 * width), 1)
    in_window = (key_ids > row_ids) & (key_ids <= row_ids + width)
    return in_window & (seg_rows[:, None] == seg_keys[None, :])


def block_forward(block_item, score_scale):
    q_block, k_window, v_window, seg_rows, seg_keys = block_item
    width = q_block.shape[1]
    scores = (
        jnp.einsum("hqd,kd->hqk", q_block, k_window, preferred_element_type=jnp.float32)
        * score_scale
    )
    allowed = allowed_mask(seg_rows, seg_keys, width)[None]
    masked = jnp.where(allowed, scores, NEG_LARGE)
    row_max = jnp.max(masked, axis=-1, keepdims=True)
    expo_terms = jnp.where(allowed, jnp.exp(masked - row_max), 0.0)
    row_total = jnp.sum(expo_terms, axis=-1, keepdims=True)
    prob_low = (expo_terms / row_total).astype(jnp.bfloat16)
    block_out = jnp.einsum("hqk,kd->hqd", prob_low, v_window, preferred_element_type=jnp.float32)
    return (block_out, (row_max + jnp.log(row_total))[..., 0])


def block_backward(block_item, score_scale):
    q_block, k_window, v_window, seg_rows, seg_keys, log_totals, grad_block = block_item
    width = q_block.shape[1]
    scores = (
        jnp.einsum("hqd,kd->hqk", q_block, k_window, preferred_element_type=jnp.float32)
        * score_scale
    )
    allowed = allowed_mask(seg_rows, seg_keys, width)[None]
    prob_full = jnp.where(allowed, jnp.exp(scores - log_totals[..., None]), 0.0)
    grad_prob = jnp.einsum("hqd,kd->hqk", grad_block, v_window, preferred_element_type=jnp.float32)
    row_dot = jnp.sum(prob_full * grad_prob, axis=-1, keepdims=True)
    grad_scores = (prob_full * (grad_prob - row_dot)).astype(jnp.bfloat16)
    grad_q = (
        jnp.einsum("hqk,kd->hqd", grad_scores, k_window, preferred_element_type=jnp.float32)
        * score_scale
    )
    grad_k = (
        jnp.einsum("hqk,hqd->kd", grad_scores, q_block, preferred_element_type=jnp.float32)
        * score_scale
    )
    grad_v = jnp.einsum(
        "hqk,hqd->kd",
        prob_full.astype(jnp.bfloat16),
        grad_block,
        preferred_element_type=jnp.float32,
    )
    return (grad_q, grad_k, grad_v)


def local(
    inputs,
    segments,
    positions,
    cotangent,
    w_query,
    w_key,
    w_value,
    w_out,
    w_gate,
    w_up,
    w_down,
    g_attn_in,
    g_attn_out,
    g_ffn_in,
    g_ffn_out,
    g_query,
    g_key,
):
    row_count = inputs.shape[0]
    head_size = w_key.shape[1]
    heads_here = w_query.shape[1] // head_size
    seqs_here = row_count // LENGTH
    blocks_per = LENGTH // WINDOW
    block_total = seqs_here * blocks_per
    score_scale = 1.0 / math.sqrt(head_size)
    share_rows = row_count // lax.axis_size("tensor")
    first_row = lax.axis_index("tensor") * share_rows

    def my_rows(values):
        return lax.dynamic_slice_in_dim(values, first_row, share_rows, 0)

    whole_x = inputs.astype(jnp.float32)
    normed = rms_scale(whole_x, g_attn_in).astype(jnp.bfloat16)
    query_raw = jnp.dot(normed, w_query, preferred_element_type=jnp.float32)
    key_raw = jnp.dot(normed, w_key, preferred_element_type=jnp.float32)
    value_raw = jnp.dot(normed, w_value, preferred_element_type=jnp.float32)
    cosine, sine_table = rope_tables(positions, head_size)
    query_heads = query_raw.reshape(row_count, heads_here, head_size).transpose(1, 0, 2)
    q_rot, q_pull = jax.vjp(
        lambda raw_vec, gain_vec: rotary_norm(raw_vec, gain_vec, cosine, sine_table),
        query_heads,
        g_query,
    )
    k_rot, k_pull = jax.vjp(
        lambda raw_vec, gain_vec: rotary_norm(raw_vec, gain_vec, cosine, sine_table), key_raw, g_key
    )
    q_blocks = (
        q_rot.astype(jnp.bfloat16)
        .reshape(heads_here, block_total, WINDOW, head_size)
        .transpose(1, 0, 2, 3)
    )
    k_windows = windows(
        k_rot.astype(jnp.bfloat16).reshape(seqs_here, blocks_per, WINDOW, head_size), 0
    ).reshape(block_total, 2 * WINDOW, head_size)
    v_windows = windows(
        value_raw.astype(jnp.bfloat16).reshape(seqs_here, blocks_per, WINDOW, head_size), 0
    ).reshape(block_total, 2 * WINDOW, head_size)
    seg_rows = segments.reshape(block_total, WINDOW)
    seg_keys = windows(segments.reshape(seqs_here, blocks_per, WINDOW), -1).reshape(
        block_total, 2 * WINDOW
    )
    block_items = (q_blocks, k_windows, v_windows, seg_rows, seg_keys)
    heads_out, log_totals = lax.map(
        lambda block_item: block_forward(block_item, score_scale), block_items
    )
    heads_low = (
        heads_out.astype(jnp.bfloat16)
        .transpose(0, 2, 1, 3)
        .reshape(row_count, heads_here * head_size)
    )
    attn_term = jnp.dot(heads_low, w_out, preferred_element_type=jnp.float32)
    attn_sum = sum_at_owner(attn_term.astype(jnp.bfloat16), "tensor", 0)
    x_rows = my_rows(whole_x)
    attn_norm, attn_pull = jax.vjp(lambda values: rms_scale(values, g_attn_out), attn_sum)
    mid_rows = x_rows + attn_norm
    ffn_in, ffn_pull = jax.vjp(lambda values: rms_scale(values, g_ffn_in), mid_rows)
    ffn_low = collect(ffn_in.astype(jnp.bfloat16), "tensor", 0)
    gate_raw = jnp.dot(ffn_low, w_gate, preferred_element_type=jnp.float32)
    up_raw = jnp.dot(ffn_low, w_up, preferred_element_type=jnp.float32)
    hidden_full, act_pull = jax.vjp(
        lambda gate_in, up_in: jax.nn.gelu(gate_in, approximate=True) * up_in, gate_raw, up_raw
    )
    hidden = hidden_full.astype(jnp.bfloat16)
    ffn_term = jnp.dot(hidden, w_down, preferred_element_type=jnp.float32)
    ffn_sum = sum_at_owner(ffn_term.astype(jnp.bfloat16), "tensor", 0)
    cot_rows = my_rows(cotangent).astype(jnp.float32)
    out_norm, out_pull = jax.vjp(lambda values: rms_scale(values, g_ffn_out), ffn_sum)
    result = mid_rows + out_norm
    grad_ffn = out_pull(cot_rows)[0]
    output, grad_ffn_low = in_one_piece(
        (result.astype(jnp.bfloat16), grad_ffn.astype(jnp.bfloat16)), "tensor", 0, 1
    )
    grad_hidden = jnp.einsum("rd,fd->rf", grad_ffn_low, w_down, preferred_element_type=jnp.float32)
    grad_down = jnp.einsum("rf,rd->fd", hidden, grad_ffn_low, preferred_element_type=jnp.float32)
    grad_gate_full, grad_up_full = act_pull(grad_hidden)
    grad_gate_low = grad_gate_full.astype(jnp.bfloat16)
    grad_up_low = grad_up_full.astype(jnp.bfloat16)
    grad_gate = jnp.einsum("rd,rf->df", ffn_low, grad_gate_low, preferred_element_type=jnp.float32)
    grad_up = jnp.einsum("rd,rf->df", ffn_low, grad_up_low, preferred_element_type=jnp.float32)
    ffn_in_term = jnp.einsum(
        "rf,df->rd", grad_gate_low, w_gate, preferred_element_type=jnp.float32
    ) + jnp.einsum("rf,df->rd", grad_up_low, w_up, preferred_element_type=jnp.float32)
    ffn_in_grad = sum_at_owner(ffn_in_term.astype(jnp.bfloat16), "tensor", 0)
    grad_mid = cot_rows + ffn_pull(ffn_in_grad)[0]
    grad_attn = attn_pull(grad_mid)[0]
    grad_attn_low = collect(grad_attn.astype(jnp.bfloat16), "tensor", 0)
    grad_out = jnp.einsum("rh,rd->hd", heads_low, grad_attn_low, preferred_element_type=jnp.float32)
    grad_heads = jnp.einsum(
        "rd,hd->rh", grad_attn_low, w_out, preferred_element_type=jnp.float32
    ).astype(jnp.bfloat16)
    grad_blocks = grad_heads.reshape(block_total, WINDOW, heads_here, head_size).transpose(
        0, 2, 1, 3
    )
    grad_qb, grad_kw, grad_vw = lax.map(
        lambda block_item: block_backward(block_item, score_scale),
        block_items + (log_totals, grad_blocks),
    )
    grad_q_rot = grad_qb.transpose(1, 0, 2, 3).reshape(heads_here, row_count, head_size)
    grad_k_rot = unwindow(
        grad_kw.reshape(seqs_here, blocks_per, 2 * WINDOW, head_size), WINDOW
    ).reshape(row_count, head_size)
    grad_v_full = unwindow(
        grad_vw.reshape(seqs_here, blocks_per, 2 * WINDOW, head_size), WINDOW
    ).reshape(row_count, head_size)
    grad_query_raw, grad_qnorm = q_pull(grad_q_rot)
    grad_key_raw, grad_knorm = k_pull(grad_k_rot)
    grad_q_low = (
        grad_query_raw.transpose(1, 0, 2)
        .reshape(row_count, heads_here * head_size)
        .astype(jnp.bfloat16)
    )
    grad_k_low = grad_key_raw.astype(jnp.bfloat16)
    grad_v_low = grad_v_full.astype(jnp.bfloat16)
    grad_query = jnp.einsum("rd,rh->dh", normed, grad_q_low, preferred_element_type=jnp.float32)
    grad_key = jnp.einsum("rd,rh->dh", normed, grad_k_low, preferred_element_type=jnp.float32)
    grad_value = jnp.einsum("rd,rh->dh", normed, grad_v_low, preferred_element_type=jnp.float32)
    input_term = jnp.einsum("rh,dh->rd", grad_q_low, w_query, preferred_element_type=jnp.float32)
    input_term = input_term + jnp.einsum(
        "rh,dh->rd", grad_k_low, w_key, preferred_element_type=jnp.float32
    )
    input_term = input_term + jnp.einsum(
        "rh,dh->rd", grad_v_low, w_value, preferred_element_type=jnp.float32
    )
    input_sum = sum_at_owner(input_term.astype(jnp.bfloat16), "tensor", 0)
    x_grad_norm = jax.vjp(lambda values: rms_scale(values, g_attn_in), x_rows)[1](input_sum)[0]
    grad_rows = grad_mid + x_grad_norm
    gain_inputs = (x_rows, input_sum, attn_sum, grad_mid, mid_rows, ffn_in_grad, ffn_sum, cot_rows)
    input_grad = collect(grad_rows.astype(jnp.bfloat16), "tensor", 0)
    grad_attn_in = gain_term(gain_inputs[0], gain_inputs[1])
    grad_attn_out = gain_term(gain_inputs[2], gain_inputs[3])
    grad_ffn_in = gain_term(gain_inputs[4], gain_inputs[5])
    grad_ffn_out = gain_term(gain_inputs[6], gain_inputs[7])
    gains = jnp.stack(
        [
            grad_attn_in,
            grad_attn_out,
            grad_ffn_in,
            grad_ffn_out,
            jnp.concatenate([grad_qnorm, grad_knorm, jnp.zeros((128,), F32)]),
        ]
    )
    gains = jnp.concatenate([gains, jnp.zeros((3, 640), F32)])
    summed = sum_grads(
        grad_query.astype(BF),
        grad_key.astype(BF),
        grad_value.astype(BF),
        grad_out.astype(BF),
        grad_gate.astype(BF),
        grad_up.astype(BF),
        grad_down.astype(BF),
        gains,
    )
    return (output, input_grad, *summed[:7], *(g.reshape(-1) for g in summed[7:]))


def solution(mesh):
    placed = (
        P("dp", None),
        P("dp"),
        P("dp"),
        P("dp", None),
        P(None, "tensor"),
        P(),
        P(),
        P("tensor", None),
        P(None, "tensor"),
        P(None, "tensor"),
        P("tensor", None),
        P(),
        P(),
        P(),
        P(),
        P(),
        P(),
    )
    return jax.shard_map(
        local,
        mesh=mesh,
        in_specs=placed,
        out_specs=(
            P("dp", None),
            P("dp", None),
            P(None, "tensor"),
            P(),
            P(),
            P("tensor", None),
            P(None, "tensor"),
            P(None, "tensor"),
            P("tensor", None),
            P(),
            P(),
            P(),
            P(),
            P(),
            P(),
        ),
        check_vma=False,
    )
```

```python
import math

import jax
import jax.numpy as jnp
from jax import lax
from jax.experimental import pallas as pl
from jax.experimental.pallas import tpu as pltpu
from jax.sharding import PartitionSpec as P

MESH = pl.DeviceIdType.MESH
BF = jnp.bfloat16
F32 = jnp.float32
VMEM = pl.BlockSpec(memory_space=pltpu.VMEM)
VMEM_LIMIT = 60 * 1024 * 1024


def neighbours():
    dp = lax.axis_index("dp")
    t = lax.axis_index("tensor")
    z = lax.rem(dp, 4)
    y = lax.rem(dp // 4, 4)
    xh = dp // 16
    xl = t // 2
    core = lax.rem(t, 2)
    ya = y + 1 - 2 * lax.rem(y, 2)
    za = z + 1 - 2 * lax.rem(z, 2)
    links = [
        (dp + (ya - y) * 4, t),
        (dp + (za - z), t),
        (dp + (3 - 2 * y) * 4, t),
        (dp + (3 - 2 * z), t),
    ]
    bits = [lax.rem((y + 1) // 2, 2), lax.rem((z + 1) // 2, 2), y // 2, z // 2]
    across = (dp + 16 - 32 * xh, t)
    sibling = (dp, t + 1 - 2 * core)
    beside = (dp, t + 2 - 4 * xl)
    return links, bits, across, sibling, beside, xl, core


def greet(devices):
    barrier = pltpu.get_barrier_semaphore()
    for d in devices:
        pl.semaphore_signal(barrier, inc=1, device_id=d, device_id_type=MESH)
    pl.semaphore_wait(barrier, len(devices))


def send(src, dst, ssem, rsem, device):
    copy = pltpu.make_async_remote_copy(
        src_ref=src, dst_ref=dst, send_sem=ssem, recv_sem=rsem, device_id=device, device_id_type=MESH
    )
    copy.start()
    return copy


class Reduction:
    def __init__(self, bufs, recvs, outs, ssem, rsem, links, bits, across):
        self.bufs, self.recvs, self.outs, self.ssem, self.rsem = bufs, recvs, outs, ssem, rsem
        self.links, self.bits, self.across = links, bits, across
        self.base = [jnp.int32(0)] * 4
        self.bases = []
        self.copies = None

    def start(self, step):
        copies = []
        for p in range(4):
            buf, recv = self.bufs[p], self.recvs[p]
            ss, rs = self.ssem.at[p, step], self.rsem.at[p, step]
            if step < 3:
                n = 4 >> step
                bit = self.bits[(p + step) % 4]
                there = self.base[p] + (1 - bit) * n
                self.base[p] = self.base[p] + bit * n
                at = (0, 4, 6)[step]
                src, dst, dev = buf.at[pl.ds(there, n)], recv.at[pl.ds(at, n)], self.links[(p + step) % 4]
            elif step < 5:
                dev = self.links[(p + 3) % 4] if step == 3 else self.across
                src, dst = buf.at[pl.ds(self.base[p], 1)], recv.at[pl.ds(4 + step, 1)]
            else:
                s = 7 - step
                n = 4 >> s
                bit = self.bits[(p + s) % 4]
                src = dst = self.outs[p].at[pl.ds(self.base[p], n)]
                self.base[p] = self.base[p] - bit * n
                dev = self.links[(p + s) % 4]
            copies.append(send(src, dst, ss, rs, dev))
        self.copies = copies

    def finish(self, step):
        for p in range(4):
            buf, recv = self.bufs[p], self.recvs[p]
            into = self.outs[p] if step == 4 else buf
            self.copies[p].wait()
            if step < 5:
                n = (4, 2, 1, 1, 1)[step]
                at = (0, 4, 6, 7, 8)[step]
                base = self.base[p]

                def add(i, carry):
                    into[base + i] = (buf[base + i].astype(F32) + recv[at + i].astype(F32)).astype(BF)
                    return carry

                lax.fori_loop(0, n, add, 0)


def sum_kernel(gate, up, down, query, out, kv, gains, a_out, o0, o1, o2, o3, kv_out, gains_out,
               a_buf, b0, b1, b2, b3, a_recv, r0, r1, r2, r3, kv_work, kv_recv, g_recv, a_ss, a_rs, b_ss, b_rs, k_ss, k_rs, g_ss, g_rs):
    links, bits, across, sibling, beside, xl, core = neighbours()
    greet(links + [across, sibling, beside])
    first = Reduction([a_buf.at[p] for p in range(4)], [a_recv.at[p] for p in range(4)],
                      [a_out.at[p] for p in range(4)], a_ss, a_rs, links, bits, across)
    second = Reduction([b0, b1, b2, b3], [r0, r1, r2, r3], [o0, o1, o2, o3], b_ss, b_rs, links, bits, across)
    gains_out[...] = gains[...]

    def swap_gains(i, device):
        return send(gains_out, g_recv.at[i], g_ss.at[i], g_rs.at[i], device)

    def add_gains(i, copy):
        copy.wait()
        gains_out[...] = gains_out[...] + g_recv[i]

    kc = send(kv.at[pl.ds((1 - core) * 2, 2)], kv_recv.at[pl.ds(0, 2)], k_ss.at[0], k_rs.at[0], sibling)
    gc = swap_gains(0, sibling)
    for p in range(4):
        cols = pl.ds(128 * p, 128)
        for c in range(8):
            a_buf[p, c, 0:80] = gate[80 * c:80 * c + 80, cols]
            a_buf[p, c, 80:160] = up[80 * c:80 * c + 80, cols]
            a_buf[p, c, 160:224] = down[64 * c:64 * c + 64, cols]
    first.start(0)
    kc.wait()
    for i in range(2):
        kv_work[i] = (kv[core * 2 + i].astype(F32) + kv_recv[i].astype(F32)).astype(BF)
    kc = send(kv_work.at[pl.ds(1 - xl, 1)], kv_recv.at[pl.ds(2, 1)], k_ss.at[1], k_rs.at[1], beside)
    add_gains(0, gc)
    gc = swap_gains(1, beside)
    for c in range(8):
        for p, b in ((0, b0), (1, b1)):
            b[c, 0:80] = query[80 * c:80 * c + 80, 128 * p:128 * p + 128]
            b[c, 80:112] = out[32 * c:32 * c + 32, 128 * p:128 * p + 128]
        b2[c, 80:112] = out[32 * c:32 * c + 32, 256:384]
        b3[c, 0:64] = down[64 * c:64 * c + 64, 512:640]
        b3[c, 64:96] = out[32 * c:32 * c + 32, 384:512]
        b3[c, 96:128] = out[32 * c:32 * c + 32, 512:640]
    kc.wait()
    mine = core * 2 + xl
    for c in range(8):
        b2[c, 0:80] = (kv_work[xl, 80 * c:80 * c + 80].astype(F32) + kv_recv[2, 80 * c:80 * c + 80].astype(F32)).astype(BF)
    second.start(0)
    add_gains(1, gc)
    for step in range(8):
        if step < 5:
            gc = swap_gains(2 + step, links[step] if step < 4 else across)
        first.finish(step)
        if step < 7:
            first.start(step + 1)
        second.finish(step)
        if step < 7:
            second.start(step + 1)
        if step < 5:
            add_gains(2 + step, gc)
    for c in range(8):
        kv_out[mine, 80 * c:80 * c + 80] = o2[c, 0:80]
    kc = send(kv_out.at[pl.ds(mine, 1)], kv_out.at[pl.ds(mine, 1)], k_ss.at[2], k_rs.at[2], beside)
    kc.wait()
    kc = send(kv_out.at[pl.ds(core * 2, 2)], kv_out.at[pl.ds(core * 2, 2)], k_ss.at[3], k_rs.at[3], sibling)
    kc.wait()


def unpack_kernel(a, b0, b1, b2, b3, kv, gains, query, key, value, out, gate, up, down, g0, g1, g2, g3, g4, g5):
    for p in range(4):
        cols = slice(128 * p, 128 * p + 128)
        for c in range(8):
            gate[80 * c:80 * c + 80, cols] = a[p, c, 0:80].astype(F32)
            up[80 * c:80 * c + 80, cols] = a[p, c, 80:160].astype(F32)
            down[64 * c:64 * c + 64, cols] = a[p, c, 160:224].astype(F32)
    for c in range(8):
        for p, b in ((0, b0), (1, b1)):
            query[80 * c:80 * c + 80, 128 * p:128 * p + 128] = b[c, 0:80].astype(F32)
            out[32 * c:32 * c + 32, 128 * p:128 * p + 128] = b[c, 80:112].astype(F32)
        out[32 * c:32 * c + 32, 256:384] = b2[c, 80:112].astype(F32)
        down[64 * c:64 * c + 64, 512:640] = b3[c, 0:64].astype(F32)
        out[32 * c:32 * c + 32, 384:512] = b3[c, 64:96].astype(F32)
        out[32 * c:32 * c + 32, 512:640] = b3[c, 96:128].astype(F32)
    for j in range(2):
        key[:, 128 * j:128 * j + 128] = kv[j].astype(F32)
        value[:, 128 * j:128 * j + 128] = kv[2 + j].astype(F32)
    for i, g in enumerate((g0, g1, g2, g3)):
        g[...] = gains[i:i + 1, :]
    g4[...] = gains[4:5, 0:256]
    g5[...] = gains[4:5, 256:512]


def sum_grads(query, key, value, out, gate, up, down, gains):
    kv = jnp.stack([key[:, :128], key[:, 128:], value[:, :128], value[:, 128:]])
    sds = jax.ShapeDtypeStruct
    dma = pltpu.SemaphoreType.DMA
    stacks = pl.pallas_call(
        sum_kernel,
        out_shape=(sds((4, 8, 224, 128), BF), sds((8, 112, 128), BF), sds((8, 112, 128), BF), sds((8, 112, 128), BF),
                   sds((8, 128, 128), BF), sds((4, 640, 128), BF), sds((8, 640), F32)),
        in_specs=[VMEM] * 7,
        out_specs=[VMEM] * 7,
        scratch_shapes=[
            pltpu.VMEM((4, 8, 224, 128), BF),
            pltpu.VMEM((8, 112, 128), BF), pltpu.VMEM((8, 112, 128), BF), pltpu.VMEM((8, 112, 128), BF),
            pltpu.VMEM((8, 128, 128), BF),
            pltpu.VMEM((4, 9, 224, 128), BF),
            pltpu.VMEM((9, 112, 128), BF), pltpu.VMEM((9, 112, 128), BF), pltpu.VMEM((9, 112, 128), BF),
            pltpu.VMEM((9, 128, 128), BF),
            pltpu.VMEM((2, 640, 128), BF),
            pltpu.VMEM((3, 640, 128), BF),
            pltpu.VMEM((7, 8, 640), F32),
            dma((4, 8)), dma((4, 8)), dma((4, 8)), dma((4, 8)), dma((4,)), dma((4,)), dma((7,)), dma((7,)),
        ],
        compiler_params=pltpu.CompilerParams(collective_id=7, has_side_effects=True, vmem_limit_bytes=VMEM_LIMIT),
        name="sum_grads",
    )(gate, up, down, query, out, kv, gains)
    outs = pl.pallas_call(
        unpack_kernel,
        out_shape=(sds((640, 256), F32), sds((640, 256), F32), sds((640, 256), F32), sds((256, 640), F32),
                   sds((640, 512), F32), sds((640, 512), F32), sds((512, 640), F32),
                   sds((1, 640), F32), sds((1, 640), F32), sds((1, 640), F32), sds((1, 640), F32),
                   sds((1, 256), F32), sds((1, 256), F32)),
        in_specs=[VMEM] * 7,
        out_specs=[VMEM] * 13,
        compiler_params=pltpu.CompilerParams(vmem_limit_bytes=VMEM_LIMIT),
        name="unpack_grads",
    )(*stacks)
    return outs

WINDOW = 512
LENGTH = 1024


EPSILON = 1e-06
ROPE_BASE = 10000.0
NEG_LARGE = -1e30


NC = 4
CR = 1024 // NC
OW = CR // 4
C0 = 0.7978845608028654
C1 = 0.044715


def nt(a, b):
    return lax.dot_general(a, b, (((1,), (1,)), ((), ())), preferred_element_type=F32)


def tn(a, b):
    return lax.dot_general(a, b, (((0,), (0,)), ((), ())), preferred_element_type=F32)


def nn(a, b):
    return jnp.dot(a, b, preferred_element_type=F32)


def inv_rms(v):
    return lax.rsqrt(jnp.mean(v * v, axis=-1, keepdims=True) + EPSILON)


def rms_back(v, r, du):
    return r * du - v * (r * r * r * jnp.mean(du * v, axis=-1, keepdims=True))


class Tensor:
    def __init__(self, sibling, beside, xl, core, ssem, rsem):
        self.sibling, self.beside, self.xl, self.core = sibling, beside, xl, core
        self.own = core * 2 + xl
        self.ssem, self.rsem = ssem, rsem
        self.used = 0

    def send(self, src, dst, device):
        i = self.used
        self.used += 1
        return send(src, dst, self.ssem.at[i], self.rsem.at[i], device)

    def sum_a(self, part, recv):
        return self.send(part.at[pl.ds((1 - self.core) * 2, 2)], recv, self.sibling)

    def sum_b(self, copy, part, recv, out, recv2):
        copy.wait()
        there = self.core * 2 + 1 - self.xl
        out[...] = (part[there].astype(F32) + recv[1 - self.xl].astype(F32)).astype(BF)
        return self.send(out, recv2, self.beside)

    def sum_c(self, copy, part, recv, recv2):
        copy.wait()
        return part[self.own].astype(F32) + recv[self.xl].astype(F32) + recv2[...].astype(F32)

    def gather_a(self, buf):
        block = buf.at[self.own]
        return self.send(block, block, self.beside), self.send(block, block, self.sibling)

    def gather_b(self, copies, buf):
        copies[0].wait()
        block = buf.at[self.core * 2 + 1 - self.xl]
        return copies[1], self.send(block, block, self.sibling)

    def gather_c(self, copies):
        for c in copies:
            c.wait()


def ffn_kernel(attn, x, cot, wg, wu, wd, g_ao, g_fi, g_fo,
               output, dattn, dmid_out, grad_gate, grad_up, grad_down, gains,
               ffn_g, dffn_g, hid, act_a, act_b, dgate, dup, part2, part3, attn_own, mid_own,
               recv_a, recv_b, sent_b, ssem, rsem):
    _, _, _, sibling, beside, xl, core = neighbours()
    greet([sibling, beside])
    t = Tensor(sibling, beside, xl, core, ssem, rsem)
    own = t.own
    state = [dict() for _ in range(NC)]
    for i in range(3):
        state[0]["g%d" % i] = None

    def rs_a(e, part):
        def run(c):
            state[c]["a"] = t.sum_a(part.at[c], recv_a.at[e, c])
        return run

    def rs_b(e, part):
        def run(c):
            state[c]["b"] = t.sum_b(state[c]["a"], part.at[c], recv_a.at[e, c], sent_b.at[e, c], recv_b.at[e, c])
        return run

    def rs_c(e, part, c):
        return t.sum_c(state[c]["b"], part.at[c], recv_a.at[e, c], recv_b.at[e, c])

    def mid_stage(c):
        a = rs_c(0, attn, c)
        attn_own[c] = a
        mid = x[c, own].astype(F32) + a * inv_rms(a) * g_ao[...]
        mid_own[c] = mid
        ffn_g[c, own] = (mid * inv_rms(mid) * g_fi[...]).astype(BF)
        state[c]["g"] = t.gather_a(ffn_g.at[c])

    def forward(buf, key):
        def run(c):
            state[c][key] = t.gather_b(state[c][key], buf.at[c])
        return run

    def up_stage(c):
        t.gather_c(state[c]["g"])
        f = ffn_g[c].reshape(CR, 640)
        gate = nn(f, wg[...])
        up = nn(f, wu[...])
        th = jnp.tanh(C0 * (gate + C1 * gate * gate * gate))
        half = 0.5 * (1.0 + th)
        act = gate * half
        slope = half + 0.5 * gate * (1.0 - th * th) * (C0 * (1.0 + 3.0 * C1 * gate * gate))
        act_a[c] = up * slope
        act_b[c] = act
        h = (act * up).astype(BF)
        hid[c] = h
        part2[c] = nn(h, wd[...]).astype(BF).reshape(4, OW, 640)
        rs_a(1, part2)(c)

    def out_stage(c):
        s = rs_c(1, part2, c)
        r = inv_rms(s)
        ct = cot[c, own].astype(F32)
        dffn_g[c, own] = rms_back(s, r, ct * g_fo[...]).astype(BF)
        state[c]["g"] = t.gather_a(dffn_g.at[c])
        output[c, own] = (mid_own[c] + s * r * g_fo[...]).astype(BF)
        state[c]["o"] = t.gather_a(output.at[c])
        gains[2:3, :] = gains[2:3, :] + jnp.sum(ct * s * r, axis=0, keepdims=True)

    def down_stage(c):
        t.gather_c(state[c]["g"])
        d = dffn_g[c].reshape(CR, 640)
        dh = nt(d, wd[...])
        dg = (dh * act_a[c]).astype(BF)
        du = (dh * act_b[c]).astype(BF)
        dgate[c] = dg
        dup[c] = du
        part3[c] = (nt(dg, wg[...]) + nt(du, wu[...])).astype(BF).reshape(4, OW, 640)
        rs_a(2, part3)(c)

    def attn_stage(c):
        d = rs_c(2, part3, c)
        mid, a = mid_own[c], attn_own[c]
        r = inv_rms(mid)
        gains[1:2, :] = gains[1:2, :] + jnp.sum(d * mid * r, axis=0, keepdims=True)
        dmid = cot[c, own].astype(F32) + rms_back(mid, r, d * g_fi[...])
        dmid_out[c] = dmid
        r = inv_rms(a)
        gains[0:1, :] = gains[0:1, :] + jnp.sum(dmid * a * r, axis=0, keepdims=True)
        dattn[c, own] = rms_back(a, r, dmid * g_ao[...]).astype(BF)
        state[c]["g"] = t.gather_a(dattn.at[c])

    def last(c):
        t.gather_c(state[c]["o"])
        t.gather_c(state[c]["g"])

    def weights_down():
        grad_down[...] = tn(hid[...].reshape(1024, 512), dffn_g[...].reshape(1024, 640)).astype(BF)

    def weights_gate():
        grad_gate[...] = tn(ffn_g[...].reshape(1024, 640), dgate[...].reshape(1024, 512)).astype(BF)

    def weights_up():
        grad_up[...] = tn(ffn_g[...].reshape(1024, 640), dup[...].reshape(1024, 512)).astype(BF)

    gains[...] = jnp.zeros_like(gains)
    stages = [
        rs_a(0, attn), rs_b(0, attn), mid_stage, forward(ffn_g, "g"), up_stage,
        rs_b(1, part2), out_stage, forward(dffn_g, "g"), down_stage,
        rs_b(2, part3), forward(output, "o"), attn_stage, forward(dattn, "g"), last,
    ]
    work = sorted(((s + SKEW * c, s, c) for s in range(len(stages)) for c in range(NC)), key=lambda w: (w[0], w[2]))
    end = len(stages) - 1 + SKEW * (NC - 1)
    fill = {(9, NC - 1): weights_down, (11, NC - 1): weights_gate, (12, NC - 1): weights_up}
    for _, s, c in work:
        if s == 9 and c == NC - 1:
            stages[s](c)
            weights_down()
        elif s == 11 and c == NC - 1:
            stages[s](c)
            weights_gate()
        elif s == 12 and c == NC - 1:
            stages[s](c)
            weights_up()
        else:
            stages[s](c)


SKEW = 1


def ffn_block(attn_term, x, cot, wg, wu, wd, g_ao, g_fi, g_fo):
    sds = jax.ShapeDtypeStruct
    dma = pltpu.SemaphoreType.DMA
    blocks = (NC, 4, OW, 640)
    count = NC * (3 * 2 + 4 * 3)
    v = pltpu.VMEM
    outs = pl.pallas_call(
        ffn_kernel,
        out_shape=(sds(blocks, BF), sds(blocks, BF), sds((NC, OW, 640), F32), sds((640, 512), BF), sds((640, 512), BF),
                   sds((512, 640), BF), sds((8, 640), F32)),
        in_specs=[VMEM] * 9,
        out_specs=[VMEM] * 7,
        scratch_shapes=[
            v(blocks, BF), v(blocks, BF), v((NC, CR, 512), BF), v((NC, CR, 512), F32), v((NC, CR, 512), F32),
            v((NC, CR, 512), BF), v((NC, CR, 512), BF), v(blocks, BF), v(blocks, BF), v((NC, OW, 640), F32),
            v((NC, OW, 640), F32), v((3, NC, 2, OW, 640), BF), v((3, NC, OW, 640), BF), v((3, NC, OW, 640), BF),
            dma((count,)), dma((count,)),
        ],
        compiler_params=pltpu.CompilerParams(collective_id=3, has_side_effects=True, vmem_limit_bytes=VMEM_LIMIT),
        name="ffn_block",
    )(attn_term.reshape(blocks), x.reshape(blocks), cot.reshape(blocks), wg, wu, wd,
      g_ao.reshape(1, 640), g_fi.reshape(1, 640), g_fo.reshape(1, 640))
    return outs


def in_blocks(x, dim, size):
    before, after = (x.shape[:dim], x.shape[dim + 1 :])
    return jnp.moveaxis(x.reshape(*before, size, -1, *after), dim, 0)


def sum_at_owner(x, axis, dim):
    size = lax.axis_size(axis)
    tiles = lax.all_to_all(in_blocks(x, dim, size), axis, 0, 0, tiled=True)
    return jnp.sum(tiles.astype(jnp.float32), axis=0)


def in_order(tiles, dim):
    tiles = jnp.moveaxis(tiles, 0, dim)
    lengths = tiles.shape
    return tiles.reshape(*lengths[:dim], lengths[dim] * lengths[dim + 1], *lengths[dim + 2 :])


def copy_for_each(x, axis):
    copies = jnp.broadcast_to(x, (lax.axis_size(axis), *x.shape))
    return lax.all_to_all(copies, axis, split_axis=0, concat_axis=0, tiled=True)


def collect(x, axis, dim):
    return in_order(copy_for_each(x, axis), dim)


def in_one_piece(arrays, axis, dim, along):
    both = jnp.concatenate(arrays, axis=along)
    out, at, gathered = (lax.all_gather(both, axis, axis=dim, tiled=True), 0, [])
    for a in arrays:
        gathered.append(lax.slice_in_dim(out, at, at + a.shape[along], axis=along))
        at += a.shape[along]
    return tuple(gathered)


def rms_scale(values, gain_vec):
    return (
        values * lax.rsqrt(jnp.mean(values * values, axis=-1, keepdims=True) + EPSILON) * gain_vec
    )


def gain_term(values, grad_vec):
    scaled = values * lax.rsqrt(jnp.mean(values * values, axis=-1, keepdims=True) + EPSILON)
    return jnp.sum(grad_vec * scaled, axis=0)


def rope_tables(positions, head_size):
    half_size = head_size // 2
    inv_freq = ROPE_BASE ** (-2.0 * jnp.arange(half_size, dtype=jnp.float32) / head_size)
    angles = positions.astype(jnp.float32)[:, None] * inv_freq[None, :]
    return (jnp.cos(angles), jnp.sin(angles))


def rotate(values, cosine, sine_table):
    half_size = values.shape[-1] // 2
    first_half = values[..., :half_size]
    second_half = values[..., half_size:]
    return jnp.concatenate(
        [
            first_half * cosine - second_half * sine_table,
            second_half * cosine + first_half * sine_table,
        ],
        axis=-1,
    )


def rotary_norm(raw_vec, gain_vec, cosine, sine_table):
    return rotate(rms_scale(raw_vec, gain_vec), cosine, sine_table)


def windows(blocks, fill_value):
    earlier = jnp.concatenate([jnp.full_like(blocks[:, :1], fill_value), blocks[:, :-1]], axis=1)
    return jnp.concatenate([earlier, blocks], axis=2)


def unwindow(grads, width):
    front_half = grads[:, :, :width]
    back_half = grads[:, :, width:]
    shifted = jnp.concatenate([front_half[:, 1:], jnp.zeros_like(front_half[:, :1])], axis=1)
    return back_half + shifted


def allowed_mask(seg_rows, seg_keys, width):
    row_ids = lax.broadcasted_iota(jnp.int32, (width, 2 * width), 0)
    key_ids = lax.broadcasted_iota(jnp.int32, (width, 2 * width), 1)
    in_window = (key_ids > row_ids) & (key_ids <= row_ids + width)
    return in_window & (seg_rows[:, None] == seg_keys[None, :])


def block_forward(block_item, score_scale):
    q_block, k_window, v_window, seg_rows, seg_keys = block_item
    width = q_block.shape[1]
    scores = (
        jnp.einsum("hqd,kd->hqk", q_block, k_window, preferred_element_type=jnp.float32)
        * score_scale
    )
    allowed = allowed_mask(seg_rows, seg_keys, width)[None]
    masked = jnp.where(allowed, scores, NEG_LARGE)
    row_max = jnp.max(masked, axis=-1, keepdims=True)
    expo_terms = jnp.where(allowed, jnp.exp(masked - row_max), 0.0)
    row_total = jnp.sum(expo_terms, axis=-1, keepdims=True)
    prob_low = (expo_terms / row_total).astype(jnp.bfloat16)
    block_out = jnp.einsum("hqk,kd->hqd", prob_low, v_window, preferred_element_type=jnp.float32)
    return (block_out, (row_max + jnp.log(row_total))[..., 0])


def block_backward(block_item, score_scale):
    q_block, k_window, v_window, seg_rows, seg_keys, log_totals, grad_block = block_item
    width = q_block.shape[1]
    scores = (
        jnp.einsum("hqd,kd->hqk", q_block, k_window, preferred_element_type=jnp.float32)
        * score_scale
    )
    allowed = allowed_mask(seg_rows, seg_keys, width)[None]
    prob_full = jnp.where(allowed, jnp.exp(scores - log_totals[..., None]), 0.0)
    grad_prob = jnp.einsum("hqd,kd->hqk", grad_block, v_window, preferred_element_type=jnp.float32)
    row_dot = jnp.sum(prob_full * grad_prob, axis=-1, keepdims=True)
    grad_scores = (prob_full * (grad_prob - row_dot)).astype(jnp.bfloat16)
    grad_q = (
        jnp.einsum("hqk,kd->hqd", grad_scores, k_window, preferred_element_type=jnp.float32)
        * score_scale
    )
    grad_k = (
        jnp.einsum("hqk,hqd->kd", grad_scores, q_block, preferred_element_type=jnp.float32)
        * score_scale
    )
    grad_v = jnp.einsum(
        "hqk,hqd->kd",
        prob_full.astype(jnp.bfloat16),
        grad_block,
        preferred_element_type=jnp.float32,
    )
    return (grad_q, grad_k, grad_v)


def local(
    inputs,
    segments,
    positions,
    cotangent,
    w_query,
    w_key,
    w_value,
    w_out,
    w_gate,
    w_up,
    w_down,
    g_attn_in,
    g_attn_out,
    g_ffn_in,
    g_ffn_out,
    g_query,
    g_key,
):
    row_count = inputs.shape[0]
    head_size = w_key.shape[1]
    heads_here = w_query.shape[1] // head_size
    seqs_here = row_count // LENGTH
    blocks_per = LENGTH // WINDOW
    block_total = seqs_here * blocks_per
    score_scale = 1.0 / math.sqrt(head_size)
    whole_x = inputs.astype(jnp.float32)
    normed = rms_scale(whole_x, g_attn_in).astype(jnp.bfloat16)
    query_raw = jnp.dot(normed, w_query, preferred_element_type=jnp.float32)
    key_raw = jnp.dot(normed, w_key, preferred_element_type=jnp.float32)
    value_raw = jnp.dot(normed, w_value, preferred_element_type=jnp.float32)
    cosine, sine_table = rope_tables(positions, head_size)
    query_heads = query_raw.reshape(row_count, heads_here, head_size).transpose(1, 0, 2)
    q_rot, q_pull = jax.vjp(
        lambda raw_vec, gain_vec: rotary_norm(raw_vec, gain_vec, cosine, sine_table),
        query_heads,
        g_query,
    )
    k_rot, k_pull = jax.vjp(
        lambda raw_vec, gain_vec: rotary_norm(raw_vec, gain_vec, cosine, sine_table), key_raw, g_key
    )
    q_blocks = (
        q_rot.astype(jnp.bfloat16)
        .reshape(heads_here, block_total, WINDOW, head_size)
        .transpose(1, 0, 2, 3)
    )
    k_windows = windows(
        k_rot.astype(jnp.bfloat16).reshape(seqs_here, blocks_per, WINDOW, head_size), 0
    ).reshape(block_total, 2 * WINDOW, head_size)
    v_windows = windows(
        value_raw.astype(jnp.bfloat16).reshape(seqs_here, blocks_per, WINDOW, head_size), 0
    ).reshape(block_total, 2 * WINDOW, head_size)
    seg_rows = segments.reshape(block_total, WINDOW)
    seg_keys = windows(segments.reshape(seqs_here, blocks_per, WINDOW), -1).reshape(
        block_total, 2 * WINDOW
    )
    block_items = (q_blocks, k_windows, v_windows, seg_rows, seg_keys)
    heads_out, log_totals = lax.map(
        lambda block_item: block_forward(block_item, score_scale), block_items
    )
    heads_low = (
        heads_out.astype(jnp.bfloat16)
        .transpose(0, 2, 1, 3)
        .reshape(row_count, heads_here * head_size)
    )
    attn_term = jnp.dot(heads_low, w_out, preferred_element_type=jnp.float32)
    output, grad_attn_low, grad_mid, grad_gate, grad_up, grad_down, ffn_gains = ffn_block(
        attn_term.astype(BF), inputs, cotangent, w_gate, w_up, w_down, g_attn_out, g_ffn_in, g_ffn_out
    )
    output = output.reshape(row_count, -1)
    grad_attn_low = grad_attn_low.reshape(row_count, -1)
    t_index = lax.axis_index("tensor")
    owner = lax.rem(t_index, 2) * 2 + t_index // 2
    grad_out = jnp.einsum("rh,rd->hd", heads_low, grad_attn_low, preferred_element_type=jnp.float32)
    grad_heads = jnp.einsum(
        "rd,hd->rh", grad_attn_low, w_out, preferred_element_type=jnp.float32
    ).astype(jnp.bfloat16)
    grad_blocks = grad_heads.reshape(block_total, WINDOW, heads_here, head_size).transpose(
        0, 2, 1, 3
    )
    grad_qb, grad_kw, grad_vw = lax.map(
        lambda block_item: block_backward(block_item, score_scale),
        block_items + (log_totals, grad_blocks),
    )
    grad_q_rot = grad_qb.transpose(1, 0, 2, 3).reshape(heads_here, row_count, head_size)
    grad_k_rot = unwindow(
        grad_kw.reshape(seqs_here, blocks_per, 2 * WINDOW, head_size), WINDOW
    ).reshape(row_count, head_size)
    grad_v_full = unwindow(
        grad_vw.reshape(seqs_here, blocks_per, 2 * WINDOW, head_size), WINDOW
    ).reshape(row_count, head_size)
    grad_query_raw, grad_qnorm = q_pull(grad_q_rot)
    grad_key_raw, grad_knorm = k_pull(grad_k_rot)
    grad_q_low = (
        grad_query_raw.transpose(1, 0, 2)
        .reshape(row_count, heads_here * head_size)
        .astype(jnp.bfloat16)
    )
    grad_k_low = grad_key_raw.astype(jnp.bfloat16)
    grad_v_low = grad_v_full.astype(jnp.bfloat16)
    grad_query = jnp.einsum("rd,rh->dh", normed, grad_q_low, preferred_element_type=jnp.float32)
    grad_key = jnp.einsum("rd,rh->dh", normed, grad_k_low, preferred_element_type=jnp.float32)
    grad_value = jnp.einsum("rd,rh->dh", normed, grad_v_low, preferred_element_type=jnp.float32)
    input_term = jnp.einsum("rh,dh->rd", grad_q_low, w_query, preferred_element_type=jnp.float32)
    input_term = input_term + jnp.einsum(
        "rh,dh->rd", grad_k_low, w_key, preferred_element_type=jnp.float32
    )
    input_term = input_term + jnp.einsum(
        "rh,dh->rd", grad_v_low, w_value, preferred_element_type=jnp.float32
    )
    owned = lambda v: lax.dynamic_index_in_dim(v.reshape(NC, 4, OW, 640), owner, 1, False).reshape(256, 640)
    term = input_term.astype(jnp.bfloat16).reshape(NC, 4, OW, 640)
    term = term.transpose(1, 0, 2, 3).reshape(2, 2, 256, 640).transpose(1, 0, 2, 3).reshape(1024, 640)
    input_sum = sum_at_owner(term, "tensor", 0)
    x_rows = owned(whole_x)
    x_grad_norm = jax.vjp(lambda values: rms_scale(values, g_attn_in), x_rows)[1](input_sum)[0]
    grad_rows = grad_mid.reshape(256, 640) + x_grad_norm
    input_grad = collect(grad_rows.astype(jnp.bfloat16), "tensor", 0)
    input_grad = input_grad.reshape(2, 2, NC, OW, 640).transpose(2, 1, 0, 3, 4).reshape(1024, 640)
    grad_attn_in = gain_term(x_rows, input_sum)
    gains = jnp.concatenate(
        [
            grad_attn_in[None],
            ffn_gains[:3],
            jnp.concatenate([grad_qnorm, grad_knorm, jnp.zeros((128,), F32)])[None],
            jnp.zeros((3, 640), F32),
        ]
    )
    summed = sum_grads(
        grad_query.astype(BF),
        grad_key.astype(BF),
        grad_value.astype(BF),
        grad_out.astype(BF),
        grad_gate,
        grad_up,
        grad_down,
        gains,
    )
    return (output, input_grad, *summed[:7], *(g.reshape(-1) for g in summed[7:]))


def solution(mesh):
    placed = (
        P("dp", None),
        P("dp"),
        P("dp"),
        P("dp", None),
        P(None, "tensor"),
        P(),
        P(),
        P("tensor", None),
        P(None, "tensor"),
        P(None, "tensor"),
        P("tensor", None),
        P(),
        P(),
        P(),
        P(),
        P(),
        P(),
    )
    return jax.shard_map(
        local,
        mesh=mesh,
        in_specs=placed,
        out_specs=(
            P("dp", None),
            P("dp", None),
            P(None, "tensor"),
            P(),
            P(),
            P("tensor", None),
            P(None, "tensor"),
            P(None, "tensor"),
            P("tensor", None),
            P(),
            P(),
            P(),
            P(),
            P(),
            P(),
        ),
        check_vma=False,
    )
```

```python
import jax, jax.numpy as jnp
from jax import lax
from jax.experimental import pallas as pl
from jax.experimental.pallas import tpu as pltpu
from jax.sharding import PartitionSpec as P

WINDOW = 512
EPSILON = 1e-06
ROPE_BASE = 10000.0
NEG_LARGE = -1e30

MESH = pl.DeviceIdType.MESH
BF = jnp.bfloat16
F32 = jnp.float32
VMEM = pl.BlockSpec(memory_space=pltpu.VMEM)
VMEM_LIMIT = 60 * 1024 * 1024


def neighbours():
    dp = lax.axis_index("dp")
    t = lax.axis_index("tensor")
    z = lax.rem(dp, 4)
    y = lax.rem(dp // 4, 4)
    xh = dp // 16
    xl = t // 2
    core = lax.rem(t, 2)
    ya = y + 1 - 2 * lax.rem(y, 2)
    za = z + 1 - 2 * lax.rem(z, 2)
    links = [
        (dp + (ya - y) * 4, t),
        (dp + (za - z), t),
        (dp + (3 - 2 * y) * 4, t),
        (dp + (3 - 2 * z), t),
    ]
    bits = [lax.rem((y + 1) // 2, 2), lax.rem((z + 1) // 2, 2), y // 2, z // 2]
    across = (dp + 16 - 32 * xh, t)
    sibling = (dp, t + 1 - 2 * core)
    beside = (dp, t + 2 - 4 * xl)
    return links, bits, across, sibling, beside, xl, core


def greet(devices):
    barrier = pltpu.get_barrier_semaphore()
    for d in devices:
        pl.semaphore_signal(barrier, inc=1, device_id=d, device_id_type=MESH)
    pl.semaphore_wait(barrier, len(devices))


def send(src, dst, ssem, rsem, device):
    copy = pltpu.make_async_remote_copy(
        src_ref=src, dst_ref=dst, send_sem=ssem, recv_sem=rsem, device_id=device, device_id_type=MESH
    )
    copy.start()
    return copy


class Reduction:
    def __init__(self, ins, bufs, recvs, outs, ssem, rsem, links, bits, across):
        self.ins, self.bufs, self.recvs, self.outs, self.ssem, self.rsem = ins, bufs, recvs, outs, ssem, rsem
        self.links, self.bits, self.across = links, bits, across
        self.base = [jnp.int32(0)] * 4
        self.bases = []
        self.copies = None

    def start(self, step):
        copies = []
        for p in range(4):
            buf, recv = (self.ins if step == 0 else self.bufs)[p], self.recvs[p]
            ss, rs = self.ssem.at[p, step], self.rsem.at[p, step]
            if step < 3:
                n = 4 >> step
                bit = self.bits[(p + step) % 4]
                there = self.base[p] + (1 - bit) * n
                self.base[p] = self.base[p] + bit * n
                at = (0, 4, 6)[step]
                src, dst, dev = buf.at[pl.ds(there, n)], recv.at[pl.ds(at, n)], self.links[(p + step) % 4]
            elif step < 5:
                dev = self.links[(p + 3) % 4] if step == 3 else self.across
                src, dst = buf.at[pl.ds(self.base[p], 1)], recv.at[pl.ds(4 + step, 1)]
            else:
                s = 7 - step
                n = 4 >> s
                bit = self.bits[(p + s) % 4]
                src = dst = self.outs[p].at[pl.ds(self.base[p], n)]
                self.base[p] = self.base[p] - bit * n
                dev = self.links[(p + s) % 4]
            copies.append(send(src, dst, ss, rs, dev))
        self.copies = copies

    def finish(self, step):
        for p in range(4):
            buf, recv = self.bufs[p], self.recvs[p]
            into = self.outs[p] if step == 4 else buf
            buf = self.ins[p] if step == 0 else buf
            self.copies[p].wait()
            if step < 5:
                n = (4, 2, 1, 1, 1)[step]
                at = (0, 4, 6, 7, 8)[step]
                base = self.base[p]

                def add(i, carry):
                    into[base + i] = (buf[base + i].astype(F32) + recv[at + i].astype(F32)).astype(BF)
                    return carry

                lax.fori_loop(0, n, add, 0)


NC = 4
CR = 1024 // NC
OW = CR // 4
C0 = 0.7978845608028654
C1 = 0.044715


def nt(a, b):
    return lax.dot_general(a, b, (((1,), (1,)), ((), ())), preferred_element_type=F32)


def tn(a, b):
    return lax.dot_general(a, b, (((0,), (0,)), ((), ())), preferred_element_type=F32)


def nn(a, b):
    return jnp.dot(a, b, preferred_element_type=F32)


def inv_rms(v):
    return lax.rsqrt(jnp.mean(v * v, axis=-1, keepdims=True) + EPSILON)


def rms_back(v, r, du):
    return r * du - v * (r * r * r * jnp.mean(du * v, axis=-1, keepdims=True))


class Tensor:
    def __init__(self, sibling, beside, xl, core, ssem, rsem):
        self.sibling, self.beside, self.xl, self.core = sibling, beside, xl, core
        self.own = core * 2 + xl
        self.ssem, self.rsem = ssem, rsem
        self.used = 0

    def send(self, src, dst, device):
        i = self.used
        self.used += 1
        return send(src, dst, self.ssem.at[i], self.rsem.at[i], device)

    def sum_a(self, part, recv):
        return self.send(part.at[pl.ds((1 - self.core) * 2, 2)], recv, self.sibling)

    def sum_b(self, copy, part, recv, out, recv2):
        copy.wait()
        there = self.core * 2 + 1 - self.xl
        out[...] = (part[there].astype(F32) + recv[1 - self.xl].astype(F32)).astype(BF)
        return self.send(out, recv2, self.beside)

    def sum_c(self, copy, part, recv, recv2):
        copy.wait()
        return part[self.own].astype(F32) + recv[self.xl].astype(F32) + recv2[...].astype(F32)

    def gather_a(self, buf):
        block = buf.at[self.own]
        return self.send(block, block, self.beside), self.send(block, block, self.sibling)

    def gather_b(self, copies, buf):
        copies[0].wait()
        block = buf.at[self.core * 2 + 1 - self.xl]
        return copies[1], self.send(block, block, self.sibling)

    def gather_c(self, copies):
        for c in copies:
            c.wait()


def turn(v, cosine, sine):
    a, b = v[:, :128], v[:, 128:]
    return jnp.concatenate([a * cosine - b * sine, b * cosine + a * sine], axis=-1)


def turn_back(v, cosine, sine):
    a, b = v[:, :128], v[:, 128:]
    return jnp.concatenate([a * cosine + b * sine, b * cosine - a * sine], axis=-1)


def key_range(i):
    first = max(0, (i - 2) * CR)
    return first, (i + 1) * CR - first


def forward_kernel(x, cot, segs, cos_t, sin_t, wq, wk, wv, wo, wg, wu, wd, g_in, g_ao, g_fi, g_fo, g_q, g_k,
               output, dattn, dmid_out, grads, down4, gains, normed, q_raw, k_raw, q, k, v, prob, heads,
               attn, ffn_g, dffn_g, hid, act_a, act_b, dgate, dup, part2, part3, attn_own, mid_own,
               recv_a, recv_b, sent_b, ssem, rsem):
    _, _, _, sibling, beside, xl, core = neighbours()
    greet([sibling, beside])
    t = Tensor(sibling, beside, xl, core, ssem, rsem)
    own = t.own
    state = [dict() for _ in range(NC)]

    def rs_a(e, part):
        def run(c):
            state[c]["a"] = t.sum_a(part.at[c], recv_a.at[e, c])
        return run

    def rs_b(e, part):
        def run(c):
            state[c]["b"] = t.sum_b(state[c]["a"], part.at[c], recv_a.at[e, c], sent_b.at[e, c], recv_b.at[e, c])
        return run

    def rs_c(e, part, c):
        return t.sum_c(state[c]["b"], part.at[c], recv_a.at[e, c], recv_b.at[e, c])

    def attention_stage(c):
        rows = slice(c * CR, c * CR + CR)
        xv = x[c].reshape(CR, 640).astype(F32)
        n = (xv * inv_rms(xv) * vec(g_in)).astype(BF)
        normed[rows] = n
        cosine, sine = cos_t[rows], sin_t[rows]
        raw = nn(n, wq[...])
        q_raw[rows] = raw
        q_low = turn(raw * inv_rms(raw) * vec(g_q), cosine, sine).astype(BF)
        q[rows] = q_low
        raw = nn(n, wk[...])
        k_raw[rows] = raw
        k[rows] = turn(raw * inv_rms(raw) * vec(g_k), cosine, sine).astype(BF)
        v[rows] = nn(n, wv[...]).astype(BF)
        first, size = key_range(c)
        keys = slice(first, first + size)
        scores = nt(q_low, k[keys]) * 0.0625
        gap = c * CR - first + lax.broadcasted_iota(jnp.int32, (CR, size), 0) - lax.broadcasted_iota(jnp.int32, (CR, size), 1)
        seg_rows = jnp.broadcast_to(segs[:, rows], (128, CR)).T[:, :1]
        allowed = (gap >= 0) & (gap < WINDOW) & (seg_rows == segs[:, keys])
        masked = jnp.where(allowed, scores, NEG_LARGE)
        e = jnp.where(allowed, jnp.exp(masked - jnp.max(masked, axis=-1, keepdims=True)), 0.0)
        p = e / jnp.sum(e, axis=-1, keepdims=True)
        prob[c, :, 0:size] = p
        h = nn(p.astype(BF), v[keys]).astype(BF)
        heads[rows] = h
        attn[c] = nn(h, wo[...]).astype(BF).reshape(4, OW, 640)
        rs_a(0, attn)(c)

    def mid_stage(c):
        a = rs_c(0, attn, c)
        attn_own[c] = a
        mid = x[c, own].astype(F32) + a * inv_rms(a) * vec(g_ao)
        mid_own[c] = mid
        ffn_g[c, own] = (mid * inv_rms(mid) * vec(g_fi)).astype(BF)
        state[c]["g"] = t.gather_a(ffn_g.at[c])

    def forward(buf, key):
        def run(c):
            state[c][key] = t.gather_b(state[c][key], buf.at[c])
        return run

    def up_stage(c):
        t.gather_c(state[c]["g"])
        f = ffn_g[c].reshape(CR, 640)
        gate = nn(f, wg[...])
        up = nn(f, wu[...])
        th = jnp.tanh(C0 * (gate + C1 * gate * gate * gate))
        half = 0.5 * (1.0 + th)
        act = gate * half
        slope = half + 0.5 * gate * (1.0 - th * th) * (C0 * (1.0 + 3.0 * C1 * gate * gate))
        act_a[c] = up * slope
        act_b[c] = act
        h = (act * up).astype(BF)
        hid[c] = h
        part2[c] = nn(h, wd[...]).astype(BF).reshape(4, OW, 640)
        rs_a(1, part2)(c)

    def out_stage(c):
        s = rs_c(1, part2, c)
        r = inv_rms(s)
        ct = cot[c, own].astype(F32)
        dffn_g[c, own] = rms_back(s, r, ct * vec(g_fo)).astype(BF)
        state[c]["g"] = t.gather_a(dffn_g.at[c])
        output[c, own] = (mid_own[c] + s * r * vec(g_fo)).astype(BF)
        state[c]["o"] = t.gather_a(output.at[c])
        gains[2:3, :] = gains[2:3, :] + jnp.sum(ct * s * r, axis=0, keepdims=True)

    def down_stage(c):
        t.gather_c(state[c]["g"])
        d = dffn_g[c].reshape(CR, 640)
        dh = nt(d, wd[...])
        dg = (dh * act_a[c]).astype(BF)
        du = (dh * act_b[c]).astype(BF)
        dgate[c] = dg
        dup[c] = du
        part3[c] = (nt(dg, wg[...]) + nt(du, wu[...])).astype(BF).reshape(4, OW, 640)
        rs_a(2, part3)(c)

    def attn_stage(c):
        d = rs_c(2, part3, c)
        mid, a = mid_own[c], attn_own[c]
        r = inv_rms(mid)
        gains[1:2, :] = gains[1:2, :] + jnp.sum(d * mid * r, axis=0, keepdims=True)
        dmid = cot[c, own].astype(F32) + rms_back(mid, r, d * vec(g_fi))
        dmid_out[c] = dmid
        r = inv_rms(a)
        gains[0:1, :] = gains[0:1, :] + jnp.sum(dmid * a * r, axis=0, keepdims=True)
        dattn[c, own] = rms_back(a, r, dmid * vec(g_ao)).astype(BF)
        state[c]["g"] = t.gather_a(dattn.at[c])

    def last(c):
        t.gather_c(state[c]["o"])
        t.gather_c(state[c]["g"])

    def weights_down():
        g = tn(hid[...].reshape(1024, 512), dffn_g[...].reshape(1024, 640)).astype(BF)
        for s in range(8):
            for p in range(4):
                grads[p, s, 160:224] = g[64 * s:64 * s + 64, 128 * p:128 * p + 128]
        down4[...] = g[:, 512:640]

    def weights_gate():
        g = tn(ffn_g[...].reshape(1024, 640), dgate[...].reshape(1024, 512)).astype(BF)
        for s in range(8):
            for p in range(4):
                grads[p, s, 0:80] = g[80 * s:80 * s + 80, 128 * p:128 * p + 128]

    def weights_up():
        g = tn(ffn_g[...].reshape(1024, 640), dup[...].reshape(1024, 512)).astype(BF)
        for s in range(8):
            for p in range(4):
                grads[p, s, 80:160] = g[80 * s:80 * s + 80, 128 * p:128 * p + 128]

    gains[...] = jnp.zeros_like(gains)
    stages = [
        attention_stage, rs_b(0, attn), mid_stage, forward(ffn_g, "g"), up_stage,
        rs_b(1, part2), out_stage, forward(dffn_g, "g"), down_stage,
        rs_b(2, part3), forward(output, "o"), attn_stage, forward(dattn, "g"), last,
    ]
    work = sorted(((s + SKEW * c, s, c) for s in range(len(stages)) for c in range(NC)), key=lambda w: (w[0], w[2]))
    fill = {9: weights_down, 11: weights_gate, 12: weights_up}
    for _, s, c in work:
        stages[s](c)
        if c == NC - 1 and s in fill:
            fill[s]()


def vec(g):
    return g[...]


SKEW = 1


def forward_part(x, cot, segs, cos_t, sin_t, weights, gains):
    sds = jax.ShapeDtypeStruct
    dma = pltpu.SemaphoreType.DMA
    blocks = (NC, 4, OW, 640)
    count = NC * (3 * 2 + 4 * 3)
    v = pltpu.VMEM
    return pl.pallas_call(
        forward_kernel,
        out_shape=(sds(blocks, BF), sds(blocks, BF), sds((NC, OW, 640), F32), sds((4, 8, 224, 128), BF),
                   sds((512, 128), BF), sds((8, 640), F32), sds((1024, 640), BF), sds((1024, 256), F32),
                   sds((1024, 256), F32), sds((1024, 256), BF), sds((1024, 256), BF), sds((1024, 256), BF),
                   sds((NC, CR, 768), F32), sds((1024, 256), BF)),
        in_specs=[VMEM] * 18,
        out_specs=[VMEM] * 14,
        scratch_shapes=[
            v(blocks, BF),
            v(blocks, BF), v(blocks, BF), v((NC, CR, 512), BF), v((NC, CR, 512), F32), v((NC, CR, 512), F32),
            v((NC, CR, 512), BF), v((NC, CR, 512), BF), v(blocks, BF), v(blocks, BF), v((NC, OW, 640), F32),
            v((NC, OW, 640), F32), v((3, NC, 2, OW, 640), BF), v((3, NC, OW, 640), BF), v((3, NC, OW, 640), BF),
            dma((count,)), dma((count,)),
        ],
        compiler_params=pltpu.CompilerParams(collective_id=3, has_side_effects=True, vmem_limit_bytes=VMEM_LIMIT),
        name="forward_part",
    )(x, cot, segs, cos_t, sin_t, *weights, *gains)


def backward_kernel(dattn, dmid, x, heads, prob, q, k, v, q_raw, k_raw, cos_t, sin_t, normed, wq, wk, wv, wo, g_in, g_q, g_k,
                grads, down4, gains, in_grad, a_out, o0, o1, o2, o3, kv_out, gains_out,
                dk, dv, dqkv, part, recv_a, recv_b, sent_b, a_buf, b0, b1, b2, b3, a_recv, r0, r1, r2, r3,
                kv, kv_work, kv_recv, g_recv,
                ssem, rsem, a_ss, a_rs, b_ss, b_rs, k_ss, k_rs, g_ss, g_rs):
    links, bits, across, sibling, beside, xl, core = neighbours()
    greet(links + [across, sibling, beside])
    t = Tensor(sibling, beside, xl, core, ssem, rsem)
    own = t.own
    state = [dict() for _ in range(NC)]
    first = Reduction([grads.at[p] for p in range(4)], [a_buf.at[p] for p in range(4)], [a_recv.at[p] for p in range(4)],
                      [a_out.at[p] for p in range(4)], a_ss, a_rs, links, bits, across)
    bs = [b0, b1, b2, b3]
    second = Reduction(bs, bs, [r0, r1, r2, r3], [o0, o1, o2, o3], b_ss, b_rs, links, bits, across)
    first.start(0)
    gains_out[...] = gains[...]

    def block(i):
        rows = slice(i * CR, i * CR + CR)
        start, size = key_range(i)
        dh = nt(dattn[i].reshape(CR, 640), wo[...]).astype(BF)
        p = prob[i, :, 0:size]
        dp = nt(dh, v[start:start + size])
        ds = (p * (dp - jnp.sum(p * dp, axis=-1, keepdims=True))).astype(BF)
        dq = nn(ds, k[start:start + size]) * 0.0625
        dk_add = tn(ds, q[rows]) * 0.0625
        dv_add = tn(p.astype(BF), dh)
        fresh = size if i == NC - 1 else (CR if i == NC - 2 else 0)
        if fresh:
            dk[start:start + fresh] = dk_add[:fresh]
            dv[start:start + fresh] = dv_add[:fresh]
        if fresh < size:
            dk[start + fresh:start + size] = dk[start + fresh:start + size] + dk_add[fresh:]
            dv[start + fresh:start + size] = dv[start + fresh:start + size] + dv_add[fresh:]
        cosine, sine = cos_t[rows], sin_t[rows]
        raws = []
        for d, raw, g, at in ((dq, q_raw[rows], g_q, 0), (dk[rows], k_raw[rows], g_k, 256)):
            du = turn_back(d, cosine, sine)
            r = inv_rms(raw)
            gains_out[4:5, at:at + 256] = gains_out[4:5, at:at + 256] + jnp.sum(du * raw * r, axis=0, keepdims=True)
            raws.append(rms_back(raw, r, du * vec(g)).astype(BF))
        raws.append(dv[rows].astype(BF))
        for j in range(3):
            dqkv[rows, 256 * j:256 * j + 256] = raws[j]
        term = nt(raws[0], wq[...]) + nt(raws[1], wk[...]) + nt(raws[2], wv[...])
        part[i] = term.astype(BF).reshape(4, OW, 640)
        state[i]["a"] = t.sum_a(part.at[i], recv_a.at[i])

    def rs_b(i):
        state[i]["b"] = t.sum_b(state[i]["a"], part.at[i], recv_a.at[i], sent_b.at[i], recv_b.at[i])

    def in_stage(i):
        d = t.sum_c(state[i]["b"], part.at[i], recv_a.at[i], recv_b.at[i])
        xv = x[i, own].astype(F32)
        r = inv_rms(xv)
        gains_out[3:4, :] = gains_out[3:4, :] + jnp.sum(d * xv * r, axis=0, keepdims=True)
        in_grad[i, own] = (dmid[i] + rms_back(xv, r, d * vec(g_in))).astype(BF)
        state[i]["g"] = t.gather_a(in_grad.at[i])

    def forward(i):
        state[i]["g"] = t.gather_b(state[i]["g"], in_grad.at[i])

    def swap_gains(i, device):
        return send(gains_out, g_recv.at[i], g_ss.at[i], g_rs.at[i], device)

    def add_gains(i, copy):
        copy.wait()
        gains_out[...] = gains_out[...] + g_recv[i]

    def out_weights():
        g = tn(heads[...], dattn[...].reshape(1024, 640)).astype(BF)
        for c in range(8):
            rows = slice(32 * c, 32 * c + 32)
            b0[c, 80:112] = g[rows, 0:128]
            b1[c, 80:112] = g[rows, 128:256]
            b2[c, 80:112] = g[rows, 256:384]
            b3[c, 0:64] = down4[64 * c:64 * c + 64, :]
            b3[c, 64:96] = g[rows, 384:512]
            b3[c, 96:128] = g[rows, 512:640]

    def next_step(red, step):
        red.finish(step)
        if step < 7:
            red.start(step + 1)

    block(3)
    out_weights()
    rs_b(3)
    block(2)
    next_step(first, 0)
    in_stage(3)
    rs_b(2)
    block(1)
    forward(3)
    in_stage(2)
    rs_b(1)
    next_step(first, 1)
    block(0)
    forward(2)
    in_stage(1)
    next_step(first, 2)
    g = tn(normed[...], dqkv[...]).astype(BF)
    for j in range(4):
        kv[j] = g[:, 256 + 128 * j:384 + 128 * j]
    kc = send(kv.at[pl.ds((1 - core) * 2, 2)], kv_recv.at[pl.ds(0, 2)], k_ss.at[0], k_rs.at[0], sibling)
    rs_b(0)
    for c in range(8):
        b0[c, 0:80] = g[80 * c:80 * c + 80, 0:128]
        b1[c, 0:80] = g[80 * c:80 * c + 80, 128:256]
    forward(1)
    kc.wait()
    for i in range(2):
        kv_work[i] = (kv[core * 2 + i].astype(F32) + kv_recv[i].astype(F32)).astype(BF)
    kc = send(kv_work.at[pl.ds(1 - xl, 1)], kv_recv.at[pl.ds(2, 1)], k_ss.at[1], k_rs.at[1], beside)
    next_step(first, 3)
    in_stage(0)
    gc = swap_gains(0, sibling)
    kc.wait()
    mine = core * 2 + xl
    for c in range(8):
        b2[c, 0:80] = (kv_work[xl, 80 * c:80 * c + 80].astype(F32) + kv_recv[2, 80 * c:80 * c + 80].astype(F32)).astype(BF)
    second.start(0)
    forward(0)
    add_gains(0, gc)
    gc = swap_gains(1, beside)
    next_step(first, 4)
    for step in range(8):
        next_step(second, step)
        if step < 3:
            next_step(first, 5 + step)
        if step < 6:
            add_gains(1 + step, gc)
            if step < 5:
                gc = swap_gains(2 + step, (links + [across])[step])
    for c in range(8):
        kv_out[mine, 80 * c:80 * c + 80] = o2[c, 0:80]
    kc = send(kv_out.at[pl.ds(mine, 1)], kv_out.at[pl.ds(mine, 1)], k_ss.at[2], k_rs.at[2], beside)
    for i in range(NC):
        t.gather_c(state[i]["g"])
    kc.wait()
    kc = send(kv_out.at[pl.ds(core * 2, 2)], kv_out.at[pl.ds(core * 2, 2)], k_ss.at[3], k_rs.at[3], sibling)
    kc.wait()


def unpack_kernel(a, b0, b1, b2, b3, kv, gains, query, key, value, out, gate, up, down, g0, g1, g2, g3, g4, g5):
    for p in range(4):
        cols = slice(128 * p, 128 * p + 128)
        for c in range(8):
            gate[80 * c:80 * c + 80, cols] = a[p, c, 0:80].astype(F32)
            up[80 * c:80 * c + 80, cols] = a[p, c, 80:160].astype(F32)
            down[64 * c:64 * c + 64, cols] = a[p, c, 160:224].astype(F32)
    for c in range(8):
        for p, b in ((0, b0), (1, b1)):
            query[80 * c:80 * c + 80, 128 * p:128 * p + 128] = b[c, 0:80].astype(F32)
            out[32 * c:32 * c + 32, 128 * p:128 * p + 128] = b[c, 80:112].astype(F32)
        out[32 * c:32 * c + 32, 256:384] = b2[c, 80:112].astype(F32)
        down[64 * c:64 * c + 64, 512:640] = b3[c, 0:64].astype(F32)
        out[32 * c:32 * c + 32, 384:512] = b3[c, 64:96].astype(F32)
        out[32 * c:32 * c + 32, 512:640] = b3[c, 96:128].astype(F32)
    for j in range(2):
        key[:, 128 * j:128 * j + 128] = kv[j].astype(F32)
        value[:, 128 * j:128 * j + 128] = kv[2 + j].astype(F32)
    for i, g in ((3, g0), (0, g1), (1, g2), (2, g3)):
        g[...] = gains[i, :]
    g4[...] = gains[4, 0:256]
    g5[...] = gains[4, 256:512]


def backward_part(*operands):
    sds = jax.ShapeDtypeStruct
    dma = pltpu.SemaphoreType.DMA
    v = pltpu.VMEM
    blocks = (NC, 4, OW, 640)
    count = NC * 5
    stacks = pl.pallas_call(
        backward_kernel,
        out_shape=(sds(blocks, BF), sds((4, 8, 224, 128), BF), sds((8, 112, 128), BF), sds((8, 112, 128), BF),
                   sds((8, 112, 128), BF), sds((8, 128, 128), BF), sds((4, 640, 128), BF), sds((8, 640), F32)),
        in_specs=[VMEM] * len(operands),
        out_specs=[VMEM] * 8,
        scratch_shapes=[
            v((1024, 256), F32), v((1024, 256), F32), v((1024, 768), BF), v(blocks, BF),
            v((NC, 2, OW, 640), BF), v((NC, OW, 640), BF), v((NC, OW, 640), BF),
            v((4, 8, 224, 128), BF),
            v((8, 112, 128), BF), v((8, 112, 128), BF), v((8, 112, 128), BF), v((8, 128, 128), BF),
            v((4, 9, 224, 128), BF),
            v((9, 112, 128), BF), v((9, 112, 128), BF), v((9, 112, 128), BF), v((9, 128, 128), BF),
            v((4, 640, 128), BF), v((2, 640, 128), BF), v((3, 640, 128), BF), v((7, 8, 640), F32),
            dma((count,)), dma((count,)),
            dma((4, 8)), dma((4, 8)), dma((4, 8)), dma((4, 8)), dma((4,)), dma((4,)), dma((7,)), dma((7,)),
        ],
        compiler_params=pltpu.CompilerParams(collective_id=7, has_side_effects=True, vmem_limit_bytes=VMEM_LIMIT),
        name="backward_part",
    )(*operands)
    outs = pl.pallas_call(
        unpack_kernel,
        out_shape=(sds((640, 256), F32), sds((640, 256), F32), sds((640, 256), F32), sds((256, 640), F32),
                   sds((640, 512), F32), sds((640, 512), F32), sds((512, 640), F32),
                   sds((640,), F32), sds((640,), F32), sds((640,), F32), sds((640,), F32),
                   sds((256,), F32), sds((256,), F32)),
        in_specs=[VMEM] * 7,
        out_specs=[VMEM] * 13,
        compiler_params=pltpu.CompilerParams(vmem_limit_bytes=VMEM_LIMIT),
        name="unpack_grads",
    )(*stacks[1:])
    return stacks[0], outs


def rope_tables(positions, head_size):
    half_size = head_size // 2
    inv_freq = ROPE_BASE ** (-2.0 * jnp.arange(half_size, dtype=jnp.float32) / head_size)
    angles = positions.astype(jnp.float32)[:, None] * inv_freq[None, :]
    return (jnp.cos(angles), jnp.sin(angles))


def local(
    inputs,
    segments,
    positions,
    cotangent,
    w_query,
    w_key,
    w_value,
    w_out,
    w_gate,
    w_up,
    w_down,
    g_attn_in,
    g_attn_out,
    g_ffn_in,
    g_ffn_out,
    g_query,
    g_key,
):
    blocks = (NC, 4, OW, 640)
    x = inputs.reshape(blocks)
    cos_t, sin_t = rope_tables(positions, 256)
    (output, dattn, dmid, grads, down4, gains, normed, q_raw, k_raw, q, k, v, prob, heads) = forward_part(
        x,
        cotangent.reshape(blocks),
        segments.reshape(1, 1024),
        cos_t,
        sin_t,
        (w_query, w_key, w_value, w_out, w_gate, w_up, w_down),
        (g_attn_in, g_attn_out, g_ffn_in, g_ffn_out, g_query, g_key),
    )
    input_grad, summed = backward_part(
        dattn, dmid, x, heads, prob, q, k, v, q_raw, k_raw, cos_t, sin_t, normed,
        w_query, w_key, w_value, w_out, g_attn_in, g_query, g_key, grads, down4, gains,
    )
    return (output.reshape(1024, 640), input_grad.reshape(1024, 640), *summed)


def solution(mesh):
    placed = (
        P("dp", None),
        P("dp"),
        P("dp"),
        P("dp", None),
        P(None, "tensor"),
        P(),
        P(),
        P("tensor", None),
        P(None, "tensor"),
        P(None, "tensor"),
        P("tensor", None),
        P(),
        P(),
        P(),
        P(),
        P(),
        P(),
    )
    return jax.shard_map(
        local,
        mesh=mesh,
        in_specs=placed,
        out_specs=(
            P("dp", None),
            P("dp", None),
            P(None, "tensor"),
            P(),
            P(),
            P("tensor", None),
            P(None, "tensor"),
            P(None, "tensor"),
            P("tensor", None),
            P(),
            P(),
            P(),
            P(),
            P(),
            P(),
        ),
        check_vma=False,
    )
```

```python
import jax, jax.numpy as jnp
from jax import lax
from jax.experimental import pallas as pl
from jax.experimental.pallas import tpu as pltpu
from jax.sharding import PartitionSpec as P

WINDOW = 512
EPSILON = 1e-06
ROPE_BASE = 10000.0
NEG_LARGE = -1e30

MESH = pl.DeviceIdType.MESH
BF = jnp.bfloat16
F32 = jnp.float32
VMEM = pl.BlockSpec(memory_space=pltpu.VMEM)
VMEM_LIMIT = 60 * 1024 * 1024


def neighbours():
    dp = lax.axis_index("dp")
    t = lax.axis_index("tensor")
    z = lax.rem(dp, 4)
    y = lax.rem(dp // 4, 4)
    xh = dp // 16
    xl = t // 2
    core = lax.rem(t, 2)
    ya = y + 1 - 2 * lax.rem(y, 2)
    za = z + 1 - 2 * lax.rem(z, 2)
    links = [
        (dp + (ya - y) * 4, t),
        (dp + (za - z), t),
        (dp + (3 - 2 * y) * 4, t),
        (dp + (3 - 2 * z), t),
    ]
    bits = [lax.rem((y + 1) // 2, 2), lax.rem((z + 1) // 2, 2), y // 2, z // 2]
    across = (dp + 16 - 32 * xh, t)
    sibling = (dp, t + 1 - 2 * core)
    beside = (dp, t + 2 - 4 * xl)
    return links, bits, across, sibling, beside, xl, core


def greet(devices):
    barrier = pltpu.get_barrier_semaphore()
    for d in devices:
        pl.semaphore_signal(barrier, inc=1, device_id=d, device_id_type=MESH)
    pl.semaphore_wait(barrier, len(devices))


def send(src, dst, ssem, rsem, device):
    copy = pltpu.make_async_remote_copy(
        src_ref=src, dst_ref=dst, send_sem=ssem, recv_sem=rsem, device_id=device, device_id_type=MESH
    )
    copy.start()
    return copy


class Reduction:
    def __init__(self, ins, bufs, recvs, outs, ssem, rsem, links, bits, across):
        self.ins, self.bufs, self.recvs, self.outs, self.ssem, self.rsem = ins, bufs, recvs, outs, ssem, rsem
        self.links, self.bits, self.across = links, bits, across
        self.base = [jnp.int32(0)] * 4
        self.bases = []
        self.copies = None

    def start(self, step):
        copies = []
        for p in range(4):
            buf, recv = (self.ins if step == 0 else self.bufs)[p], self.recvs[p]
            ss, rs = self.ssem.at[p, step], self.rsem.at[p, step]
            if step < 3:
                n = 4 >> step
                bit = self.bits[(p + step) % 4]
                there = self.base[p] + (1 - bit) * n
                self.base[p] = self.base[p] + bit * n
                at = (0, 4, 6)[step]
                src, dst, dev = buf.at[pl.ds(there, n)], recv.at[pl.ds(at, n)], self.links[(p + step) % 4]
            elif step < 5:
                dev = self.links[(p + 3) % 4] if step == 3 else self.across
                src, dst = buf.at[pl.ds(self.base[p], 1)], recv.at[pl.ds(4 + step, 1)]
            else:
                s = 7 - step
                n = 4 >> s
                bit = self.bits[(p + s) % 4]
                src = dst = self.outs[p].at[pl.ds(self.base[p], n)]
                self.base[p] = self.base[p] - bit * n
                dev = self.links[(p + s) % 4]
            copies.append(send(src, dst, ss, rs, dev))
        self.copies = copies

    def finish(self, step):
        for p in range(4):
            buf, recv = self.bufs[p], self.recvs[p]
            into = self.outs[p] if step == 4 else buf
            buf = self.ins[p] if step == 0 else buf
            self.copies[p].wait()
            if step < 5:
                n = (4, 2, 1, 1, 1)[step]
                at = (0, 4, 6, 7, 8)[step]
                base = self.base[p]

                def add(i, carry):
                    into[base + i] = (buf[base + i].astype(F32) + recv[at + i].astype(F32)).astype(BF)
                    return carry

                lax.fori_loop(0, n, add, 0)


NC = 4
CR = 1024 // NC
OW = CR // 2
C0 = 0.7978845608028654
C1 = 0.044715


def nt(a, b):
    return lax.dot_general(a, b, (((1,), (1,)), ((), ())), preferred_element_type=F32)


def tn(a, b):
    return lax.dot_general(a, b, (((0,), (0,)), ((), ())), preferred_element_type=F32)


def nn(a, b):
    return jnp.dot(a, b, preferred_element_type=F32)


def inv_rms(v):
    return lax.rsqrt(jnp.mean(v * v, axis=-1, keepdims=True) + EPSILON)


def rms_back(v, r, du):
    return r * du - v * (r * r * r * jnp.mean(du * v, axis=-1, keepdims=True))


def turn(v, cosine, sine):
    a, b = v[:, :128], v[:, 128:]
    return jnp.concatenate([a * cosine - b * sine, b * cosine + a * sine], axis=-1)


def turn_back(v, cosine, sine):
    a, b = v[:, :128], v[:, 128:]
    return jnp.concatenate([a * cosine + b * sine, b * cosine - a * sine], axis=-1)


def key_range(i):
    first = max(0, (i - 2) * CR)
    return first, (i + 1) * CR - first


def vec(g):
    return g[...]


class KeyValue:
    def __init__(self, kv, work, recv, last, out, ssem, rsem, links, bits, across, sibling, beside, xl, core):
        self.kv, self.work, self.recv, self.last, self.out, self.ssem, self.rsem = kv, work, recv, last, out, ssem, rsem
        self.xl, self.core = xl, core
        self.mine = core * 2 + xl
        self.b0, self.b1 = bits[0], bits[1]
        self.at = self.b0 * 2 + self.b1
        self.devices = [sibling, beside, links[0], links[1], links[2], links[3], across, links[1], links[0], beside, sibling]

    def start(self, step):
        work, recv, last, out, at, b0, mine = self.work, self.recv, self.last, self.out, self.at, self.b0, self.mine
        if step == 0:
            src, dst = self.kv.at[pl.ds((1 - self.core) * 2, 2)], recv.at[pl.ds(0, 2)]
        elif step == 1:
            src, dst = work.at[1 - self.xl], recv.at[2]
        elif step == 2:
            src, dst = last.at[pl.ds((1 - b0) * 2, 2)], recv.at[3, pl.ds(0, 2)]
        elif step == 3:
            src, dst = last.at[b0 * 2 + 1 - self.b1], recv.at[3, 2]
        elif step == 4:
            src, dst = last.at[at], recv.at[3, 3]
        elif step < 7:
            src, dst = last.at[at], recv.at[4, step - 5]
        elif step == 7:
            src = dst = out.at[mine, at]
        elif step == 8:
            src = dst = out.at[mine, pl.ds(b0 * 2, 2)]
        elif step == 9:
            src = dst = out.at[mine]
        else:
            src = dst = out.at[pl.ds(self.core * 2, 2)]
        self.copy = send(src, dst, self.ssem.at[step], self.rsem.at[step], self.devices[step])

    def finish(self, step):
        self.copy.wait()
        kv, work, recv, last, at = self.kv, self.work, self.recv, self.last, self.at
        if step == 0:
            for i in range(2):
                work[i] = (kv[self.core * 2 + i].astype(F32) + recv[i].astype(F32)).astype(BF)
        elif step == 1:
            last[...] = (work[self.xl].astype(F32) + recv[2].astype(F32)).astype(BF)
        elif step == 2:
            for i in range(2):
                last[self.b0 * 2 + i] = (last[self.b0 * 2 + i].astype(F32) + recv[3, i].astype(F32)).astype(BF)
        elif step < 5:
            last[at] = (last[at].astype(F32) + recv[3, step - 1].astype(F32)).astype(BF)
        elif step == 5:
            last[at] = (last[at].astype(F32) + recv[4, 0].astype(F32)).astype(BF)
        elif step == 6:
            self.out[self.mine, at] = (last[at].astype(F32) + recv[4, 1].astype(F32)).astype(BF)


def layer_kernel(x, cot, segs, cos_t, sin_t, wq, wk, wv, wo, wg, wu, wd, g_in, g_ao, g_fi, g_fo, g_q, g_k,
                 output, in_grad, a_out, o0, o1, o2, o3, kv_out, gains,
                 normed, q_raw, k_raw, q, k, v, prob, heads, part, ffn_g, dffn_g, dattn, hid, act_a, act_b, dgate, dup,
                 attn_own, mid_own, recv_a, recv_b, dk, dv, dqkv,
                 a_buf, b0, b1, b2, b3, a_recv, r0, r1, r2, r3, kv, kv_work, kv_recv, kv_last, g_recv,
                 ssem, rsem, a_ss, a_rs, b_ss, b_rs, k_ss, k_rs, g_ss, g_rs):
    links, bits, across, sibling, beside, xl, core = neighbours()
    greet(links + [across, sibling, beside])
    own = core
    state = [dict() for _ in range(NC)]
    used = [0]

    def post(src, dst, device):
        i = used[0]
        used[0] += 1
        return send(src, dst, ssem.at[i], rsem.at[i], device)

    def share(e, c):
        state[c]["a"] = post(part.at[e, c, 1 - own], recv_a.at[e, c], sibling)

    def exchange(e):
        def run(c):
            state[c]["a"].wait()
            part[e, c, own] = (part[e, c, own].astype(F32) + recv_a[e, c].astype(F32)).astype(BF)
            state[c]["b"] = post(part.at[e, c, own], recv_b.at[e, c], beside)
        return run

    def total(e, c):
        state[c]["b"].wait()
        return part[e, c, own].astype(F32) + recv_b[e, c].astype(F32)

    def give(buf, c):
        return post(buf.at[c, own], buf.at[c, own], sibling)

    def keys_stage():
        for c in range(NC - 1, -1, -1):
            rows = slice(c * CR, c * CR + CR)
            xv = x[c].reshape(CR, 640).astype(F32)
            n = (xv * inv_rms(xv) * vec(g_in)).astype(BF)
            normed[rows] = n
            raw = nn(n, wk[...])
            k_raw[rows] = raw
            k[rows] = turn(raw * inv_rms(raw) * vec(g_k), cos_t[rows], sin_t[rows]).astype(BF)
            v[rows] = nn(n, wv[...]).astype(BF)

    def attention_stage(c):
        rows = slice(c * CR, c * CR + CR)
        raw = nn(normed[rows], wq[...])
        q_raw[rows] = raw
        q_low = turn(raw * inv_rms(raw) * vec(g_q), cos_t[rows], sin_t[rows]).astype(BF)
        q[rows] = q_low
        first, size = key_range(c)
        keys = slice(first, first + size)
        scores = nt(q_low, k[keys]) * 0.0625
        gap = c * CR - first + lax.broadcasted_iota(jnp.int32, (CR, size), 0) - lax.broadcasted_iota(jnp.int32, (CR, size), 1)
        seg_rows = jnp.broadcast_to(segs[:, rows], (128, CR)).T[:, :1]
        allowed = (gap >= 0) & (gap < WINDOW) & (seg_rows == segs[:, keys])
        masked = jnp.where(allowed, scores, NEG_LARGE)
        e = jnp.where(allowed, jnp.exp(masked - jnp.max(masked, axis=-1, keepdims=True)), 0.0)
        p = e / jnp.sum(e, axis=-1, keepdims=True)
        prob[c, :, 0:size] = p
        h = nn(p.astype(BF), v[keys]).astype(BF)
        heads[rows] = h
        part[0, c] = nn(h, wo[...]).astype(BF).reshape(2, OW, 640)
        share(0, c)

    def mid_stage(c):
        a = total(0, c)
        attn_own[c] = a
        mid = x[c, own].astype(F32) + a * inv_rms(a) * vec(g_ao)
        mid_own[c] = mid
        ffn_g[c, own] = (mid * inv_rms(mid) * vec(g_fi)).astype(BF)
        state[c]["g"] = give(ffn_g, c)

    def up_stage(c):
        state[c]["g"].wait()
        f = ffn_g[c].reshape(CR, 640)
        gate = nn(f, wg[...])
        up = nn(f, wu[...])
        th = jnp.tanh(C0 * (gate + C1 * gate * gate * gate))
        half = 0.5 * (1.0 + th)
        act = gate * half
        slope = half + 0.5 * gate * (1.0 - th * th) * (C0 * (1.0 + 3.0 * C1 * gate * gate))
        act_a[c] = up * slope
        act_b[c] = act
        h = (act * up).astype(BF)
        hid[c] = h
        part[1, c] = nn(h, wd[...]).astype(BF).reshape(2, OW, 640)
        share(1, c)

    def out_stage(c):
        s = total(1, c)
        r = inv_rms(s)
        ct = cot[c, own].astype(F32)
        dffn_g[c, own] = rms_back(s, r, ct * vec(g_fo)).astype(BF)
        state[c]["g"] = give(dffn_g, c)
        output[c, own] = (mid_own[c] + s * r * vec(g_fo)).astype(BF)
        state[c]["o"] = give(output, c)
        gains[2:3, :] = gains[2:3, :] + jnp.sum(ct * s * r, axis=0, keepdims=True)

    def down_stage(c):
        state[c]["g"].wait()
        d = dffn_g[c].reshape(CR, 640)
        dh = nt(d, wd[...])
        dg = (dh * act_a[c]).astype(BF)
        du = (dh * act_b[c]).astype(BF)
        dgate[c] = dg
        dup[c] = du
        part[2, c] = (nt(dg, wg[...]) + nt(du, wu[...])).astype(BF).reshape(2, OW, 640)
        share(2, c)

    def attn_stage(c):
        d = total(2, c)
        mid, a = mid_own[c], attn_own[c]
        r = inv_rms(mid)
        gains[1:2, :] = gains[1:2, :] + jnp.sum(d * mid * r, axis=0, keepdims=True)
        dmid = cot[c, own].astype(F32) + rms_back(mid, r, d * vec(g_fi))
        mid_own[c] = dmid
        r = inv_rms(a)
        gains[0:1, :] = gains[0:1, :] + jnp.sum(dmid * a * r, axis=0, keepdims=True)
        dattn[c, own] = rms_back(a, r, dmid * vec(g_ao)).astype(BF)
        state[c]["g"] = give(dattn, c)

    def back_stage(i):
        state[i]["g"].wait()
        rows = slice(i * CR, i * CR + CR)
        start, size = key_range(i)
        dh = nt(dattn[i].reshape(CR, 640), wo[...]).astype(BF)
        p = prob[i, :, 0:size]
        dp = nt(dh, v[start:start + size])
        ds = (p * (dp - jnp.sum(p * dp, axis=-1, keepdims=True))).astype(BF)
        dq = nn(ds, k[start:start + size]) * 0.0625
        dk_add = tn(ds, q[rows]) * 0.0625
        dv_add = tn(p.astype(BF), dh)
        fresh = size if i == NC - 1 else (CR if i == NC - 2 else 0)
        if fresh:
            dk[start:start + fresh] = dk_add[:fresh]
            dv[start:start + fresh] = dv_add[:fresh]
        if fresh < size:
            dk[start + fresh:start + size] = dk[start + fresh:start + size] + dk_add[fresh:]
            dv[start + fresh:start + size] = dv[start + fresh:start + size] + dv_add[fresh:]
        cosine, sine = cos_t[rows], sin_t[rows]
        raws = []
        for d, raw, g, at in ((dq, q_raw[rows], g_q, 0), (dk[rows], k_raw[rows], g_k, 256)):
            du = turn_back(d, cosine, sine)
            r = inv_rms(raw)
            gains[4:5, at:at + 256] = gains[4:5, at:at + 256] + jnp.sum(du * raw * r, axis=0, keepdims=True)
            raws.append(rms_back(raw, r, du * vec(g)).astype(BF))
        raws.append(dv[rows].astype(BF))
        for j in range(3):
            dqkv[rows, 256 * j:256 * j + 256] = raws[j]
        term = nt(raws[0], wq[...]) + nt(raws[1], wk[...]) + nt(raws[2], wv[...])
        part[3, i] = term.astype(BF).reshape(2, OW, 640)
        share(3, i)

    def in_stage(i):
        d = total(3, i)
        xv = x[i, own].astype(F32)
        r = inv_rms(xv)
        gains[3:4, :] = gains[3:4, :] + jnp.sum(d * xv * r, axis=0, keepdims=True)
        in_grad[i, own] = (mid_own[i] + rms_back(xv, r, d * vec(g_in))).astype(BF)
        state[i]["g"] = give(in_grad, i)

    def weights_down():
        g = tn(hid[...].reshape(1024, 512), dffn_g[...].reshape(1024, 640)).astype(BF)
        for s in range(8):
            for p in range(4):
                a_buf[p, s, 160:224] = g[64 * s:64 * s + 64, 128 * p:128 * p + 128]
            b2[s, 0:64] = g[64 * s:64 * s + 64, 512:640]

    def weights_ffn(source, at):
        g = tn(ffn_g[...].reshape(1024, 640), source[...].reshape(1024, 512)).astype(BF)
        for s in range(8):
            for p in range(4):
                a_buf[p, s, at:at + 80] = g[80 * s:80 * s + 80, 128 * p:128 * p + 128]

    def weights_out():
        g = tn(heads[...], dattn[...].reshape(1024, 640)).astype(BF)
        for c in range(8):
            rows = slice(32 * c, 32 * c + 32)
            b0[c, 80:112] = g[rows, 0:128]
            b1[c, 80:112] = g[rows, 128:256]
            b2[c, 64:96] = g[rows, 256:384]
            b3[c, 0:32] = g[rows, 384:512]
            b3[c, 32:64] = g[rows, 512:640]

    def weights_in():
        g = tn(normed[...], dqkv[...]).astype(BF)
        for j in range(4):
            kv[j] = g[:, 256 + 128 * j:384 + 128 * j].reshape(4, 160, 128)
        for c in range(8):
            b0[c, 0:80] = g[80 * c:80 * c + 80, 0:128]
            b1[c, 0:80] = g[80 * c:80 * c + 80, 128:256]

    bufs = [a_buf.at[p] for p in range(4)]
    first = Reduction(bufs, bufs, [a_recv.at[p] for p in range(4)], [a_out.at[p] for p in range(4)], a_ss, a_rs, links, bits, across)
    bufs = [b0, b1, b2, b3]
    second = Reduction(bufs, bufs, [r0, r1, r2, r3], [o0, o1, o2, o3], b_ss, b_rs, links, bits, across)
    third = KeyValue(kv, kv_work, kv_recv, kv_last, kv_out, k_ss, k_rs, links, bits, across, sibling, beside, xl, core)
    done = {}

    def begin(red):
        red.start(0)
        done[id(red)] = 0

    def advance(red, steps):
        at = done[id(red)]
        if at < steps:
            red.finish(at)
            at += 1
            if at < steps:
                red.start(at)
            done[id(red)] = at

    gains[...] = jnp.zeros_like(gains)
    keys_stage()
    stages = [
        attention_stage, exchange(0), mid_stage, up_stage, exchange(1), out_stage, down_stage, exchange(2), attn_stage,
        back_stage, exchange(3), in_stage,
    ]
    after = AFTER
    for tick in range(len(stages) + NC - 1):
        for p in range(NC):
            s = tick - p
            if 0 <= s < len(stages):
                stages[s](NC - 1 - p)
                for job in after.get((s, p), ()):
                    if job == "down":
                        weights_down()
                    elif job == "gate":
                        weights_ffn(dgate, 0)
                    elif job == "up":
                        weights_ffn(dup, 80)
                        begin(first)
                    elif job == "out":
                        weights_out()
                    elif job == "in":
                        weights_in()
                        begin(third)
                        begin(second)
                    elif job == "1":
                        advance(first, 8)
                    elif job == "2":
                        advance(second, 8)
                    elif job == "3":
                        advance(third, 11)
    gains[0:4, :] = gains[0:4, :] * 0.5
    order = [sibling, beside] + links + [across]
    for i in range(11):
        if i < 7:
            gc = send(gains, g_recv.at[i], g_ss.at[i], g_rs.at[i], order[i])
        advance(third, 11)
        advance(second, 8)
        advance(first, 8)
        if i < 7:
            gc.wait()
            gains[...] = gains[...] + g_recv[i]
    for c in range(NC):
        state[c]["o"].wait()
        state[c]["g"].wait()


AFTER = {
    (6, 3): ("down", "gate", "up"),
    (9, 1): ("1",),
    (9, 2): ("1",),
    (9, 3): ("out", "in", "1"),
    (10, 3): ("1", "3"),
    (11, 2): ("2", "3"),
    (11, 3): ("1", "2", "3"),
}


def unpack_kernel(a, b0, b1, b2, b3, kv, gains, query, key, value, out, gate, up, down, g0, g1, g2, g3, g4, g5):
    for p in range(4):
        cols = slice(128 * p, 128 * p + 128)
        for c in range(8):
            gate[80 * c:80 * c + 80, cols] = a[p, c, 0:80].astype(F32)
            up[80 * c:80 * c + 80, cols] = a[p, c, 80:160].astype(F32)
            down[64 * c:64 * c + 64, cols] = a[p, c, 160:224].astype(F32)
    for c in range(8):
        for p, b in ((0, b0), (1, b1)):
            query[80 * c:80 * c + 80, 128 * p:128 * p + 128] = b[c, 0:80].astype(F32)
            out[32 * c:32 * c + 32, 128 * p:128 * p + 128] = b[c, 80:112].astype(F32)
        out[32 * c:32 * c + 32, 256:384] = b2[c, 64:96].astype(F32)
        down[64 * c:64 * c + 64, 512:640] = b2[c, 0:64].astype(F32)
        out[32 * c:32 * c + 32, 384:512] = b3[c, 0:32].astype(F32)
        out[32 * c:32 * c + 32, 512:640] = b3[c, 32:64].astype(F32)
    for j in range(2):
        key[:, 128 * j:128 * j + 128] = kv[j].reshape(640, 128).astype(F32)
        value[:, 128 * j:128 * j + 128] = kv[2 + j].reshape(640, 128).astype(F32)
    for i, g in ((3, g0), (0, g1), (1, g2), (2, g3)):
        g[...] = gains[i, :]
    g4[...] = gains[4, 0:256]
    g5[...] = gains[4, 256:512]


def layer(*operands):
    sds = jax.ShapeDtypeStruct
    dma = pltpu.SemaphoreType.DMA
    v = pltpu.VMEM
    blocks = (NC, 2, OW, 640)
    half = (NC, OW, 640)
    count = NC * 12
    stacks = pl.pallas_call(
        layer_kernel,
        out_shape=(sds(blocks, BF), sds(blocks, BF), sds((4, 8, 224, 128), BF), sds((8, 112, 128), BF), sds((8, 112, 128), BF),
                   sds((8, 96, 128), BF), sds((8, 64, 128), BF), sds((4, 4, 160, 128), BF), sds((8, 640), F32)),
        in_specs=[VMEM] * len(operands),
        out_specs=[VMEM] * 9,
        scratch_shapes=[
            v((1024, 640), BF), v((1024, 256), F32), v((1024, 256), F32), v((1024, 256), BF), v((1024, 256), BF),
            v((1024, 256), BF), v((NC, CR, 768), F32), v((1024, 256), BF), v((4, *blocks), BF), v(blocks, BF), v(blocks, BF),
            v(blocks, BF), v((NC, CR, 512), BF), v((NC, CR, 512), F32), v((NC, CR, 512), F32), v((NC, CR, 512), BF),
            v((NC, CR, 512), BF), v(half, F32), v(half, F32), v((4, *half), BF), v((4, *half), BF),
            v((1024, 256), F32), v((1024, 256), F32), v((1024, 768), BF),
            v((4, 8, 224, 128), BF),
            v((8, 112, 128), BF), v((8, 112, 128), BF), v((8, 96, 128), BF), v((8, 64, 128), BF),
            v((4, 9, 224, 128), BF),
            v((9, 112, 128), BF), v((9, 112, 128), BF), v((9, 96, 128), BF), v((9, 64, 128), BF),
            v((4, 4, 160, 128), BF), v((2, 4, 160, 128), BF), v((5, 4, 160, 128), BF), v((4, 160, 128), BF),
            v((7, 8, 640), F32),
            dma((count + 16,)), dma((count + 16,)),
            dma((4, 8)), dma((4, 8)), dma((4, 8)), dma((4, 8)), dma((11,)), dma((11,)), dma((7,)), dma((7,)),
        ],
        compiler_params=pltpu.CompilerParams(collective_id=7, has_side_effects=True, vmem_limit_bytes=VMEM_LIMIT),
        name="layer",
    )(*operands)
    outs = pl.pallas_call(
        unpack_kernel,
        out_shape=(sds((640, 256), F32), sds((640, 256), F32), sds((640, 256), F32), sds((256, 640), F32),
                   sds((640, 512), F32), sds((640, 512), F32), sds((512, 640), F32),
                   sds((640,), F32), sds((640,), F32), sds((640,), F32), sds((640,), F32),
                   sds((256,), F32), sds((256,), F32)),
        in_specs=[VMEM] * 7,
        out_specs=[VMEM] * 13,
        compiler_params=pltpu.CompilerParams(vmem_limit_bytes=VMEM_LIMIT),
        name="unpack_grads",
    )(*stacks[2:])
    return stacks[0], stacks[1], outs


def rope_tables(positions, head_size):
    half_size = head_size // 2
    inv_freq = ROPE_BASE ** (-2.0 * jnp.arange(half_size, dtype=jnp.float32) / head_size)
    angles = positions.astype(jnp.float32)[:, None] * inv_freq[None, :]
    return (jnp.cos(angles), jnp.sin(angles))


def local(
    inputs,
    segments,
    positions,
    cotangent,
    w_query,
    w_key,
    w_value,
    w_out,
    w_gate,
    w_up,
    w_down,
    g_attn_in,
    g_attn_out,
    g_ffn_in,
    g_ffn_out,
    g_query,
    g_key,
):
    blocks = (NC, 2, OW, 640)
    cos_t, sin_t = rope_tables(positions, 256)
    output, input_grad, summed = layer(
        inputs.reshape(blocks), cotangent.reshape(blocks), segments.reshape(1, 1024), cos_t, sin_t,
        w_query, w_key, w_value, w_out, w_gate, w_up, w_down,
        g_attn_in, g_attn_out, g_ffn_in, g_ffn_out, g_query, g_key,
    )
    return (output.reshape(1024, 640), input_grad.reshape(1024, 640), *summed)


def solution(mesh):
    placed = (
        P("dp", None),
        P("dp"),
        P("dp"),
        P("dp", None),
        P(None, "tensor"),
        P(),
        P(),
        P("tensor", None),
        P(None, "tensor"),
        P(None, "tensor"),
        P("tensor", None),
        P(),
        P(),
        P(),
        P(),
        P(),
        P(),
    )
    return jax.shard_map(
        local,
        mesh=mesh,
        in_specs=placed,
        out_specs=(
            P("dp", None),
            P("dp", None),
            P(None, "tensor"),
            P(),
            P(),
            P("tensor", None),
            P(None, "tensor"),
            P(None, "tensor"),
            P("tensor", None),
            P(),
            P(),
            P(),
            P(),
            P(),
            P(),
        ),
        check_vma=False,
    )
```

```python
import jax, jax.numpy as jnp
from jax import lax
from jax.experimental import pallas as pl
from jax.experimental.pallas import tpu as pltpu
from jax.sharding import PartitionSpec as P

WINDOW = 512
EPSILON = 1e-06
ROPE_BASE = 10000.0
NEG_LARGE = -1e30

MESH = pl.DeviceIdType.MESH
BF = jnp.bfloat16
F32 = jnp.float32
VMEM = pl.BlockSpec(memory_space=pltpu.VMEM)
VMEM_LIMIT = 60 * 1024 * 1024


def neighbours():
    dp = lax.axis_index("dp")
    t = lax.axis_index("tensor")
    z = lax.rem(dp, 4)
    y = lax.rem(dp // 4, 4)
    xh = dp // 16
    xl = t // 2
    core = lax.rem(t, 2)
    ya = y + 1 - 2 * lax.rem(y, 2)
    za = z + 1 - 2 * lax.rem(z, 2)
    links = [
        (dp + (ya - y) * 4, t),
        (dp + (za - z), t),
        (dp + (3 - 2 * y) * 4, t),
        (dp + (3 - 2 * z), t),
    ]
    bits = [lax.rem((y + 1) // 2, 2), lax.rem((z + 1) // 2, 2), y // 2, z // 2]
    across = (dp + 16 - 32 * xh, t)
    sibling = (dp, t + 1 - 2 * core)
    beside = (dp, t + 2 - 4 * xl)
    corner = (dp + 16 - 32 * xh, t + 2 - 4 * xl)
    return links, bits, across, sibling, beside, corner, xl, core


def greet(devices):
    barrier = pltpu.get_barrier_semaphore()
    for d in devices:
        pl.semaphore_signal(barrier, inc=1, device_id=d, device_id_type=MESH)
    pl.semaphore_wait(barrier, len(devices))


def send(src, dst, ssem, rsem, device):
    copy = pltpu.make_async_remote_copy(
        src_ref=src, dst_ref=dst, send_sem=ssem, recv_sem=rsem, device_id=device, device_id_type=MESH
    )
    copy.start()
    return copy


class Reduction:
    def __init__(self, ids, bufs, recvs, outs, ssem, rsem, links, bits, across, more=()):
        self.ids, self.bufs, self.recvs, self.outs, self.ssem, self.rsem = ids, bufs, recvs, outs, ssem, rsem
        self.links, self.bits, self.across, self.more = links, bits, across, more
        self.base = [jnp.int32(0)] * len(ids)
        self.at = 0

    def start(self):
        step = self.at
        self.copies = []
        for i, p in enumerate(self.ids):
            buf, recv = self.bufs[i], self.recvs[i]
            ss, rs = self.ssem.at[i, step], self.rsem.at[i, step]
            if step < 3:
                n = 4 >> step
                bit = self.bits[(p + step) % 4]
                there = self.base[i] + (1 - bit) * n
                self.base[i] = self.base[i] + bit * n
                at = (0, 4, 6)[step]
                src, dst, dev = buf.at[pl.ds(there, n)], recv.at[pl.ds(at, n)], self.links[(p + step) % 4]
            elif step < 5:
                dev = self.links[(p + 3) % 4] if step == 3 else self.across
                src, dst = buf.at[self.base[i]], recv.at[4 + step]
            else:
                s = 7 - step
                n = 4 >> s
                bit = self.bits[(p + s) % 4]
                src = dst = self.outs[i].at[pl.ds(self.base[i], n)]
                self.base[i] = self.base[i] - bit * n
                dev = self.links[(p + s) % 4]
            self.copies.append(send(src, dst, ss, rs, dev))
            if step == 4:
                for j, dev in enumerate(self.more):
                    self.copies.append(send(buf.at[self.base[i], pl.ds(0, 80)], recv.at[9 + j, pl.ds(0, 80)],
                                            self.ssem.at[i, 8 + j], self.rsem.at[i, 8 + j], dev))

    def advance(self):
        step = self.at
        if step == 8:
            return
        for copy in self.copies:
            copy.wait()
        if step < 5:
            n = (4, 2, 1, 1, 1)[step]
            at = (0, 4, 6, 7, 8)[step]
            for i in range(len(self.ids)):
                buf, recv, base = self.bufs[i], self.recvs[i], self.base[i]
                into = self.outs[i] if step == 4 else buf

                def add(j, carry):
                    into[base + j] = (buf[base + j].astype(F32) + recv[at + j].astype(F32)).astype(BF)
                    return carry

                lax.fori_loop(0, n, add, 0)
                if step == 4 and self.more:
                    pair = recv[9, 0:80].astype(F32) + recv[10, 0:80].astype(F32)
                    into[base, 0:80] = (buf[base, 0:80].astype(F32) + recv[8, 0:80].astype(F32) + pair).astype(BF)
        self.at = step + 1
        if self.at < 8:
            self.start()


NC = 4
CR = 1024 // NC
OW = CR // 2
C0 = 0.7978845608028654
C1 = 0.044715


def nt(a, b):
    return lax.dot_general(a, b, (((1,), (1,)), ((), ())), preferred_element_type=F32)


def tn(a, b):
    return lax.dot_general(a, b, (((0,), (0,)), ((), ())), preferred_element_type=F32)


def nn(a, b):
    return jnp.dot(a, b, preferred_element_type=F32)


def inv_rms(v):
    return lax.rsqrt(jnp.mean(v * v, axis=-1, keepdims=True) + EPSILON)


def rms_back(v, r, du):
    return r * du - v * (r * r * r * jnp.mean(du * v, axis=-1, keepdims=True))


def turn(v, cosine, sine):
    a, b = v[:, :128], v[:, 128:]
    return jnp.concatenate([a * cosine - b * sine, b * cosine + a * sine], axis=-1)


def turn_back(v, cosine, sine):
    a, b = v[:, :128], v[:, 128:]
    return jnp.concatenate([a * cosine + b * sine, b * cosine - a * sine], axis=-1)


def key_range(i):
    first = max(0, (i - 2) * CR)
    return first, (i + 1) * CR - first


def vec(g):
    return g[...]


def layer_kernel(x, cot, segs, cos_t, sin_t, wq, wk, wv, wo, wg, wu, wd, g_in, g_ao, g_fi, g_fo, g_q, g_k,
                 output, in_grad, a_out, o0, o1, o2, o3, kv_out, gains,
                 normed, q_raw, k_raw, q, k, v, prob, heads, part, ffn_g, dffn_g, dattn, hid, act_a, act_b, dgate, dup,
                 attn_own, mid_own, recv_a, recv_b, dk, dv, dqkv,
                 a_buf, b0, b1, b2, b3, a_recv, r0, r1, r2, r3, kv, kv_recv, g_recv,
                 ssem, rsem, a_ss, a_rs, b_ss, b_rs, c_ss, c_rs, k_ss, k_rs, g_ss, g_rs):
    links, bits, across, sibling, beside, corner, xl, core = neighbours()
    greet(links + [across, sibling, beside, corner])
    own = core
    state = [dict() for _ in range(NC)]
    used = [0]

    def post(src, dst, device):
        i = used[0]
        used[0] += 1
        return send(src, dst, ssem.at[i], rsem.at[i], device)

    def share(e, c):
        state[c]["a"] = post(part.at[e, c, 1 - own], recv_a.at[e, c], sibling)

    def exchange(e):
        def run(c):
            state[c]["a"].wait()
            part[e, c, own] = (part[e, c, own].astype(F32) + recv_a[e, c].astype(F32)).astype(BF)
            state[c]["b"] = post(part.at[e, c, own], recv_b.at[e, c], beside)
        return run

    def total(e, c):
        state[c]["b"].wait()
        return part[e, c, own].astype(F32) + recv_b[e, c].astype(F32)

    def give(buf, c):
        return post(buf.at[c, own], buf.at[c, own], sibling)

    def keys_stage():
        for c in range(NC - 1, -1, -1):
            rows = slice(c * CR, c * CR + CR)
            xv = x[c].reshape(CR, 640).astype(F32)
            n = (xv * inv_rms(xv) * vec(g_in)).astype(BF)
            normed[rows] = n
            raw = nn(n, wk[...])
            k_raw[rows] = raw
            k[rows] = turn(raw * inv_rms(raw) * vec(g_k), cos_t[rows], sin_t[rows]).astype(BF)
            v[rows] = nn(n, wv[...]).astype(BF)

    def attention_stage(c):
        rows = slice(c * CR, c * CR + CR)
        raw = nn(normed[rows], wq[...])
        q_raw[rows] = raw
        q_low = turn(raw * inv_rms(raw) * vec(g_q), cos_t[rows], sin_t[rows]).astype(BF)
        q[rows] = q_low
        first, size = key_range(c)
        keys = slice(first, first + size)
        scores = nt(q_low, k[keys]) * 0.0625
        gap = c * CR - first + lax.broadcasted_iota(jnp.int32, (CR, size), 0) - lax.broadcasted_iota(jnp.int32, (CR, size), 1)
        seg_rows = jnp.broadcast_to(segs[:, rows], (128, CR)).T[:, :1]
        allowed = (gap >= 0) & (gap < WINDOW) & (seg_rows == segs[:, keys])
        masked = jnp.where(allowed, scores, NEG_LARGE)
        e = jnp.where(allowed, jnp.exp(masked - jnp.max(masked, axis=-1, keepdims=True)), 0.0)
        p = e / jnp.sum(e, axis=-1, keepdims=True)
        prob[c, :, 0:size] = p
        h = nn(p.astype(BF), v[keys]).astype(BF)
        heads[rows] = h
        part[0, c] = nn(h, wo[...]).astype(BF).reshape(2, OW, 640)
        share(0, c)

    def mid_stage(c):
        a = total(0, c)
        attn_own[c] = a
        mid = x[c, own].astype(F32) + a * inv_rms(a) * vec(g_ao)
        mid_own[c] = mid
        ffn_g[c, own] = (mid * inv_rms(mid) * vec(g_fi)).astype(BF)
        state[c]["g"] = give(ffn_g, c)

    def up_stage(c):
        state[c]["g"].wait()
        f = ffn_g[c].reshape(CR, 640)
        gate = nn(f, wg[...])
        up = nn(f, wu[...])
        th = jnp.tanh(C0 * (gate + C1 * gate * gate * gate))
        half = 0.5 * (1.0 + th)
        act = gate * half
        slope = half + 0.5 * gate * (1.0 - th * th) * (C0 * (1.0 + 3.0 * C1 * gate * gate))
        act_a[c] = up * slope
        act_b[c] = act
        h = (act * up).astype(BF)
        hid[c] = h
        part[1, c] = nn(h, wd[...]).astype(BF).reshape(2, OW, 640)
        share(1, c)

    def out_stage(c):
        s = total(1, c)
        r = inv_rms(s)
        ct = cot[c, own].astype(F32)
        dffn_g[c, own] = rms_back(s, r, ct * vec(g_fo)).astype(BF)
        state[c]["g"] = give(dffn_g, c)
        output[c, own] = (mid_own[c] + s * r * vec(g_fo)).astype(BF)
        state[c]["o"] = give(output, c)
        gains[2:3, :] = gains[2:3, :] + jnp.sum(ct * s * r, axis=0, keepdims=True)

    def down_stage(c):
        state[c]["g"].wait()
        d = dffn_g[c].reshape(CR, 640)
        dh = nt(d, wd[...])
        dg = (dh * act_a[c]).astype(BF)
        du = (dh * act_b[c]).astype(BF)
        dgate[c] = dg
        dup[c] = du
        part[2, c] = (nt(dg, wg[...]) + nt(du, wu[...])).astype(BF).reshape(2, OW, 640)
        share(2, c)

    def attn_stage(c):
        d = total(2, c)
        mid, a = mid_own[c], attn_own[c]
        r = inv_rms(mid)
        gains[1:2, :] = gains[1:2, :] + jnp.sum(d * mid * r, axis=0, keepdims=True)
        dmid = cot[c, own].astype(F32) + rms_back(mid, r, d * vec(g_fi))
        mid_own[c] = dmid
        r = inv_rms(a)
        gains[0:1, :] = gains[0:1, :] + jnp.sum(dmid * a * r, axis=0, keepdims=True)
        dattn[c, own] = rms_back(a, r, dmid * vec(g_ao)).astype(BF)
        state[c]["g"] = give(dattn, c)

    def back_stage(i):
        state[i]["g"].wait()
        rows = slice(i * CR, i * CR + CR)
        start, size = key_range(i)
        dh = nt(dattn[i].reshape(CR, 640), wo[...]).astype(BF)
        p = prob[i, :, 0:size]
        dp = nt(dh, v[start:start + size])
        ds = (p * (dp - jnp.sum(p * dp, axis=-1, keepdims=True))).astype(BF)
        dq = nn(ds, k[start:start + size]) * 0.0625
        dk_add = tn(ds, q[rows]) * 0.0625
        dv_add = tn(p.astype(BF), dh)
        fresh = size if i == NC - 1 else (CR if i == NC - 2 else 0)
        if fresh:
            dk[start:start + fresh] = dk_add[:fresh]
            dv[start:start + fresh] = dv_add[:fresh]
        if fresh < size:
            dk[start + fresh:start + size] = dk[start + fresh:start + size] + dk_add[fresh:]
            dv[start + fresh:start + size] = dv[start + fresh:start + size] + dv_add[fresh:]
        cosine, sine = cos_t[rows], sin_t[rows]
        raws = []
        for d, raw, g, at in ((dq, q_raw[rows], g_q, 0), (dk[rows], k_raw[rows], g_k, 256)):
            du = turn_back(d, cosine, sine)
            r = inv_rms(raw)
            gains[4:5, at:at + 256] = gains[4:5, at:at + 256] + jnp.sum(du * raw * r, axis=0, keepdims=True)
            raws.append(rms_back(raw, r, du * vec(g)).astype(BF))
        raws.append(dv[rows].astype(BF))
        for j in range(3):
            dqkv[rows, 256 * j:256 * j + 256] = raws[j]
        if i == 0:
            weights_out()
            weights_in()
        term = nt(raws[0], wq[...]) + nt(raws[1], wk[...]) + nt(raws[2], wv[...])
        part[3, i] = term.astype(BF).reshape(2, OW, 640)
        share(3, i)

    def in_stage(i):
        d = total(3, i)
        xv = x[i, own].astype(F32)
        r = inv_rms(xv)
        gains[3:4, :] = gains[3:4, :] + jnp.sum(d * xv * r, axis=0, keepdims=True)
        in_grad[i, own] = (mid_own[i] + rms_back(xv, r, d * vec(g_in))).astype(BF)
        state[i]["g"] = give(in_grad, i)

    def weights_down():
        g = tn(hid[...].reshape(1024, 512), dffn_g[...].reshape(1024, 640)).astype(BF)
        for s in range(8):
            for p in range(4):
                a_buf[p, s, 160:224] = g[64 * s:64 * s + 64, 128 * p:128 * p + 128]
            for p in range(4):
                a_buf[p, s, 224:240] = g[128 * p + 16 * s:128 * p + 16 * s + 16, 512:640]

    def weights_ffn(source, at):
        g = tn(ffn_g[...].reshape(1024, 640), source[...].reshape(1024, 512)).astype(BF)
        for s in range(8):
            for p in range(4):
                a_buf[p, s, at:at + 80] = g[80 * s:80 * s + 80, 128 * p:128 * p + 128]

    def weights_out():
        g = tn(heads[...], dattn[...].reshape(1024, 640)).astype(BF)
        for c in range(8):
            rows = slice(32 * c, 32 * c + 32)
            b0[c, 80:112] = g[rows, 0:128]
            b1[c, 80:112] = g[rows, 128:256]
            b1[c, 112:144] = g[rows, 256:384]
            b2[c, 80:112] = g[rows, 384:512]
            b3[c, 80:112] = g[rows, 512:640]

    def weights_in():
        g = tn(normed[...], dqkv[...]).astype(BF)
        for c in range(8):
            rows = slice(80 * c, 80 * c + 80)
            for j in range(4):
                kv[j, c] = g[rows, 256 + 128 * j:384 + 128 * j]
            b0[c, 0:80] = g[rows, 0:128]
            b1[c, 0:80] = g[rows, 128:256]
        extra["kv"] = send(kv.at[pl.ds((1 - core) * 2, 2)], kv_recv, k_ss.at[0], k_rs.at[0], sibling)
        second.start()

    def begin_third():
        extra["kv"].wait()
        for i, b in ((0, b2), (1, b3)):
            for c in range(8):
                b[c, 0:80] = (kv[core * 2 + i, c].astype(F32) + kv_recv[i, c].astype(F32)).astype(BF)
        third.start()

    extra = {}
    first = Reduction((0, 1, 2, 3), [a_buf.at[p] for p in range(4)], [a_recv.at[p] for p in range(4)],
                      [a_out.at[p] for p in range(4)], a_ss, a_rs, links, bits, across)
    second = Reduction((0, 1), [b0, b1], [r0, r1], [o0, o1], b_ss, b_rs, links, bits, across)
    third = Reduction((3, 0), [b2, b3], [r2, r3], [o2, o3], c_ss, c_rs, links, bits, across, (beside, corner))
    jobs = {
        "down": weights_down, "gate": lambda: weights_ffn(dgate, 0), "up": lambda: weights_ffn(dup, 80),
        "first": first.start, "third": begin_third, "1": first.advance, "2": second.advance, "3": third.advance,
    }
    gains[...] = jnp.zeros_like(gains)
    keys_stage()
    stages = [
        attention_stage, exchange(0), mid_stage, up_stage, exchange(1), out_stage, down_stage, exchange(2), attn_stage,
        back_stage, exchange(3), in_stage,
    ]
    for tick in range(len(stages) + NC - 1):
        for p in range(NC):
            s = tick - p
            if 0 <= s < len(stages):
                stages[s](NC - 1 - p)
                for job in AFTER.get((s, p), ()):
                    jobs[job]()
    gains[0:4, :] = gains[0:4, :] * 0.5
    order = [(sibling,), (beside, across, corner), (links[0],), (links[1],), (links[2],), (links[3],)]
    slot, sent = 0, False
    for i in range(10):
        if i < len(order):
            gc = []
            for device in order[i]:
                gc.append(send(gains, g_recv.at[slot], g_ss.at[slot], g_rs.at[slot], device))
                slot += 1
        third.advance()
        if third.at == 8 and not sent:
            sent = True
            for j, o in ((0, o2), (1, o3)):
                for c in range(8):
                    kv_out[core * 2 + j, c] = o[c, 0:80]
            kc = send(kv_out.at[pl.ds(core * 2, 2)], kv_out.at[pl.ds(core * 2, 2)], k_ss.at[1], k_rs.at[1], sibling)
        second.advance()
        first.advance()
        if i < len(order):
            for c in gc:
                c.wait()
            if i == 1:
                gains[...] = (gains[...] + g_recv[slot - 2]) + (g_recv[slot - 3] + g_recv[slot - 1])
            else:
                gains[...] = gains[...] + g_recv[slot - 1]
    kc.wait()
    for c in range(NC):
        state[c]["o"].wait()
        state[c]["g"].wait()


AFTER = {
    (6, 3): ("down", "gate", "up", "first"),
    (7, 3): ("1",),
    (10, 1): ("1",),
    (8, 3): ("1",),
    (10, 2): ("1",),
    (9, 3): ("third", "1", "2"),
    (11, 2): ("2", "3"),
    (10, 3): ("1",),
    (11, 3): ("2", "3", "1"),
}


def unpack_kernel(a, b0, b1, b2, b3, kv, gains, query, key, value, out, gate, up, down, g0, g1, g2, g3, g4, g5):
    for c in range(8):
        for p in range(4):
            cols = slice(128 * p, 128 * p + 128)
            gate[80 * c:80 * c + 80, cols] = a[p, c, 0:80].astype(F32)
            up[80 * c:80 * c + 80, cols] = a[p, c, 80:160].astype(F32)
            down[64 * c:64 * c + 64, cols] = a[p, c, 160:224].astype(F32)
            down[128 * p + 16 * c:128 * p + 16 * c + 16, 512:640] = a[p, c, 224:240].astype(F32)
        for p, b in ((0, b0), (1, b1)):
            query[80 * c:80 * c + 80, 128 * p:128 * p + 128] = b[c, 0:80].astype(F32)
        for p, b, at in ((0, b0, 80), (1, b1, 80), (2, b1, 112), (3, b2, 80), (4, b3, 80)):
            out[32 * c:32 * c + 32, 128 * p:128 * p + 128] = b[c, at:at + 32].astype(F32)
        for j in range(2):
            key[80 * c:80 * c + 80, 128 * j:128 * j + 128] = kv[j, c].astype(F32)
            value[80 * c:80 * c + 80, 128 * j:128 * j + 128] = kv[2 + j, c].astype(F32)
    for i, g in ((3, g0), (0, g1), (1, g2), (2, g3)):
        g[...] = gains[i, :]
    g4[...] = gains[4, 0:256]
    g5[...] = gains[4, 256:512]


def layer(*operands):
    sds = jax.ShapeDtypeStruct
    dma = pltpu.SemaphoreType.DMA
    v = pltpu.VMEM
    blocks = (NC, 2, OW, 640)
    half = (NC, OW, 640)
    count = NC * 12
    stacks = pl.pallas_call(
        layer_kernel,
        out_shape=(sds(blocks, BF), sds(blocks, BF), sds((4, 8, 240, 128), BF), sds((8, 112, 128), BF), sds((8, 144, 128), BF),
                   sds((8, 112, 128), BF), sds((8, 112, 128), BF), sds((4, 8, 80, 128), BF), sds((8, 640), F32)),
        in_specs=[VMEM] * len(operands),
        out_specs=[VMEM] * 9,
        scratch_shapes=[
            v((1024, 640), BF), v((1024, 256), F32), v((1024, 256), F32), v((1024, 256), BF), v((1024, 256), BF),
            v((1024, 256), BF), v((NC, CR, 768), F32), v((1024, 256), BF), v((4, *blocks), BF), v(blocks, BF), v(blocks, BF),
            v(blocks, BF), v((NC, CR, 512), BF), v((NC, CR, 512), F32), v((NC, CR, 512), F32), v((NC, CR, 512), BF),
            v((NC, CR, 512), BF), v(half, F32), v(half, F32), v((4, *half), BF), v((4, *half), BF),
            v((1024, 256), F32), v((1024, 256), F32), v((1024, 768), BF),
            v((4, 8, 240, 128), BF),
            v((8, 112, 128), BF), v((8, 144, 128), BF), v((8, 112, 128), BF), v((8, 112, 128), BF),
            v((4, 9, 240, 128), BF),
            v((9, 112, 128), BF), v((9, 144, 128), BF), v((11, 112, 128), BF), v((11, 112, 128), BF),
            v((4, 8, 80, 128), BF), v((2, 8, 80, 128), BF),
            v((8, 8, 640), F32),
            dma((count + 16,)), dma((count + 16,)),
            dma((4, 8)), dma((4, 8)), dma((2, 8)), dma((2, 8)), dma((2, 10)), dma((2, 10)), dma((2,)), dma((2,)),
            dma((8,)), dma((8,)),
        ],
        compiler_params=pltpu.CompilerParams(collective_id=7, has_side_effects=True, vmem_limit_bytes=VMEM_LIMIT),
        name="layer",
    )(*operands)
    outs = pl.pallas_call(
        unpack_kernel,
        out_shape=(sds((640, 256), F32), sds((640, 256), F32), sds((640, 256), F32), sds((256, 640), F32),
                   sds((640, 512), F32), sds((640, 512), F32), sds((512, 640), F32),
                   sds((640,), F32), sds((640,), F32), sds((640,), F32), sds((640,), F32),
                   sds((256,), F32), sds((256,), F32)),
        in_specs=[VMEM] * 7,
        out_specs=[VMEM] * 13,
        compiler_params=pltpu.CompilerParams(vmem_limit_bytes=VMEM_LIMIT),
        name="unpack_grads",
    )(*stacks[2:])
    return stacks[0], stacks[1], outs


def rope_tables(positions, head_size):
    half_size = head_size // 2
    inv_freq = ROPE_BASE ** (-2.0 * jnp.arange(half_size, dtype=jnp.float32) / head_size)
    angles = positions.astype(jnp.float32)[:, None] * inv_freq[None, :]
    return (jnp.cos(angles), jnp.sin(angles))


def local(
    inputs,
    segments,
    positions,
    cotangent,
    w_query,
    w_key,
    w_value,
    w_out,
    w_gate,
    w_up,
    w_down,
    g_attn_in,
    g_attn_out,
    g_ffn_in,
    g_ffn_out,
    g_query,
    g_key,
):
    blocks = (NC, 2, OW, 640)
    cos_t, sin_t = rope_tables(positions, 256)
    output, input_grad, summed = layer(
        inputs.reshape(blocks), cotangent.reshape(blocks), segments.reshape(1, 1024), cos_t, sin_t,
        w_query, w_key, w_value, w_out, w_gate, w_up, w_down,
        g_attn_in, g_attn_out, g_ffn_in, g_ffn_out, g_query, g_key,
    )
    return (output.reshape(1024, 640), input_grad.reshape(1024, 640), *summed)


def solution(mesh):
    placed = (
        P("dp", None),
        P("dp"),
        P("dp"),
        P("dp", None),
        P(None, "tensor"),
        P(),
        P(),
        P("tensor", None),
        P(None, "tensor"),
        P(None, "tensor"),
        P("tensor", None),
        P(),
        P(),
        P(),
        P(),
        P(),
        P(),
    )
    return jax.shard_map(
        local,
        mesh=mesh,
        in_specs=placed,
        out_specs=(
            P("dp", None),
            P("dp", None),
            P(None, "tensor"),
            P(),
            P(),
            P("tensor", None),
            P(None, "tensor"),
            P(None, "tensor"),
            P("tensor", None),
            P(),
            P(),
            P(),
            P(),
            P(),
            P(),
        ),
        check_vma=False,
    )
```

```python
import jax, jax.numpy as jnp
from jax import lax
from jax.experimental import pallas as pl
from jax.experimental.pallas import tpu as pltpu
from jax.sharding import PartitionSpec as P

WINDOW = 512
EPSILON = 1e-06
ROPE_BASE = 10000.0
NEG_LARGE = -1e30

MESH = pl.DeviceIdType.MESH
BF = jnp.bfloat16
F32 = jnp.float32
VMEM = pl.BlockSpec(memory_space=pltpu.VMEM)
VMEM_LIMIT = 60 * 1024 * 1024


def neighbours():
    dp = lax.axis_index("dp")
    t = lax.axis_index("tensor")
    z = lax.rem(dp, 4)
    y = lax.rem(dp // 4, 4)
    xh = dp // 16
    xl = t // 2
    core = lax.rem(t, 2)
    ya = y + 1 - 2 * lax.rem(y, 2)
    za = z + 1 - 2 * lax.rem(z, 2)
    links = [
        (dp + (ya - y) * 4, t),
        (dp + (za - z), t),
        (dp + (3 - 2 * y) * 4, t),
        (dp + (3 - 2 * z), t),
    ]
    bits = [lax.rem((y + 1) // 2, 2), lax.rem((z + 1) // 2, 2), y // 2, z // 2]
    across = (dp + 16 - 32 * xh, t)
    sibling = (dp, t + 1 - 2 * core)
    beside = (dp, t + 2 - 4 * xl)
    corner = (dp + 16 - 32 * xh, t + 2 - 4 * xl)
    return links, bits, across, sibling, beside, corner, xl, core


def greet(devices):
    barrier = pltpu.get_barrier_semaphore()
    for d in devices:
        pl.semaphore_signal(barrier, inc=1, device_id=d, device_id_type=MESH)
    pl.semaphore_wait(barrier, len(devices))


def send(src, dst, ssem, rsem, device):
    copy = pltpu.make_async_remote_copy(
        src_ref=src, dst_ref=dst, send_sem=ssem, recv_sem=rsem, device_id=device, device_id_type=MESH
    )
    copy.start()
    return copy


class Reduction:
    def __init__(self, ids, bufs, recvs, outs, ssem, rsem, links, bits, across, more=()):
        self.ids, self.bufs, self.recvs, self.outs, self.ssem, self.rsem = ids, bufs, recvs, outs, ssem, rsem
        self.links, self.bits, self.across, self.more = links, bits, across, more
        self.base = [jnp.int32(0)] * len(ids)
        self.at = 0

    def start(self):
        step = self.at
        self.copies = []
        for i, p in enumerate(self.ids):
            buf, recv = self.bufs[i], self.recvs[i]
            ss, rs = self.ssem.at[i, step], self.rsem.at[i, step]
            if step < 3:
                n = 4 >> step
                bit = self.bits[(p + step) % 4]
                there = self.base[i] + (1 - bit) * n
                self.base[i] = self.base[i] + bit * n
                at = (0, 4, 6)[step]
                src, dst, dev = buf.at[pl.ds(there, n)], recv.at[pl.ds(at, n)], self.links[(p + step) % 4]
            elif step < 5:
                dev = self.links[(p + 3) % 4] if step == 3 else self.across
                src, dst = buf.at[self.base[i]], recv.at[4 + step]
            else:
                s = 7 - step
                n = 4 >> s
                bit = self.bits[(p + s) % 4]
                src = dst = self.outs[i].at[pl.ds(self.base[i], n)]
                self.base[i] = self.base[i] - bit * n
                dev = self.links[(p + s) % 4]
            self.copies.append(send(src, dst, ss, rs, dev))
            if step == 4:
                for j, dev in enumerate(self.more):
                    self.copies.append(send(buf.at[self.base[i], pl.ds(0, 80)], recv.at[9 + j, pl.ds(0, 80)],
                                            self.ssem.at[i, 8 + j], self.rsem.at[i, 8 + j], dev))

    def advance(self):
        step = self.at
        if step == 8:
            return
        for copy in self.copies:
            copy.wait()
        if step < 5:
            n = (4, 2, 1, 1, 1)[step]
            at = (0, 4, 6, 7, 8)[step]
            for i in range(len(self.ids)):
                buf, recv, base = self.bufs[i], self.recvs[i], self.base[i]
                into = self.outs[i] if step == 4 else buf

                def add(j, carry):
                    into[base + j] = (buf[base + j].astype(F32) + recv[at + j].astype(F32)).astype(BF)
                    return carry

                lax.fori_loop(0, n, add, 0)
                if step == 4 and self.more:
                    pair = recv[9, 0:80].astype(F32) + recv[10, 0:80].astype(F32)
                    into[base, 0:80] = (buf[base, 0:80].astype(F32) + recv[8, 0:80].astype(F32) + pair).astype(BF)
        self.at = step + 1
        if self.at < 8:
            self.start()


NC = 4
CR = 1024 // NC
OW = CR // 2
C0 = 0.7978845608028654
C1 = 0.044715


def nt(a, b):
    return lax.dot_general(a, b, (((1,), (1,)), ((), ())), preferred_element_type=F32)


def tn(a, b):
    return lax.dot_general(a, b, (((0,), (0,)), ((), ())), preferred_element_type=F32)


def nn(a, b):
    return jnp.dot(a, b, preferred_element_type=F32)


def inv_rms(v):
    return lax.rsqrt(jnp.mean(v * v, axis=-1, keepdims=True) + EPSILON)


def rms_back(v, r, du):
    return r * du - v * (r * r * r * jnp.mean(du * v, axis=-1, keepdims=True))


def turn(v, cosine, sine):
    a, b = v[:, :128], v[:, 128:]
    return jnp.concatenate([a * cosine - b * sine, b * cosine + a * sine], axis=-1)


def turn_back(v, cosine, sine):
    a, b = v[:, :128], v[:, 128:]
    return jnp.concatenate([a * cosine + b * sine, b * cosine - a * sine], axis=-1)


def key_range(i):
    first = max(0, (i - 2) * CR)
    return first, (i + 1) * CR - first


def vec(g):
    return g[...]


def layer_kernel(x, cot, segs, cos_t, sin_t, wq, wk, wv, wo, wg, wu, wd, g_in, g_ao, g_fi, g_fo, g_q, g_k,
                 output, in_grad, a_out, o0, o1, o2, o3, kv_out, gains,
                 normed, q_raw, k_raw, q, k, v, prob, heads, part, ffn_g, dffn_g, dattn, hid, act_a, act_b, dgate, dup,
                 attn_own, mid_own, recv_a, recv_b, dk, dv, dqkv,
                 a_buf, b0, b1, b2, b3, a_recv, r0, r1, r2, r3, kv, kv_recv, g_recv, in_acc, out_acc, down_acc, up_acc,
                 ssem, rsem, a_ss, a_rs, b_ss, b_rs, c_ss, c_rs, k_ss, k_rs, g_ss, g_rs):
    links, bits, across, sibling, beside, corner, xl, core = neighbours()
    greet(links + [across, sibling, beside, corner])
    own = core
    state = [dict() for _ in range(NC)]
    used = [0]

    def post(src, dst, device):
        i = used[0]
        used[0] += 1
        return send(src, dst, ssem.at[i], rsem.at[i], device)

    def share(e, c):
        state[c]["a"] = post(part.at[e, c, 1 - own], recv_a.at[e, c], sibling)

    def exchange(e):
        def run(c):
            state[c]["a"].wait()
            part[e, c, own] = (part[e, c, own].astype(F32) + recv_a[e, c].astype(F32)).astype(BF)
            state[c]["b"] = post(part.at[e, c, own], recv_b.at[e, c], beside)
        return run

    def total(e, c):
        state[c]["b"].wait()
        return part[e, c, own].astype(F32) + recv_b[e, c].astype(F32)

    def give(buf, c):
        return post(buf.at[c, own], buf.at[c, own], sibling)

    def keys_stage():
        for c in range(NC - 1, -1, -1):
            rows = slice(c * CR, c * CR + CR)
            xv = x[c].reshape(CR, 640).astype(F32)
            n = (xv * inv_rms(xv) * vec(g_in)).astype(BF)
            normed[rows] = n
            raw = nn(n, wk[...])
            k_raw[rows] = raw
            k[rows] = turn(raw * inv_rms(raw) * vec(g_k), cos_t[rows], sin_t[rows]).astype(BF)
            v[rows] = nn(n, wv[...]).astype(BF)

    def attention_stage(c):
        rows = slice(c * CR, c * CR + CR)
        raw = nn(normed[rows], wq[...])
        q_raw[rows] = raw
        q_low = turn(raw * inv_rms(raw) * vec(g_q), cos_t[rows], sin_t[rows]).astype(BF)
        q[rows] = q_low
        first, size = key_range(c)
        keys = slice(first, first + size)
        scores = nt(q_low, k[keys]) * 0.0625
        gap = c * CR - first + lax.broadcasted_iota(jnp.int32, (CR, size), 0) - lax.broadcasted_iota(jnp.int32, (CR, size), 1)
        seg_rows = jnp.broadcast_to(segs[:, rows], (128, CR)).T[:, :1]
        allowed = (gap >= 0) & (gap < WINDOW) & (seg_rows == segs[:, keys])
        masked = jnp.where(allowed, scores, NEG_LARGE)
        e = jnp.where(allowed, jnp.exp(masked - jnp.max(masked, axis=-1, keepdims=True)), 0.0)
        p = e / jnp.sum(e, axis=-1, keepdims=True)
        prob[c, :, 0:size] = p
        h = nn(p.astype(BF), v[keys]).astype(BF)
        heads[rows] = h
        part[0, c] = nn(h, wo[...]).astype(BF).reshape(2, OW, 640)
        share(0, c)

    def mid_stage(c):
        a = total(0, c)
        attn_own[c] = a
        mid = x[c, own].astype(F32) + a * inv_rms(a) * vec(g_ao)
        mid_own[c] = mid
        ffn_g[c, own] = (mid * inv_rms(mid) * vec(g_fi)).astype(BF)
        state[c]["g"] = give(ffn_g, c)

    def up_stage(c):
        state[c]["g"].wait()
        f = ffn_g[c].reshape(CR, 640)
        gate = nn(f, wg[...])
        up = nn(f, wu[...])
        th = jnp.tanh(C0 * (gate + C1 * gate * gate * gate))
        half = 0.5 * (1.0 + th)
        act = gate * half
        slope = half + 0.5 * gate * (1.0 - th * th) * (C0 * (1.0 + 3.0 * C1 * gate * gate))
        act_a[c] = up * slope
        act_b[c] = act
        h = (act * up).astype(BF)
        hid[c] = h
        part[1, c] = nn(h, wd[...]).astype(BF).reshape(2, OW, 640)
        share(1, c)

    def out_stage(c):
        s = total(1, c)
        r = inv_rms(s)
        ct = cot[c, own].astype(F32)
        dffn_g[c, own] = rms_back(s, r, ct * vec(g_fo)).astype(BF)
        state[c]["g"] = give(dffn_g, c)
        output[c, own] = (mid_own[c] + s * r * vec(g_fo)).astype(BF)
        state[c]["o"] = give(output, c)
        gains[2:3, :] = gains[2:3, :] + jnp.sum(ct * s * r, axis=0, keepdims=True)

    def down_stage(c):
        state[c]["g"].wait()
        d = dffn_g[c].reshape(CR, 640)
        dh = nt(d, wd[...])
        dg = (dh * act_a[c]).astype(BF)
        du = (dh * act_b[c]).astype(BF)
        dgate[c] = dg
        dup[c] = du
        part[2, c] = (nt(dg, wg[...]) + nt(du, wu[...])).astype(BF).reshape(2, OW, 640)
        share(2, c)

    def attn_stage(c):
        d = total(2, c)
        mid, a = mid_own[c], attn_own[c]
        r = inv_rms(mid)
        gains[1:2, :] = gains[1:2, :] + jnp.sum(d * mid * r, axis=0, keepdims=True)
        dmid = cot[c, own].astype(F32) + rms_back(mid, r, d * vec(g_fi))
        mid_own[c] = dmid
        r = inv_rms(a)
        gains[0:1, :] = gains[0:1, :] + jnp.sum(dmid * a * r, axis=0, keepdims=True)
        dattn[c, own] = rms_back(a, r, dmid * vec(g_ao)).astype(BF)
        state[c]["g"] = give(dattn, c)

    def back_stage(i):
        state[i]["g"].wait()
        rows = slice(i * CR, i * CR + CR)
        start, size = key_range(i)
        dh = nt(dattn[i].reshape(CR, 640), wo[...]).astype(BF)
        p = prob[i, :, 0:size]
        dp = nt(dh, v[start:start + size])
        ds = (p * (dp - jnp.sum(p * dp, axis=-1, keepdims=True))).astype(BF)
        dq = nn(ds, k[start:start + size]) * 0.0625
        dk_add = tn(ds, q[rows]) * 0.0625
        dv_add = tn(p.astype(BF), dh)
        fresh = size if i == NC - 1 else (CR if i == NC - 2 else 0)
        if fresh:
            dk[start:start + fresh] = dk_add[:fresh]
            dv[start:start + fresh] = dv_add[:fresh]
        if fresh < size:
            dk[start + fresh:start + size] = dk[start + fresh:start + size] + dk_add[fresh:]
            dv[start + fresh:start + size] = dv[start + fresh:start + size] + dv_add[fresh:]
        cosine, sine = cos_t[rows], sin_t[rows]
        raws = []
        for d, raw, g, at in ((dq, q_raw[rows], g_q, 0), (dk[rows], k_raw[rows], g_k, 256)):
            du = turn_back(d, cosine, sine)
            r = inv_rms(raw)
            gains[4:5, at:at + 256] = gains[4:5, at:at + 256] + jnp.sum(du * raw * r, axis=0, keepdims=True)
            raws.append(rms_back(raw, r, du * vec(g)).astype(BF))
        raws.append(dv[rows].astype(BF))
        for j in range(3):
            dqkv[rows, 256 * j:256 * j + 256] = raws[j]
        if i == 0:
            weights_out()
            weights_in()
        term = nt(raws[0], wq[...]) + nt(raws[1], wk[...]) + nt(raws[2], wv[...])
        xv = x[i].reshape(CR, 640).astype(F32)
        gains[3:4, :] = gains[3:4, :] + jnp.sum(term * (xv * inv_rms(xv)), axis=0, keepdims=True)
        part[3, i] = term.astype(BF).reshape(2, OW, 640)
        share(3, i)

    def in_stage(i):
        d = total(3, i)
        xv = x[i, own].astype(F32)
        r = inv_rms(xv)
        in_grad[i, own] = (mid_own[i] + rms_back(xv, r, d * vec(g_in))).astype(BF)
        state[i]["g"] = give(in_grad, i)

    def ffn_early():
        n = 1024 - CR
        f = ffn_g[1:].reshape(n, 640)
        down_acc[...] = tn(hid[1:].reshape(n, 512), dffn_g[1:].reshape(n, 640))
        up_acc[0] = tn(f, dgate[1:].reshape(n, 512))
        up_acc[1] = tn(f, dup[1:].reshape(n, 512))

    def weights_down():
        g = (down_acc[...] + tn(hid[0], dffn_g[0].reshape(CR, 640))).astype(BF)
        for s in range(8):
            for p in range(4):
                a_buf[p, s, 160:224] = g[64 * s:64 * s + 64, 128 * p:128 * p + 128]
            for p in range(4):
                a_buf[p, s, 224:240] = g[128 * p + 16 * s:128 * p + 16 * s + 16, 512:640]

    def weights_ffn(source, at):
        g = (up_acc[at // 80] + tn(ffn_g[0].reshape(CR, 640), source[0])).astype(BF)
        for s in range(8):
            for p in range(4):
                a_buf[p, s, at:at + 80] = g[80 * s:80 * s + 80, 128 * p:128 * p + 128]

    def weights_early():
        out_acc[...] = tn(heads[CR:], dattn[1:].reshape(1024 - CR, 640))
        in_acc[...] = tn(normed[CR:], dqkv[CR:])

    def weights_out():
        g = (out_acc[...] + tn(heads[0:CR], dattn[0].reshape(CR, 640))).astype(BF)
        for c in range(8):
            rows = slice(32 * c, 32 * c + 32)
            b0[c, 80:112] = g[rows, 0:128]
            b1[c, 80:112] = g[rows, 128:256]
            b1[c, 112:144] = g[rows, 256:384]
            b2[c, 80:112] = g[rows, 384:512]
            b3[c, 80:112] = g[rows, 512:640]

    def weights_in():
        g = (in_acc[...] + tn(normed[0:CR], dqkv[0:CR])).astype(BF)
        for c in range(8):
            rows = slice(80 * c, 80 * c + 80)
            for j in range(4):
                kv[j, c] = g[rows, 256 + 128 * j:384 + 128 * j]
            b0[c, 0:80] = g[rows, 0:128]
            b1[c, 0:80] = g[rows, 128:256]
        extra["kv"] = send(kv.at[pl.ds((1 - core) * 2, 2)], kv_recv, k_ss.at[0], k_rs.at[0], sibling)
        second.start()

    def begin_third():
        extra["kv"].wait()
        for i, b in ((0, b2), (1, b3)):
            for c in range(8):
                b[c, 0:80] = (kv[core * 2 + i, c].astype(F32) + kv_recv[i, c].astype(F32)).astype(BF)
        third.start()

    extra = {"gain": 0}
    order = [(sibling,), (beside, across, corner), (links[0],), (links[1],), (links[2],), (links[3],)]

    def send_gains():
        i = extra["gain"]
        if i < 6:
            at = (0, 1, 4, 5, 6, 7)[i]
            extra["copies"] = [send(gains, g_recv.at[at + j], g_ss.at[at + j], g_rs.at[at + j], d) for j, d in enumerate(order[i])]

    def begin_gains():
        gains[0:3, :] = gains[0:3, :] * 0.5
        send_gains()

    def swap_gains():
        i = extra["gain"]
        if i == 6:
            return
        for copy in extra["copies"]:
            copy.wait()
        if i == 1:
            gains[...] = (gains[...] + g_recv[2]) + (g_recv[1] + g_recv[3])
        else:
            gains[...] = gains[...] + g_recv[(0, 1, 4, 5, 6, 7)[i]]
        extra["gain"] = i + 1
        send_gains()

    first = Reduction((0, 1, 2, 3), [a_buf.at[p] for p in range(4)], [a_recv.at[p] for p in range(4)],
                      [a_out.at[p] for p in range(4)], a_ss, a_rs, links, bits, across)
    second = Reduction((0, 1), [b0, b1], [r0, r1], [o0, o1], b_ss, b_rs, links, bits, across)
    third = Reduction((3, 0), [b2, b3], [r2, r3], [o2, o3], c_ss, c_rs, links, bits, across, (beside, corner))
    jobs = {
        "down": weights_down, "gate": lambda: weights_ffn(dgate, 0), "up": lambda: weights_ffn(dup, 80),
        "first": first.start, "third": begin_third, "1": first.advance, "2": second.advance, "3": third.advance,
        "gains": begin_gains, "g": swap_gains, "acc": weights_early, "ffn": ffn_early,
    }
    gains[...] = jnp.zeros_like(gains)
    keys_stage()
    stages = [
        attention_stage, exchange(0), mid_stage, up_stage, exchange(1), out_stage, down_stage, exchange(2), attn_stage,
        back_stage, exchange(3), in_stage,
    ]
    for tick in range(len(stages) + NC - 1):
        for p in range(NC):
            s = tick - p
            if 0 <= s < len(stages):
                stages[s](NC - 1 - p)
                for job in AFTER.get((s, p), ()):
                    jobs[job]()
    sent = False
    for i in range(9):
        third.advance()
        if third.at == 8 and not sent:
            sent = True
            for j, o in ((0, o2), (1, o3)):
                for c in range(8):
                    kv_out[core * 2 + j, c] = o[c, 0:80]
            kc = send(kv_out.at[pl.ds(core * 2, 2)], kv_out.at[pl.ds(core * 2, 2)], k_ss.at[1], k_rs.at[1], sibling)
        second.advance()
        swap_gains()
        if i in LATE:
            first.advance()
    kc.wait()
    for c in range(NC):
        state[c]["o"].wait()
        state[c]["g"].wait()


AFTER = {
    (6, 2): ("ffn",),
    (6, 3): ("down", "gate", "up", "first"),
    (8, 2): ("1",),
    (10, 1): ("1",),
    (9, 2): ("acc",),
    (8, 3): ("1",),
    (9, 3): ("gains", "third", "1", "2"),
    (11, 2): ("2", "3", "g"),
    (10, 3): ("1",),
    (11, 3): ("2", "3", "g"),
}
LATE = (0, 2, 5)


def unpack_kernel(a, b0, b1, b2, b3, kv, gains, y, dx, query_o, key_o, value_o, out_o, gate_o, up_o, down_o, y_o, dx_o,
                  g0, g1, g2, g3, g4, g5, query, key, value, out, gate, up, down, sems):
    copies = []

    def leave(src, dst):
        copy = pltpu.make_async_copy(src, dst, sems.at[len(copies)])
        copy.start()
        copies.append(copy)

    leave(y, y_o)
    leave(dx, dx_o)
    for c in range(8):
        for p in range(4):
            gate[80 * c:80 * c + 80, 128 * p:128 * p + 128] = a[p, c, 0:80].astype(F32)
    leave(gate, gate_o)
    for c in range(8):
        for p in range(4):
            up[80 * c:80 * c + 80, 128 * p:128 * p + 128] = a[p, c, 80:160].astype(F32)
    leave(up, up_o)
    for c in range(8):
        for p in range(4):
            down[64 * c:64 * c + 64, 128 * p:128 * p + 128] = a[p, c, 160:224].astype(F32)
            down[128 * p + 16 * c:128 * p + 16 * c + 16, 512:640] = a[p, c, 224:240].astype(F32)
    leave(down, down_o)
    for c in range(8):
        for p, b, at in ((0, b0, 80), (1, b1, 80), (2, b1, 112), (3, b2, 80), (4, b3, 80)):
            out[32 * c:32 * c + 32, 128 * p:128 * p + 128] = b[c, at:at + 32].astype(F32)
    leave(out, out_o)
    for c in range(8):
        for p, b in ((0, b0), (1, b1)):
            query[80 * c:80 * c + 80, 128 * p:128 * p + 128] = b[c, 0:80].astype(F32)
    leave(query, query_o)
    for c in range(8):
        for j in range(2):
            key[80 * c:80 * c + 80, 128 * j:128 * j + 128] = kv[j, c].astype(F32)
            value[80 * c:80 * c + 80, 128 * j:128 * j + 128] = kv[2 + j, c].astype(F32)
    leave(key, key_o)
    leave(value, value_o)
    for i, g in ((3, g0), (0, g1), (1, g2), (2, g3)):
        g[...] = gains[i, :]
    g4[...] = gains[4, 0:256]
    g5[...] = gains[4, 256:512]
    for copy in copies:
        copy.wait()


def layer(*operands):
    sds = jax.ShapeDtypeStruct
    dma = pltpu.SemaphoreType.DMA
    v = pltpu.VMEM
    blocks = (NC, 2, OW, 640)
    half = (NC, OW, 640)
    count = NC * 12
    stacks = pl.pallas_call(
        layer_kernel,
        out_shape=(sds(blocks, BF), sds(blocks, BF), sds((4, 8, 240, 128), BF), sds((8, 112, 128), BF), sds((8, 144, 128), BF),
                   sds((8, 112, 128), BF), sds((8, 112, 128), BF), sds((4, 8, 80, 128), BF), sds((8, 640), F32)),
        in_specs=[VMEM] * len(operands),
        out_specs=[VMEM] * 9,
        scratch_shapes=[
            v((1024, 640), BF), v((1024, 256), F32), v((1024, 256), F32), v((1024, 256), BF), v((1024, 256), BF),
            v((1024, 256), BF), v((NC, CR, 768), F32), v((1024, 256), BF), v((4, *blocks), BF), v(blocks, BF), v(blocks, BF),
            v(blocks, BF), v((NC, CR, 512), BF), v((NC, CR, 512), F32), v((NC, CR, 512), F32), v((NC, CR, 512), BF),
            v((NC, CR, 512), BF), v(half, F32), v(half, F32), v((4, *half), BF), v((4, *half), BF),
            v((1024, 256), F32), v((1024, 256), F32), v((1024, 768), BF),
            v((4, 8, 240, 128), BF),
            v((8, 112, 128), BF), v((8, 144, 128), BF), v((8, 112, 128), BF), v((8, 112, 128), BF),
            v((4, 9, 240, 128), BF),
            v((9, 112, 128), BF), v((9, 144, 128), BF), v((11, 112, 128), BF), v((11, 112, 128), BF),
            v((4, 8, 80, 128), BF), v((2, 8, 80, 128), BF),
            v((8, 8, 640), F32), v((640, 768), F32), v((256, 640), F32), v((512, 640), F32), v((2, 640, 512), F32),
            dma((count + 16,)), dma((count + 16,)),
            dma((4, 8)), dma((4, 8)), dma((2, 8)), dma((2, 8)), dma((2, 10)), dma((2, 10)), dma((2,)), dma((2,)),
            dma((8,)), dma((8,)),
        ],
        compiler_params=pltpu.CompilerParams(collective_id=7, has_side_effects=True, vmem_limit_bytes=VMEM_LIMIT),
        name="layer",
    )(*operands)
    big = [(640, 256), (640, 256), (640, 256), (256, 640), (640, 512), (640, 512), (512, 640)]
    small = [(640,), (640,), (640,), (640,), (256,), (256,)]
    anywhere = pl.BlockSpec(memory_space=pl.ANY)
    outs = pl.pallas_call(
        unpack_kernel,
        out_shape=[sds(shape, F32) for shape in big] + [sds(blocks, BF)] * 2 + [sds(shape, F32) for shape in small],
        in_specs=[VMEM] * 9,
        out_specs=[anywhere] * 9 + [VMEM] * 6,
        scratch_shapes=[v(shape, F32) for shape in big] + [dma((9,))],
        compiler_params=pltpu.CompilerParams(vmem_limit_bytes=VMEM_LIMIT),
        name="unpack_grads",
    )(*stacks[2:], stacks[0], stacks[1])
    return outs[7], outs[8], (*outs[:7], *outs[9:])


def rope_tables(positions, head_size):
    half_size = head_size // 2
    inv_freq = ROPE_BASE ** (-2.0 * jnp.arange(half_size, dtype=jnp.float32) / head_size)
    angles = positions.astype(jnp.float32)[:, None] * inv_freq[None, :]
    return (jnp.cos(angles), jnp.sin(angles))


def local(
    inputs,
    segments,
    positions,
    cotangent,
    w_query,
    w_key,
    w_value,
    w_out,
    w_gate,
    w_up,
    w_down,
    g_attn_in,
    g_attn_out,
    g_ffn_in,
    g_ffn_out,
    g_query,
    g_key,
):
    blocks = (NC, 2, OW, 640)
    cos_t, sin_t = rope_tables(positions, 256)
    output, input_grad, summed = layer(
        inputs.reshape(blocks), cotangent.reshape(blocks), segments.reshape(1, 1024), cos_t, sin_t,
        w_query, w_key, w_value, w_out, w_gate, w_up, w_down,
        g_attn_in, g_attn_out, g_ffn_in, g_ffn_out, g_query, g_key,
    )
    return (output.reshape(1024, 640), input_grad.reshape(1024, 640), *summed)


def solution(mesh):
    placed = (
        P("dp", None),
        P("dp"),
        P("dp"),
        P("dp", None),
        P(None, "tensor"),
        P(),
        P(),
        P("tensor", None),
        P(None, "tensor"),
        P(None, "tensor"),
        P("tensor", None),
        P(),
        P(),
        P(),
        P(),
        P(),
        P(),
    )
    return jax.shard_map(
        local,
        mesh=mesh,
        in_specs=placed,
        out_specs=(
            P("dp", None),
            P("dp", None),
            P(None, "tensor"),
            P(),
            P(),
            P("tensor", None),
            P(None, "tensor"),
            P(None, "tensor"),
            P("tensor", None),
            P(),
            P(),
            P(),
            P(),
            P(),
            P(),
        ),
        check_vma=False,
    )
```

```python
import jax
import jax.numpy as jnp
import numpy as np
from jax import lax
from jax.experimental import pallas as pl
from jax.experimental.pallas import tpu as pltpu
from jax.sharding import PartitionSpec as P

WINDOW = 512
EPSILON = 1e-06
ROPE_BASE = 10000.0
NEG_LARGE = -1e30

MESH = pl.DeviceIdType.MESH
BF = jnp.bfloat16
F32 = jnp.float32
VMEM = pl.BlockSpec(memory_space=pltpu.VMEM)
VMEM_LIMIT = 60 * 1024 * 1024


def neighbours():
    dp = lax.axis_index("dp")
    t = lax.axis_index("tensor")
    z = lax.rem(dp, 4)
    y = lax.rem(dp // 4, 4)
    xh = dp // 16
    xl = t // 2
    core = lax.rem(t, 2)
    ya = y + 1 - 2 * lax.rem(y, 2)
    za = z + 1 - 2 * lax.rem(z, 2)
    links = [
        (dp + (ya - y) * 4, t),
        (dp + (za - z), t),
        (dp + (3 - 2 * y) * 4, t),
        (dp + (3 - 2 * z), t),
    ]
    bits = [lax.rem((y + 1) // 2, 2), lax.rem((z + 1) // 2, 2), y // 2, z // 2]
    across = (dp + 16 - 32 * xh, t)
    sibling = (dp, t + 1 - 2 * core)
    beside = (dp, t + 2 - 4 * xl)
    corner = (dp + 16 - 32 * xh, t + 2 - 4 * xl)
    return links, bits, across, sibling, beside, corner, xl, core


def greet(devices):
    barrier = pltpu.get_barrier_semaphore()
    for d in devices:
        pl.semaphore_signal(barrier, inc=1, device_id=d, device_id_type=MESH)
    pl.semaphore_wait(barrier, len(devices))


def send(src, dst, ssem, rsem, device):
    copy = pltpu.make_async_remote_copy(
        src_ref=src, dst_ref=dst, send_sem=ssem, recv_sem=rsem, device_id=device, device_id_type=MESH
    )
    copy.start()
    return copy


class Reduction:
    def __init__(self, ids, bufs, recvs, outs, ssem, rsem, links, bits, across, more=()):
        self.ids, self.bufs, self.recvs, self.outs, self.ssem, self.rsem = ids, bufs, recvs, outs, ssem, rsem
        self.links, self.bits, self.across, self.more = links, bits, across, more
        self.base = [jnp.int32(0)] * len(ids)
        self.at = 0

    def start(self):
        step = self.at
        self.copies = []
        for i, p in enumerate(self.ids):
            buf, recv = self.bufs[i], self.recvs[i]
            ss, rs = self.ssem.at[i, step], self.rsem.at[i, step]
            if step < 3:
                n = 4 >> step
                bit = self.bits[(p + step) % 4]
                there = self.base[i] + (1 - bit) * n
                self.base[i] = self.base[i] + bit * n
                at = (0, 4, 6)[step]
                src, dst, dev = buf.at[pl.ds(there, n)], recv.at[pl.ds(at, n)], self.links[(p + step) % 4]
            elif step < 5:
                dev = self.links[(p + 3) % 4] if step == 3 else self.across
                src, dst = buf.at[self.base[i]], recv.at[4 + step]
            else:
                s = 7 - step
                n = 4 >> s
                bit = self.bits[(p + s) % 4]
                src = dst = self.outs[i].at[pl.ds(self.base[i], n)]
                self.base[i] = self.base[i] - bit * n
                dev = self.links[(p + s) % 4]
            self.copies.append(send(src, dst, ss, rs, dev))
            if step == 4:
                for j, dev in enumerate(self.more):
                    self.copies.append(send(buf.at[self.base[i], pl.ds(0, 80)], recv.at[9 + j, pl.ds(0, 80)],
                                            self.ssem.at[i, 8 + j], self.rsem.at[i, 8 + j], dev))

    def advance(self):
        step = self.at
        if step == 8:
            return
        for copy in self.copies:
            copy.wait()
        if step < 5:
            n = (4, 2, 1, 1, 1)[step]
            at = (0, 4, 6, 7, 8)[step]
            for i in range(len(self.ids)):
                buf, recv, base = self.bufs[i], self.recvs[i], self.base[i]
                into = self.outs[i] if step == 4 else buf

                def add(j, carry):
                    into[base + j] = (buf[base + j].astype(F32) + recv[at + j].astype(F32)).astype(BF)
                    return carry

                lax.fori_loop(0, n, add, 0)
                if step == 4 and self.more:
                    pair = recv[9, 0:80].astype(F32) + recv[10, 0:80].astype(F32)
                    into[base, 0:80] = (buf[base, 0:80].astype(F32) + recv[8, 0:80].astype(F32) + pair).astype(BF)
        self.at = step + 1
        if self.at < 8:
            self.start()


NC = 4
CR = 1024 // NC
OW = CR // 2
C0 = 0.7978845608028654
C1 = 0.044715


def nt(a, b):
    return lax.dot_general(a, b, (((1,), (1,)), ((), ())), preferred_element_type=F32)


def tn(a, b):
    return lax.dot_general(a, b, (((0,), (0,)), ((), ())), preferred_element_type=F32)


def nn(a, b):
    return jnp.dot(a, b, preferred_element_type=F32)


def inv_rms(v):
    return lax.rsqrt(jnp.mean(v * v, axis=-1, keepdims=True) + EPSILON)


def rms_back(v, r, du):
    return r * du - v * (r * r * r * jnp.mean(du * v, axis=-1, keepdims=True))


def turn(v, cosine, sine):
    a, b = v[:, :128], v[:, 128:]
    return jnp.concatenate([a * cosine - b * sine, b * cosine + a * sine], axis=-1)


def turn_back(v, cosine, sine):
    a, b = v[:, :128], v[:, 128:]
    return jnp.concatenate([a * cosine + b * sine, b * cosine - a * sine], axis=-1)


def key_range(i):
    first = max(0, (i - 2) * CR)
    return first, (i + 1) * CR - first


def vec(g):
    return g[...]


def layer_kernel(x, cot, segs, pos, far, near, wq, wk, wv, wo, wg, wu, wd, g_in, g_ao, g_fi, g_fo, g_q, g_k,
                 output, in_grad, a_out, o0, o1, o2, o3, kv_out, gains,
                 normed, q_raw, k_raw, q, k, v, prob, heads, part, ffn_g, dffn_g, dattn, hid, act_a, act_b, dgate, dup,
                 attn_own, mid_own, recv_a, recv_b, dk, dv, dqkv,
                 a_buf, b0, b1, b2, b3, a_recv, r0, r1, r2, r3, kv, kv_recv, g_recv, in_acc, out_acc, down_acc, up_acc, cos_t, sin_t,
                 ssem, rsem, a_ss, a_rs, b_ss, b_rs, c_ss, c_rs, k_ss, k_rs, g_ss, g_rs):
    links, bits, across, sibling, beside, corner, xl, core = neighbours()
    greet(links + [across, sibling, beside, corner])
    own = core
    state = [dict() for _ in range(NC)]
    used = [0]

    def post(src, dst, device):
        i = used[0]
        used[0] += 1
        return send(src, dst, ssem.at[i], rsem.at[i], device)

    def share(e, c):
        state[c]["a"] = post(part.at[e, c, 1 - own], recv_a.at[e, c], sibling)

    def exchange(e):
        def run(c):
            state[c]["a"].wait()
            part[e, c, own] = (part[e, c, own].astype(F32) + recv_a[e, c].astype(F32)).astype(BF)
            state[c]["b"] = post(part.at[e, c, own], recv_b.at[e, c], beside)
        return run

    def total(e, c):
        state[c]["b"].wait()
        return part[e, c, own].astype(F32) + recv_b[e, c].astype(F32)

    def give(buf, c):
        return post(buf.at[c, own], buf.at[c, own], sibling)

    def keys_stage():
        for c in range(NC - 1, -1, -1):
            rows = slice(c * CR, c * CR + CR)
            at = pos[:, rows]
            picked = []
            for table, index in ((far, lax.shift_right_logical(at, 5)), (near, at & 31)):
                hot = (lax.broadcasted_iota(jnp.int32, (table.shape[0], CR), 0) == index).astype(F32).astype(BF)
                parts = tn(hot, table[...])
                picked.append(parts[:, 0:256] + (parts[:, 256:512] + parts[:, 512:768]))
            (c1, s1), (c2, s2) = ((t[:, :128], t[:, 128:]) for t in picked)
            cos_t[rows] = c1 * c2 - s1 * s2
            sin_t[rows] = s1 * c2 + c1 * s2
            xv = x[c].reshape(CR, 640).astype(F32)
            n = (xv * inv_rms(xv) * vec(g_in)).astype(BF)
            normed[rows] = n
            raw = nn(n, wk[...])
            k_raw[rows] = raw
            k[rows] = turn(raw * inv_rms(raw) * vec(g_k), cos_t[rows], sin_t[rows]).astype(BF)
            v[rows] = nn(n, wv[...]).astype(BF)

    def attention_stage(c):
        rows = slice(c * CR, c * CR + CR)
        raw = nn(normed[rows], wq[...])
        q_raw[rows] = raw
        q_low = turn(raw * inv_rms(raw) * vec(g_q), cos_t[rows], sin_t[rows]).astype(BF)
        q[rows] = q_low
        first, size = key_range(c)
        keys = slice(first, first + size)
        scores = nt(q_low, k[keys]) * 0.0625
        gap = c * CR - first + lax.broadcasted_iota(jnp.int32, (CR, size), 0) - lax.broadcasted_iota(jnp.int32, (CR, size), 1)
        seg_rows = jnp.broadcast_to(segs[:, rows], (128, CR)).T[:, :1]
        allowed = (gap >= 0) & (gap < WINDOW) & (seg_rows == segs[:, keys])
        masked = jnp.where(allowed, scores, NEG_LARGE)
        e = jnp.where(allowed, jnp.exp(masked - jnp.max(masked, axis=-1, keepdims=True)), 0.0)
        p = e / jnp.sum(e, axis=-1, keepdims=True)
        prob[c, :, 0:size] = p
        h = nn(p.astype(BF), v[keys]).astype(BF)
        heads[rows] = h
        part[0, c] = nn(h, wo[...]).astype(BF).reshape(2, OW, 640)
        share(0, c)

    def mid_stage(c):
        a = total(0, c)
        attn_own[c] = a
        mid = x[c, own].astype(F32) + a * inv_rms(a) * vec(g_ao)
        mid_own[c] = mid
        ffn_g[c, own] = (mid * inv_rms(mid) * vec(g_fi)).astype(BF)
        state[c]["g"] = give(ffn_g, c)

    def up_stage(c):
        state[c]["g"].wait()
        f = ffn_g[c].reshape(CR, 640)
        gate = nn(f, wg[...])
        up = nn(f, wu[...])
        th = jnp.tanh(C0 * (gate + C1 * gate * gate * gate))
        half = 0.5 * (1.0 + th)
        act = gate * half
        slope = half + 0.5 * gate * (1.0 - th * th) * (C0 * (1.0 + 3.0 * C1 * gate * gate))
        act_a[c] = up * slope
        act_b[c] = act
        h = (act * up).astype(BF)
        hid[c] = h
        part[1, c] = nn(h, wd[...]).astype(BF).reshape(2, OW, 640)
        share(1, c)

    def out_stage(c):
        s = total(1, c)
        r = inv_rms(s)
        ct = cot[c, own].astype(F32)
        dffn_g[c, own] = rms_back(s, r, ct * vec(g_fo)).astype(BF)
        state[c]["g"] = give(dffn_g, c)
        output[c, own] = (mid_own[c] + s * r * vec(g_fo)).astype(BF)
        state[c]["o"] = give(output, c)
        gains[2:3, :] = gains[2:3, :] + jnp.sum(ct * s * r, axis=0, keepdims=True)

    def down_stage(c):
        state[c]["g"].wait()
        d = dffn_g[c].reshape(CR, 640)
        dh = nt(d, wd[...])
        dg = (dh * act_a[c]).astype(BF)
        du = (dh * act_b[c]).astype(BF)
        dgate[c] = dg
        dup[c] = du
        part[2, c] = (nt(dg, wg[...]) + nt(du, wu[...])).astype(BF).reshape(2, OW, 640)
        share(2, c)

    def attn_stage(c):
        d = total(2, c)
        mid, a = mid_own[c], attn_own[c]
        r = inv_rms(mid)
        gains[1:2, :] = gains[1:2, :] + jnp.sum(d * mid * r, axis=0, keepdims=True)
        dmid = cot[c, own].astype(F32) + rms_back(mid, r, d * vec(g_fi))
        mid_own[c] = dmid
        r = inv_rms(a)
        gains[0:1, :] = gains[0:1, :] + jnp.sum(dmid * a * r, axis=0, keepdims=True)
        dattn[c, own] = rms_back(a, r, dmid * vec(g_ao)).astype(BF)
        state[c]["g"] = give(dattn, c)

    def back_stage(i):
        state[i]["g"].wait()
        rows = slice(i * CR, i * CR + CR)
        start, size = key_range(i)
        dh = nt(dattn[i].reshape(CR, 640), wo[...]).astype(BF)
        p = prob[i, :, 0:size]
        dp = nt(dh, v[start:start + size])
        ds = (p * (dp - jnp.sum(p * dp, axis=-1, keepdims=True))).astype(BF)
        dq = nn(ds, k[start:start + size]) * 0.0625
        dk_add = tn(ds, q[rows]) * 0.0625
        dv_add = tn(p.astype(BF), dh)
        fresh = size if i == NC - 1 else (CR if i == NC - 2 else 0)
        if fresh:
            dk[start:start + fresh] = dk_add[:fresh]
            dv[start:start + fresh] = dv_add[:fresh]
        if fresh < size:
            dk[start + fresh:start + size] = dk[start + fresh:start + size] + dk_add[fresh:]
            dv[start + fresh:start + size] = dv[start + fresh:start + size] + dv_add[fresh:]
        cosine, sine = cos_t[rows], sin_t[rows]
        raws = []
        for d, raw, g, at in ((dq, q_raw[rows], g_q, 0), (dk[rows], k_raw[rows], g_k, 256)):
            du = turn_back(d, cosine, sine)
            r = inv_rms(raw)
            gains[4:5, at:at + 256] = gains[4:5, at:at + 256] + jnp.sum(du * raw * r, axis=0, keepdims=True)
            raws.append(rms_back(raw, r, du * vec(g)).astype(BF))
        raws.append(dv[rows].astype(BF))
        for j in range(3):
            dqkv[rows, 256 * j:256 * j + 256] = raws[j]
        if i == 0:
            weights_out()
            weights_in()
        term = nt(raws[0], wq[...]) + nt(raws[1], wk[...]) + nt(raws[2], wv[...])
        xv = x[i].reshape(CR, 640).astype(F32)
        gains[3:4, :] = gains[3:4, :] + jnp.sum(term * (xv * inv_rms(xv)), axis=0, keepdims=True)
        part[3, i] = term.astype(BF).reshape(2, OW, 640)
        share(3, i)

    def in_stage(i):
        d = total(3, i)
        xv = x[i, own].astype(F32)
        r = inv_rms(xv)
        in_grad[i, own] = (mid_own[i] + rms_back(xv, r, d * vec(g_in))).astype(BF)
        state[i]["g"] = give(in_grad, i)

    def ffn_early():
        n = 1024 - CR
        f = ffn_g[1:].reshape(n, 640)
        down_acc[...] = tn(hid[1:].reshape(n, 512), dffn_g[1:].reshape(n, 640))
        up_acc[0] = tn(f, dgate[1:].reshape(n, 512))
        up_acc[1] = tn(f, dup[1:].reshape(n, 512))

    def weights_down():
        g = (down_acc[...] + tn(hid[0], dffn_g[0].reshape(CR, 640))).astype(BF)
        for s in range(8):
            for p in range(4):
                a_buf[p, s, 160:224] = g[64 * s:64 * s + 64, 128 * p:128 * p + 128]
            for p in range(4):
                a_buf[p, s, 224:240] = g[128 * p + 16 * s:128 * p + 16 * s + 16, 512:640]

    def weights_ffn(source, at):
        g = (up_acc[at // 80] + tn(ffn_g[0].reshape(CR, 640), source[0])).astype(BF)
        for s in range(8):
            for p in range(4):
                a_buf[p, s, at:at + 80] = g[80 * s:80 * s + 80, 128 * p:128 * p + 128]

    def weights_early():
        out_acc[...] = tn(heads[CR:], dattn[1:].reshape(1024 - CR, 640))
        in_acc[...] = tn(normed[CR:], dqkv[CR:])

    def weights_out():
        g = (out_acc[...] + tn(heads[0:CR], dattn[0].reshape(CR, 640))).astype(BF)
        for c in range(8):
            rows = slice(32 * c, 32 * c + 32)
            b0[c, 80:112] = g[rows, 0:128]
            b1[c, 80:112] = g[rows, 128:256]
            b1[c, 112:144] = g[rows, 256:384]
            b2[c, 80:112] = g[rows, 384:512]
            b3[c, 80:112] = g[rows, 512:640]

    def weights_in():
        g = (in_acc[...] + tn(normed[0:CR], dqkv[0:CR])).astype(BF)
        for c in range(8):
            rows = slice(80 * c, 80 * c + 80)
            for j in range(4):
                kv[j, c] = g[rows, 256 + 128 * j:384 + 128 * j]
            b0[c, 0:80] = g[rows, 0:128]
            b1[c, 0:80] = g[rows, 128:256]
        extra["kv"] = send(kv.at[pl.ds((1 - core) * 2, 2)], kv_recv, k_ss.at[0], k_rs.at[0], sibling)
        second.start()

    def begin_third():
        extra["kv"].wait()
        for i, b in ((0, b2), (1, b3)):
            for c in range(8):
                b[c, 0:80] = (kv[core * 2 + i, c].astype(F32) + kv_recv[i, c].astype(F32)).astype(BF)
        third.start()

    extra = {"gain": 0}
    order = [(sibling,), (beside, across, corner), (links[0],), (links[1],), (links[2],), (links[3],)]

    def send_gains():
        i = extra["gain"]
        if i < 6:
            at = (0, 1, 4, 5, 6, 7)[i]
            extra["copies"] = [send(gains, g_recv.at[at + j], g_ss.at[at + j], g_rs.at[at + j], d) for j, d in enumerate(order[i])]

    def begin_gains():
        gains[0:3, :] = gains[0:3, :] * 0.5
        send_gains()

    def swap_gains():
        i = extra["gain"]
        if i == 6:
            return
        for copy in extra["copies"]:
            copy.wait()
        if i == 1:
            gains[...] = (gains[...] + g_recv[2]) + (g_recv[1] + g_recv[3])
        else:
            gains[...] = gains[...] + g_recv[(0, 1, 4, 5, 6, 7)[i]]
        extra["gain"] = i + 1
        send_gains()

    first = Reduction((0, 1, 2, 3), [a_buf.at[p] for p in range(4)], [a_recv.at[p] for p in range(4)],
                      [a_out.at[p] for p in range(4)], a_ss, a_rs, links, bits, across)
    second = Reduction((0, 1), [b0, b1], [r0, r1], [o0, o1], b_ss, b_rs, links, bits, across)
    third = Reduction((3, 0), [b2, b3], [r2, r3], [o2, o3], c_ss, c_rs, links, bits, across, (beside, corner))
    jobs = {
        "down": weights_down, "gate": lambda: weights_ffn(dgate, 0), "up": lambda: weights_ffn(dup, 80),
        "first": first.start, "third": begin_third, "1": first.advance, "2": second.advance, "3": third.advance,
        "gains": begin_gains, "g": swap_gains, "acc": weights_early, "ffn": ffn_early,
    }
    gains[...] = jnp.zeros_like(gains)
    keys_stage()
    stages = [
        attention_stage, exchange(0), mid_stage, up_stage, exchange(1), out_stage, down_stage, exchange(2), attn_stage,
        back_stage, exchange(3), in_stage,
    ]
    for tick in range(len(stages) + NC - 1):
        for p in range(NC):
            s = tick - p
            if 0 <= s < len(stages):
                stages[s](NC - 1 - p)
                for job in AFTER.get((s, p), ()):
                    jobs[job]()
    sent = False
    for i in range(9):
        third.advance()
        if third.at == 8 and not sent:
            sent = True
            for j, o in ((0, o2), (1, o3)):
                for c in range(8):
                    kv_out[core * 2 + j, c] = o[c, 0:80]
            kc = send(kv_out.at[pl.ds(core * 2, 2)], kv_out.at[pl.ds(core * 2, 2)], k_ss.at[1], k_rs.at[1], sibling)
        second.advance()
        swap_gains()
        if i in LATE:
            first.advance()
    kc.wait()
    for c in range(NC):
        state[c]["o"].wait()
        state[c]["g"].wait()


AFTER = {
    (6, 2): ("ffn",),
    (6, 3): ("down", "gate", "up", "first"),
    (8, 2): ("1",),
    (10, 1): ("1",),
    (9, 2): ("acc",),
    (8, 3): ("1",),
    (9, 3): ("gains", "third", "1", "2"),
    (11, 2): ("2", "3", "g"),
    (10, 3): ("1",),
    (11, 3): ("2", "3", "g"),
}
LATE = (0, 2, 5)


def unpack_kernel(a, b0, b1, b2, b3, kv, gains, y, dx, query_o, key_o, value_o, out_o, gate_o, up_o, down_o, y_o, dx_o,
                  g0, g1, g2, g3, g4, g5, query, key, value, out, gate, up, down, sems):
    copies = []

    def leave(src, dst):
        copy = pltpu.make_async_copy(src, dst, sems.at[len(copies)])
        copy.start()
        copies.append(copy)

    leave(y, y_o)
    leave(dx, dx_o)
    for c in range(8):
        for p in range(4):
            gate[80 * c:80 * c + 80, 128 * p:128 * p + 128] = a[p, c, 0:80].astype(F32)
    leave(gate, gate_o)
    for c in range(8):
        for p in range(4):
            up[80 * c:80 * c + 80, 128 * p:128 * p + 128] = a[p, c, 80:160].astype(F32)
    leave(up, up_o)
    for c in range(8):
        for p in range(4):
            down[64 * c:64 * c + 64, 128 * p:128 * p + 128] = a[p, c, 160:224].astype(F32)
            down[128 * p + 16 * c:128 * p + 16 * c + 16, 512:640] = a[p, c, 224:240].astype(F32)
    leave(down, down_o)
    for c in range(8):
        for p, b, at in ((0, b0, 80), (1, b1, 80), (2, b1, 112), (3, b2, 80), (4, b3, 80)):
            out[32 * c:32 * c + 32, 128 * p:128 * p + 128] = b[c, at:at + 32].astype(F32)
    leave(out, out_o)
    for c in range(8):
        for p, b in ((0, b0), (1, b1)):
            query[80 * c:80 * c + 80, 128 * p:128 * p + 128] = b[c, 0:80].astype(F32)
    leave(query, query_o)
    for c in range(8):
        for j in range(2):
            key[80 * c:80 * c + 80, 128 * j:128 * j + 128] = kv[j, c].astype(F32)
            value[80 * c:80 * c + 80, 128 * j:128 * j + 128] = kv[2 + j, c].astype(F32)
    leave(key, key_o)
    leave(value, value_o)
    for i, g in ((3, g0), (0, g1), (1, g2), (2, g3)):
        g[...] = gains[i, :]
    g4[...] = gains[4, 0:256]
    g5[...] = gains[4, 256:512]
    for copy in copies:
        copy.wait()


def layer(*operands):
    sds = jax.ShapeDtypeStruct
    dma = pltpu.SemaphoreType.DMA
    v = pltpu.VMEM
    blocks = (NC, 2, OW, 640)
    half = (NC, OW, 640)
    count = NC * 12
    stacks = pl.pallas_call(
        layer_kernel,
        out_shape=(sds(blocks, BF), sds(blocks, BF), sds((4, 8, 240, 128), BF), sds((8, 112, 128), BF), sds((8, 144, 128), BF),
                   sds((8, 112, 128), BF), sds((8, 112, 128), BF), sds((4, 8, 80, 128), BF), sds((8, 640), F32)),
        in_specs=[VMEM] * len(operands),
        out_specs=[VMEM] * 9,
        scratch_shapes=[
            v((1024, 640), BF), v((1024, 256), F32), v((1024, 256), F32), v((1024, 256), BF), v((1024, 256), BF),
            v((1024, 256), BF), v((NC, CR, 768), F32), v((1024, 256), BF), v((4, *blocks), BF), v(blocks, BF), v(blocks, BF),
            v(blocks, BF), v((NC, CR, 512), BF), v((NC, CR, 512), F32), v((NC, CR, 512), F32), v((NC, CR, 512), BF),
            v((NC, CR, 512), BF), v(half, F32), v(half, F32), v((4, *half), BF), v((4, *half), BF),
            v((1024, 256), F32), v((1024, 256), F32), v((1024, 768), BF),
            v((4, 8, 240, 128), BF),
            v((8, 112, 128), BF), v((8, 144, 128), BF), v((8, 112, 128), BF), v((8, 112, 128), BF),
            v((4, 9, 240, 128), BF),
            v((9, 112, 128), BF), v((9, 144, 128), BF), v((11, 112, 128), BF), v((11, 112, 128), BF),
            v((4, 8, 80, 128), BF), v((2, 8, 80, 128), BF),
            v((8, 8, 640), F32), v((640, 768), F32), v((256, 640), F32), v((512, 640), F32), v((2, 640, 512), F32),
            v((1024, 128), F32), v((1024, 128), F32),
            dma((count + 16,)), dma((count + 16,)),
            dma((4, 8)), dma((4, 8)), dma((2, 8)), dma((2, 8)), dma((2, 10)), dma((2, 10)), dma((2,)), dma((2,)),
            dma((8,)), dma((8,)),
        ],
        compiler_params=pltpu.CompilerParams(collective_id=7, has_side_effects=True, vmem_limit_bytes=VMEM_LIMIT),
        name="layer",
    )(*operands)
    big = [(640, 256), (640, 256), (640, 256), (256, 640), (640, 512), (640, 512), (512, 640)]
    small = [(640,), (640,), (640,), (640,), (256,), (256,)]
    anywhere = pl.BlockSpec(memory_space=pl.ANY)
    outs = pl.pallas_call(
        unpack_kernel,
        out_shape=[sds(shape, F32) for shape in big] + [sds(blocks, BF)] * 2 + [sds(shape, F32) for shape in small],
        in_specs=[VMEM] * 9,
        out_specs=[anywhere] * 9 + [VMEM] * 6,
        scratch_shapes=[v(shape, F32) for shape in big] + [dma((9,))],
        compiler_params=pltpu.CompilerParams(vmem_limit_bytes=VMEM_LIMIT),
        name="unpack_grads",
    )(*stacks[2:], stacks[0], stacks[1])
    return outs[7], outs[8], (*outs[:7], *outs[9:])


def turn_table(count, step):
    angles = np.arange(count)[:, None] * float(step) * ROPE_BASE ** (-2.0 * np.arange(128)[None, :] / 256)
    rest = np.concatenate([np.cos(angles), np.sin(angles)], axis=1)
    parts = []
    for _ in range(3):
        parts.append(rest.astype(np.float32).astype(BF))
        rest = rest - parts[-1].astype(np.float64)
    return jnp.asarray(np.concatenate(parts, axis=1))


def local(
    inputs,
    segments,
    positions,
    cotangent,
    w_query,
    w_key,
    w_value,
    w_out,
    w_gate,
    w_up,
    w_down,
    g_attn_in,
    g_attn_out,
    g_ffn_in,
    g_ffn_out,
    g_query,
    g_key,
):
    blocks = (NC, 2, OW, 640)
    output, input_grad, summed = layer(
        inputs.reshape(blocks), cotangent.reshape(blocks), segments.reshape(1, 1024), positions.reshape(1, 1024),
        turn_table(64, 32), turn_table(32, 1),
        w_query, w_key, w_value, w_out, w_gate, w_up, w_down,
        g_attn_in, g_attn_out, g_ffn_in, g_ffn_out, g_query, g_key,
    )
    return (output.reshape(1024, 640), input_grad.reshape(1024, 640), *summed)


def solution(mesh):
    placed = (
        P("dp", None),
        P("dp"),
        P("dp"),
        P("dp", None),
        P(None, "tensor"),
        P(),
        P(),
        P("tensor", None),
        P(None, "tensor"),
        P(None, "tensor"),
        P("tensor", None),
        P(),
        P(),
        P(),
        P(),
        P(),
        P(),
    )
    return jax.shard_map(
        local,
        mesh=mesh,
        in_specs=placed,
        out_specs=(
            P("dp", None),
            P("dp", None),
            P(None, "tensor"),
            P(),
            P(),
            P("tensor", None),
            P(None, "tensor"),
            P(None, "tensor"),
            P("tensor", None),
            P(),
            P(),
            P(),
            P(),
            P(),
            P(),
        ),
        check_vma=False,
    )
```
